256 devices in a mesh: obs: 8 (over z), grid: 32 (over y, x, core).
Axes of the slice: x: 4, y: 4, z: 8, core: 2. Of those that a mesh axis runs over, the one named last changes fastest.
Arguments:
- departures: bfloat16 [524288, 128], P(('obs', 'grid')), may hold values from -8 to 8
- innovation: float32 [524288], P(('obs', 'grid')), may hold values from -12 to 12
- obs_weight: float32 [524288], P(('obs', 'grid')), may hold values from 0.004 to 0.04
- send_rows: int32 [256, 256, 64], P(('obs', 'grid')), may hold values from -1 to 2047, as said below
- send_counts: int32 [256, 256], P(('obs', 'grid')), may hold values from 16 to 64, as said below
- state: bfloat16 [384, 128, 4096], P('obs', None, 'grid'), may hold values from -6 to 6
Outputs:
- analysis: bfloat16 [384, 128, 4096], P('obs', None, 'grid')
The draws below stay inside these ranges and needn't reach their ends.
Inputs may be any that keep to these rules, and one draw needn't show every extreme that they name: For each shard s and patch p the first send_counts[s, p] places of send_rows[s, p] hold rows of shard s (0 to 2047) and the others -1; the rows sent by one shard go to 2 to 7 different patches each, every row at least once; some patch gets 64 rows from every shard. `send_counts`: consistent with send_rows.
All inputs are finite; a program needn't handle non-finite values.
Results may differ from the reference program's by a relative error of at most 0.0055.
Values may be sent and summed in bfloat16 or wider, within the bound.
No kernel may reach another device: no remote copies, remote signals or barrier semaphores. Data moves between devices by JAX's collectives and lax.ppermute only.
A program may use at most 64 MiB of HBM per device.

```python
import math
import jax
import jax.numpy as jnp
from jax import lax

K = 128
PR = 48
COLS = 128
CAP = 64
ITERS = 6
PATCHES = 256
ROWS_DEV = 2048
ROWS = 524288
LAT = 384
LON = 4096
N_OBS = 8
N_GRID = 32


def shuffle(sub_key):
    return jax.random.permutation(sub_key, ROWS_DEV)


def relay_plan(key):
    perm_key, hot_key, drawn_key, rows_key = jax.random.split(key, 4)
    patch_order = jax.random.permutation(perm_key, PATCHES)
    patch_rank = jnp.argsort(patch_order)
    hot_mask = patch_rank < PATCHES // 16
    drawn_counts = CAP // 4 + jax.random.randint(drawn_key, (PATCHES, PATCHES), 0, CAP // 2 + 1)
    hot_counts = 5 * CAP // 8 + jax.random.randint(hot_key, (PATCHES, PATCHES), 0, 3 * CAP // 8 + 1)
    counts = jnp.where(hot_mask[None, :], hot_counts, drawn_counts)
    counts = jnp.where((patch_rank == 0)[None, :], CAP, counts).astype(jnp.int32)
    offsets = jnp.cumsum(counts, axis=1) - counts
    places = jnp.arange(CAP, dtype=jnp.int32)
    flat_place = offsets[:, :, None] + places[None, None, :]
    row_perms = jax.vmap(shuffle)(jax.random.split(rows_key, PATCHES))
    chosen = jnp.take_along_axis(row_perms, (flat_place % ROWS_DEV).reshape(PATCHES, -1), axis=1)
    chosen = chosen.reshape(PATCHES, PATCHES, CAP)
    slot_rows = jnp.where(places[None, None, :] < counts[:, :, None], chosen, -1).astype(jnp.int32)
    return (counts, slot_rows)


def draw_send_rows(key, part):
    return relay_plan(key)[1]


def draw_send_counts(key, part):
    return relay_plan(key)[0]


def weight_plan(key):
    weight_key = jax.random.fold_in(key, 11)
    uniform_part = jax.random.uniform(weight_key, (ROWS,), jnp.float32)
    weight_value = jnp.exp(math.log(0.004) + uniform_part * math.log(10.0))
    low_rows = (uniform_part < math.log(0.007 / 0.004) / math.log(10.0)).astype(jnp.float32)
    return (weight_value, low_rows)


def draw_obs_weight(key, part):
    return weight_plan(key)[0]


def draw_departures(key, part):
    low_rows = weight_plan(key)[1]
    key = jax.random.fold_in(key, 7)
    noise_key, scale_key, lean_key, common_key, shard_key, lowc_key = jax.random.split(key, 6)
    noise = jax.random.normal(noise_key, (ROWS, K), jnp.float32)
    lowest, highest, lean = (0.5, 2.0, 0.5)
    member_scale = jnp.exp(jax.random.uniform(scale_key, (K,), jnp.float32, math.log(lowest), math.log(highest)))
    direction = jax.random.normal(lean_key, (K,), jnp.float32) * lean
    common = jax.random.normal(common_key, (ROWS, 1), jnp.float32)
    base = noise * member_scale[None, :] + common * direction[None, :]
    base = base * (1.0 + 0.4 * low_rows[:, None])
    shard_dirs = jax.random.normal(shard_key, (PATCHES, 1, K), jnp.float32)
    low_common = jax.random.normal(lowc_key, (ROWS,), jnp.float32) * low_rows
    shard_lean = (2.0 * low_common.reshape(PATCHES, ROWS_DEV, 1) * shard_dirs).reshape(ROWS, K)
    value = base + shard_lean
    return jnp.clip(value, -8.0, 8.0).astype(jnp.bfloat16)


def shard_levels(key, dims, cuts, smallest, high):
    gain = 1.0
    for dim, shards_of in cuts:
        steps = jax.random.uniform(jax.random.fold_in(jax.random.fold_in(key, 6), dim), (shards_of,), jnp.float32, smallest / len(cuts), high / len(cuts))
        gain = gain * jnp.repeat(jnp.exp(steps), dims[dim] // shards_of).reshape((-1,) + (1,) * (len(dims) - 1 - dim))
    return gain


def centred(key, extent, scale, most, shards=(), held_as=jnp.bfloat16):
    result = scale * jax.random.normal(key, extent, jnp.float32)
    if shards:
        result = result * shard_levels(key, extent, shards, -0.22, 0.18)
    return jnp.clip(result, -most, most).astype(held_as)


def setup_inputs(seed: int = 0) -> dict:
    seeds = jax.random.split(jax.random.key(seed), 7)
    departures = draw_departures(jax.random.fold_in(seeds[6], 71), 0)
    innovation = centred(seeds[1], (ROWS,), 3.0, 12.0, ((0, 256),), jnp.float32)
    obs_weight = draw_obs_weight(jax.random.fold_in(seeds[6], 71), 0)
    send_rows = draw_send_rows(jax.random.fold_in(seeds[6], 71), 0)
    send_counts = draw_send_counts(jax.random.fold_in(seeds[6], 71), 0)
    state = centred(seeds[5], (LAT, K, LON), 1.0, 6.0, ((0, 8), (2, 32)))
    return {"departures": departures, "innovation": innovation, "obs_weight": obs_weight, "send_rows": send_rows, "send_counts": send_counts, "state": state}


def transform(gram_matrix, innov_pull):
    members = gram_matrix.shape[0]
    identity = jnp.eye(members, dtype=jnp.float32)
    system = gram_matrix + (members - 1.0) * identity
    frob_norm = jnp.sqrt(jnp.sum(system * system))
    iterate = system / frob_norm
    inverse = identity
    for sweep in range(ITERS):
        newton_step = 1.5 * identity - 0.5 * jnp.dot(inverse, iterate, precision=lax.Precision.HIGHEST)
        iterate = jnp.dot(iterate, newton_step, precision=lax.Precision.HIGHEST)
        inverse = jnp.dot(newton_step, inverse, precision=lax.Precision.HIGHEST)
    covariance = jnp.dot(inverse, inverse, precision=lax.Precision.HIGHEST) / frob_norm
    mean_shift = jnp.dot(covariance, innov_pull, precision=lax.Precision.HIGHEST)
    spread = inverse * jnp.sqrt((members - 1.0) / frob_norm)
    return mean_shift[:, None] + spread

def column_coefs(columns):
    position = (jnp.arange(columns).astype(jnp.float32) + 0.5) / columns
    left_coef = jnp.maximum(0.5 - position, 0.0)
    right_coef = jnp.maximum(position - 0.5, 0.0)
    return (left_coef, 1.0 - left_coef - right_coef, right_coef)

def analyse_block(row_block, beside_all, coefs):
    member_mean = lax.optimization_barrier(jnp.mean(row_block.astype(jnp.float32), axis=1, keepdims=True))
    perturb = (row_block.astype(jnp.float32) - member_mean).astype(jnp.bfloat16)
    total = member_mean
    for side in range(3):
        total = total + coefs[side] * jnp.einsum('ik,ric->rkc', beside_all[side].astype(jnp.float32), perturb.astype(jnp.float32))
    return total.astype(jnp.bfloat16)

def reference(departures, innovation, obs_weight, send_rows, send_counts, state):
    weight_root = jnp.sqrt(obs_weight)
    scaled = (departures.astype(jnp.float32) * weight_root[:, None]).astype(jnp.bfloat16)
    scaled_innov = (innovation * weight_root).astype(jnp.bfloat16)
    places = jnp.arange(CAP).astype(jnp.int32)
    row_base = jnp.arange(PATCHES).astype(jnp.int32) * ROWS_DEV

    def patch_weights(target):
        row_picks = (jnp.maximum(send_rows[:, target, :], 0) + row_base[:, None]).astype(jnp.int32).reshape(-1)
        live_mask = (places[None, :] < send_counts[:, target][:, None]).astype(jnp.bfloat16).reshape(-1)
        flat_rows = jnp.take(scaled, row_picks, axis=0) * live_mask[:, None]
        flat_innov = jnp.take(scaled_innov, row_picks, axis=0) * live_mask
        gram_matrix = lax.dot_general(flat_rows, flat_rows, (((0,), (0,)), ((), ())), preferred_element_type=jnp.float32)
        innov_pull = jnp.dot(flat_innov[None, :], flat_rows, preferred_element_type=jnp.float32)[0]
        return transform(gram_matrix, innov_pull).astype(jnp.bfloat16)
    weights = lax.map(patch_weights, jnp.arange(PATCHES).astype(jnp.int32))
    patch_grid = weights.reshape(N_OBS, N_GRID, K, K)
    left_grid = jnp.roll(patch_grid, 1, axis=1)
    right_grid = jnp.roll(patch_grid, -1, axis=1)
    state_split = state.reshape(N_OBS, PR, K, N_GRID, COLS)
    coefs = column_coefs(COLS)
    zero_start = jnp.zeros((), jnp.int32)

    def patch_out(patch_index):
        row_part = (patch_index // N_GRID).astype(jnp.int32)
        col_part = (patch_index % N_GRID).astype(jnp.int32)
        row_block = lax.dynamic_slice(state_split, (row_part, zero_start, zero_start, col_part, zero_start), (1, PR, K, 1, COLS)).reshape(PR, K, COLS)
        beside_all = jnp.stack([left_grid[row_part, col_part], patch_grid[row_part, col_part], right_grid[row_part, col_part]])
        return analyse_block(row_block, beside_all, coefs)
    blocks_out = lax.map(patch_out, jnp.arange(PATCHES).astype(jnp.int32))
    blocks_out = blocks_out.reshape(N_OBS, N_GRID, PR, K, COLS).transpose(0, 2, 3, 1, 4)
    return blocks_out.reshape(LAT, K, LON)
```

```python
import functools

import jax
import jax.numpy as jnp
from jax import lax
from jax.experimental import pallas as pl
from jax.experimental.pallas import tpu as pltpu
from jax.sharding import PartitionSpec as P

ITERS = 6
Y, X, CORES = 4, 4, 2
F32, BF16 = jnp.float32, jnp.bfloat16
K = 128
LOW = 512
BLOCKS = 4
TABLE = BLOCKS * K + 16
PACK = 112
VMEM = 48 * 1024 * 1024


def hop(value, dy, dx, dc):
    pairs = []
    for place in range(Y * X * CORES):
        y, x, c = place // (X * CORES), place // CORES % X, place % CORES
        pairs.append((place, ((y + dy) % Y * X + (x + dx) % X) * CORES + (c ^ dc)))
    return lax.ppermute(value, "grid", pairs)


def dims(m, n):
    return (((m,), (n,)), ((), ()))


def table_kernel(departures, innovation, obs_weight, table):
    root = jnp.sqrt(obs_weight[...].reshape(1, BLOCKS * LOW))
    innov = innovation[...].reshape(1, BLOCKS * LOW) * root
    row = lax.broadcasted_iota(jnp.int32, (16, LOW), 0)
    tail = jnp.zeros((16, LOW), F32)
    for block in range(BLOCKS):
        span = slice(block * LOW, (block + 1) * LOW)
        rows = departures[span, :].astype(F32).T * root[:, span]
        table[block * K : (block + 1) * K, :] = rows.astype(BF16)
        tail = jnp.where(row == block, innov[:, span], tail)
    table[BLOCKS * K :, :] = tail.astype(BF16)


def make_table(departures, innovation, obs_weight):
    return pl.pallas_call(
        table_kernel,
        out_shape=jax.ShapeDtypeStruct((TABLE, LOW), BF16),
        cost_estimate=pl.CostEstimate(flops=2_000_000, bytes_accessed=1_000_000, transcendentals=0),
    )(departures, innovation, obs_weight)


def picks_kernel(place, send_rows, *parts):
    x, c = place[0], place[1]
    for part in range(X * CORES):
        dx, dc = part // CORES, part % CORES
        cx = lax.rem(x + dx, X) * CORES + jnp.bitwise_xor(c, dc)
        for y in range(Y):
            rows = send_rows[pl.ds(y * X * CORES + cx, 8, stride=Y * X * CORES), :]
            pairs = jnp.concatenate([rows[0:4], rows[4:8]], axis=1)
            parts[part][2 * y : 2 * y + 2, :] = jnp.concatenate([pairs[0:2], pairs[2:4]], axis=1)


def make_picks(place, send_rows):
    vmem = pl.BlockSpec(memory_space=pltpu.VMEM)
    return pl.pallas_call(
        picks_kernel,
        out_shape=[jax.ShapeDtypeStruct((8, 256), jnp.int32)] * (X * CORES),
        in_specs=[pl.BlockSpec(memory_space=pltpu.SMEM), vmem],
        out_specs=[vmem] * (X * CORES),
        cost_estimate=pl.CostEstimate(flops=2_000_000, bytes_accessed=200_000, transcendentals=0),
    )(place, send_rows)


def pick(tables, picks):
    high = lax.shift_right_arithmetic(picks, 9)
    low = jnp.where(picks >= 0, jnp.bitwise_and(picks, LOW - 1), -1)
    one_hot = (lax.broadcasted_iota(jnp.int32, (LOW, 256), 0) == low).astype(BF16)
    found = [jnp.dot(part[...], one_hot, preferred_element_type=F32) for part in tables]
    blocks = []
    for part in found:
        blocks += [part[i * K : (i + 1) * K] for i in range(part.shape[0] // K)]
    tail = found[-1][-16:]
    members, innov = blocks[0], tail[0:1]
    for block in range(1, BLOCKS):
        here = high == block
        members = jnp.where(here, blocks[block], members)
        innov = jnp.where(here, tail[block : block + 1], innov)
    return jnp.concatenate([members, jnp.broadcast_to(innov, (16, 256))], axis=0).astype(BF16)


def grams(first, second, first_picks, second_picks):
    a, b = pick(first, first_picks), pick(second, second_picks)
    even = lax.broadcasted_iota(jnp.int32, (K, 256), 1) % K < K // 2
    totals = []
    for half in range(2):
        span = slice(half * K, (half + 1) * K)
        both = jnp.concatenate([a[:, span], b[:, span]], axis=1)
        rows = both[:K]
        none = jnp.zeros_like(rows)
        split = jnp.concatenate([jnp.where(even, rows, none), jnp.where(even, none, rows)], axis=0)
        totals.append(lax.dot_general(both, split, dims(1, 1), preferred_element_type=F32))
    return totals


def partial_kernel(chained, first, second, first_picks, second_picks, *rest):
    step = pl.program_id(0)
    out = rest[-1]
    picks = [ref[pl.ds(step, 1), :] for ref in (first_picks, second_picks)]
    totals = grams([first], [second], *picks)
    for half in range(2):
        out[0, half] = totals[half] + rest[0][0, half] if chained else totals[half]


def partial_grams(first, second, first_picks, second_picks, before=None):
    whole = lambda shape: pl.BlockSpec(shape, lambda i: (0,) * len(shape))
    spec = pl.BlockSpec((1, 2, 144, 256), lambda i: (i, 0, 0, 0))
    chained = before is not None
    args = (first, second, first_picks, second_picks) + ((before,) if chained else ())
    return pl.pallas_call(
        functools.partial(partial_kernel, chained),
        grid=(8,),
        out_shape=jax.ShapeDtypeStruct((8, 2, 144, 256), F32),
        in_specs=[whole((TABLE, LOW))] * 2 + [whole((8, 256))] * 2 + [spec] * chained,
        out_specs=spec,
        compiler_params=pltpu.CompilerParams(vmem_limit_bytes=VMEM),
        cost_estimate=pl.CostEstimate(
            flops=2 * 2 * TABLE * LOW * 2048, bytes_accessed=4_000_000, transcendentals=0
        ),
    )(*args)


def pack(total, side):
    gram = total[0:K, side * K : (side + 1) * K]
    lane = lax.broadcasted_iota(jnp.int32, (32, K), 1)
    fold = jnp.where(lane < 64, pltpu.roll(gram[64:96], 64, 1), gram[96:128])
    return jnp.concatenate([gram[0:64], fold, total[K : K + 16, side * K : (side + 1) * K]], axis=0)


def unpack(packed):
    lane = lax.broadcasted_iota(jnp.int32, (64, K), 1)
    fold = packed[64:96]
    lower = jnp.where(lane >= 64, jnp.concatenate([pltpu.roll(fold, 64, 1), fold], axis=0), 0.0)
    corner = jnp.concatenate([jnp.where(lane >= 64, packed[0:64], 0.0), jnp.zeros_like(lower)], axis=0)
    return jnp.concatenate([packed[0:64], lower], axis=0) + corner.T, packed[96:97]


def last_kernel(count, shift, place, a_low, a_high, b_low, b_high, a_picks, b_picks, before, *outs):
    step = pl.program_id(0)
    part = step // 2
    row = 2 * lax.rem(place[0] + shift(part), Y) + step % 2
    picks = [ref[pl.ds(row, 1), :] for ref in (a_picks, b_picks)]
    totals = grams([a_low, a_high], [b_low, b_high], *picks)
    totals = [totals[half] + before[0, half] for half in range(2)]
    for which in range(count):

        @pl.when(part == which)
        def _():
            for half in range(2):
                for side in range(2):
                    patch = step % 2 + 2 * half + 4 * side
                    outs[which][patch] = pack(totals[half], side).astype(outs[which].dtype)


def last_grams(shifts, dtype, place, tables, picks, before):
    whole = lambda shape: pl.BlockSpec(shape, lambda i, p: (0,) * len(shape))
    count = len(shifts)

    def shift(part):
        value = jnp.int32(shifts[0])
        for which in range(1, count):
            value = jnp.where(part == which, shifts[which], value)
        return value

    def block(i, p):
        return (2 * lax.rem(p[0] + shift(i // 2), Y) + i % 2, 0, 0, 0)

    return pl.pallas_call(
        functools.partial(last_kernel, count, shift),
        grid_spec=pltpu.PrefetchScalarGridSpec(
            num_scalar_prefetch=1,
            grid=(2 * count,),
            in_specs=[whole((256, LOW)), whole((272, LOW))] * 2
            + [whole((8, 256))] * 2
            + [pl.BlockSpec((1, 2, 144, 256), block)],
            out_specs=[whole((8, PACK, K))] * count,
        ),
        out_shape=[jax.ShapeDtypeStruct((8, PACK, K), dtype)] * count,
        compiler_params=pltpu.CompilerParams(vmem_limit_bytes=VMEM),
        cost_estimate=pl.CostEstimate(
            flops=count * 2 * TABLE * LOW * 1024, bytes_accessed=3_000_000, transcendentals=0
        ),
    )(place, *tables, *picks, before)


def spread_kernel(place, own, a, b, c, *outs):
    for part in range(8):
        row = lax.rem(place[0] + part, 8)
        total = own[row] + a[row].astype(F32) + b[row].astype(F32) + c[row].astype(F32)
        outs[part][...] = total.astype(outs[part].dtype)


def spread(place, own, others):
    vmem = pl.BlockSpec(memory_space=pltpu.VMEM)
    return pl.pallas_call(
        spread_kernel,
        out_shape=[jax.ShapeDtypeStruct((PACK, K), F32)]
        + [jax.ShapeDtypeStruct((PACK, K), BF16)] * 7,
        in_specs=[pl.BlockSpec(memory_space=pltpu.SMEM)] + [vmem] * 4,
        out_specs=[vmem] * 8,
    )(place, own, *others)


def split(value):
    high = value.astype(BF16)
    return high, (value - high.astype(F32)).astype(BF16)


def product(left, right):
    lh, ll = split(left)
    rh, rl = split(right)
    return jnp.dot(
        jnp.concatenate([lh, lh, ll], axis=1),
        jnp.concatenate([rh, rl, rh], axis=0),
        preferred_element_type=F32,
    )


def weights_kernel(own, *rest):
    out = rest[-1]
    total = own[...]
    for ref in rest[:-1]:
        total = total + ref[...].astype(F32)
    gram, pull = unpack(total)
    row = lax.broadcasted_iota(jnp.int32, (K, K), 0)
    col = lax.broadcasted_iota(jnp.int32, (K, K), 1)
    identity = (row == col).astype(F32)
    system = gram + (K - 1.0) * identity
    squares = jnp.sum(jnp.sum(system * system, axis=0, keepdims=True), axis=1, keepdims=True)
    frob = jnp.sqrt(squares)
    iterate = system / frob
    inverse = 1.5 * identity - 0.5 * iterate
    iterate = product(inverse, iterate)
    for sweep in range(1, ITERS):
        newton = 1.5 * identity - 0.5 * product(inverse, iterate)
        if sweep < ITERS - 1:
            both = product(newton, jnp.concatenate([iterate, inverse], axis=1))
            iterate, inverse = both[:, :K], both[:, K:]
        else:
            inverse = product(newton, inverse)
    shift = product(product(jnp.broadcast_to(pull, (16, K)), inverse), inverse)[0:1] / frob
    out[...] = (jnp.sqrt((K - 1.0) / frob) * inverse.T + shift).astype(BF16)


def transposed_weights(parts):
    return pl.pallas_call(
        weights_kernel,
        out_shape=jax.ShapeDtypeStruct((K, K), BF16),
    )(*parts)


def analysis_kernel(own, left, right, state, out):
    rows = state.shape[0]
    weights = jnp.concatenate([own[...], left[...], right[...]], axis=0)
    lane = lax.broadcasted_iota(jnp.int32, (1, 2 * K), 1) % K
    position = (lane.astype(F32) + 0.5) / K
    left_coef = jnp.maximum(0.5 - position, 0.0)
    right_coef = jnp.maximum(position - 0.5, 0.0)
    own_coef = 1.0 - left_coef - right_coef
    side_coef = left_coef + right_coef
    is_left = lane < K // 2
    for pair in range(rows // 2):
        values = [state[2 * pair + i].astype(F32) for i in range(2)]
        means = [jnp.mean(value, axis=0, keepdims=True) for value in values]
        mean = jnp.concatenate(means, axis=1)
        perturb = jnp.concatenate(
            [(values[i] - means[i]).astype(BF16) for i in range(2)], axis=1
        )
        sums = jnp.dot(weights, perturb, preferred_element_type=F32)
        side = jnp.where(is_left, sums[K : 2 * K], sums[2 * K :])
        total = (mean + own_coef * sums[:K] + side_coef * side).astype(BF16)
        for i in range(2):
            out[2 * pair + i] = total[:, i * K : (i + 1) * K]


def analyse(own, left, right, state):
    rows = state.shape[0]
    tile = 8
    small = pl.BlockSpec((K, K), lambda i: (0, 0))
    large = pl.BlockSpec((tile, K, K), lambda i: (i, 0, 0))
    return pl.pallas_call(
        analysis_kernel,
        grid=(rows // tile,),
        out_shape=jax.ShapeDtypeStruct(state.shape, BF16),
        in_specs=[small] * 3 + [large],
        out_specs=large,
        compiler_params=pltpu.CompilerParams(vmem_limit_bytes=VMEM),
        cost_estimate=pl.CostEstimate(
            flops=6 * rows * K * K * K, bytes_accessed=4 * rows * K * K, transcendentals=0
        ),
    )(own, left, right, state)


def on_device(departures, innovation, obs_weight, send_rows, send_counts, state):
    n_obs = lax.axis_size("obs")
    n_grid = lax.axis_size("grid")
    z = lax.axis_index("obs")
    g = lax.axis_index("grid")
    x_and_core = jnp.stack([g // CORES % X, g % CORES]).astype(jnp.int32)
    y_place = (g // (X * CORES)).astype(jnp.int32).reshape(1)
    z_place = z.astype(jnp.int32).reshape(1)

    table = make_table(departures, innovation, obs_weight)
    left = hop(table, 0, 1, 0)
    right = hop(table, 0, -1, 0)
    other = hop(table, 0, 0, 1)

    mine = make_picks(x_and_core, send_rows[0])
    picks = [
        mine[part] if part == 0 else hop(mine[part], 0, part // CORES, part % CORES)
        for part in range(X * CORES)
    ]
    totals = partial_grams(table, other, picks[0], picks[1])

    far_low = hop(left[:256], 0, 1, 0)
    far_high = hop(right[256:], 0, -1, 0)
    left_other = hop(left, 0, 0, 1)
    right_other = hop(right, 0, 0, 1)
    totals = partial_grams(left, right, picks[2], picks[6], totals)
    totals = partial_grams(left_other, right_other, picks[3], picks[7], totals)
    far = (far_low, far_high, hop(far_low, 0, 0, 1), hop(far_high, 0, 0, 1))

    sent = last_grams((2, 1, 3), BF16, y_place, far, (picks[4], picks[5]), totals)
    kept = last_grams((0,), F32, y_place, far, (picks[4], picks[5]), totals)[0]
    arrived = [hop(part, shift, 0, 0) for part, shift in zip(sent, (2, 1, 3))]

    parts = spread(z_place, kept, arrived)
    parts = [parts[0]] + [
        lax.ppermute(parts[i], "obs", [(j, (j + i) % n_obs) for j in range(n_obs)])
        for i in range(1, n_obs)
    ]
    own = transposed_weights(parts)
    low = lax.ppermute(own, "grid", [(j, (j + 1) % n_grid) for j in range(n_grid)])
    high = lax.ppermute(own, "grid", [(j, (j - 1) % n_grid) for j in range(n_grid)])
    return analyse(own, low, high, state)


def solution(mesh):
    in_specs = (
        P(("obs", "grid"), None),
        P(("obs", "grid")),
        P(("obs", "grid")),
        P(("obs", "grid"), None, None),
        P(("obs", "grid"), None),
        P("obs", None, "grid"),
    )
    out_specs = P("obs", None, "grid")
    return jax.shard_map(
        on_device, mesh=mesh, in_specs=in_specs, out_specs=out_specs, check_vma=False
    )
```

```python
import functools

import jax
import jax.numpy as jnp
from jax import lax
from jax.experimental import pallas as pl
from jax.experimental.pallas import tpu as pltpu
from jax.sharding import PartitionSpec as P

ITERS = 6
Y, X, CORES = 4, 4, 2
F32, BF16 = jnp.float32, jnp.bfloat16
K = 128
LOW = 512
BLOCKS = 4
TABLE = BLOCKS * K + 16
PACK = 112
VMEM = 20 * 1024 * 1024


def params():
    return pltpu.CompilerParams(vmem_limit_bytes=VMEM)


def cost(flops):
    return pl.CostEstimate(flops=int(flops), bytes_accessed=4_000_000, transcendentals=0)


def in_vmem(count):
    return [pl.BlockSpec(memory_space=pltpu.VMEM)] * count


def hop(value, dy, dx, dc):
    pairs = []
    for place in range(Y * X * CORES):
        y, x, c = place // (X * CORES), place // CORES % X, place % CORES
        pairs.append((place, ((y + dy) % Y * X + (x + dx) % X) * CORES + (c ^ dc)))
    return lax.ppermute(value, "grid", pairs)


def dims(m, n):
    return (((m,), (n,)), ((), ()))


def message_kernel(departures, innovation, obs_weight, send_rows, near, to_right, to_left, turned):
    grid = lax.axis_index("grid")
    x, c = lax.rem(lax.div(grid, CORES), X), lax.rem(grid, CORES)
    turned[...] = send_rows[...].T
    groups = []
    for dx in range(X):
        halves = []
        for dc in range(CORES):
            cx = lax.rem(x + dx, X) * CORES + lax.rem(c + dc, CORES)
            lines = []
            for y in range(Y):
                rows = turned[pl.ds(y * X * CORES + cx, 8, stride=Y * X * CORES), :]
                pairs = jnp.concatenate([rows[0:4], rows[4:8]], axis=1)
                fours = jnp.concatenate([pairs[0:2], pairs[2:4]], axis=1)
                lines.append(jnp.concatenate([fours[0:1], fours[1:2]], axis=1))
            picks = jnp.concatenate(lines, axis=0)
            halves.append(lax.shift_right_arithmetic(picks, 8))
            halves.append(jnp.bitwise_and(picks, 255))
        groups.append(jnp.concatenate(halves, axis=0).astype(F32).astype(BF16))
    near[TABLE:, :] = groups[0]
    to_right[:16, :] = groups[2]
    to_right[16 + TABLE :, :] = groups[1]
    to_left[TABLE:, :] = groups[3]
    root = jnp.sqrt(obs_weight[...].reshape(1, BLOCKS * LOW))
    innov = innovation[...].reshape(1, BLOCKS * LOW) * root
    row = lax.broadcasted_iota(jnp.int32, (16, LOW), 0)
    tail = jnp.zeros((16, LOW), F32)
    for block in range(BLOCKS):
        span = slice(block * LOW, (block + 1) * LOW)
        rows = (departures[span, :].astype(F32).T * root[:, span]).astype(BF16)
        near[block * K : (block + 1) * K, :] = rows
        to_right[16 + block * K : 16 + (block + 1) * K, :] = rows
        to_left[block * K : (block + 1) * K, :] = rows
        tail = jnp.where(row == block, innov[:, span], tail)
    tail = tail.astype(BF16)
    near[BLOCKS * K : TABLE, :] = tail
    to_right[16 + BLOCKS * K : 16 + TABLE, :] = tail
    to_left[BLOCKS * K : TABLE, :] = tail


def make_messages(departures, innovation, obs_weight, send_rows):
    return pl.pallas_call(
        message_kernel,
        out_shape=[
            jax.ShapeDtypeStruct((TABLE + extra, LOW), BF16) for extra in (16, 32, 16)
        ],
        in_specs=in_vmem(4),
        out_specs=in_vmem(3),
        scratch_shapes=[pltpu.VMEM((send_rows.shape[1], send_rows.shape[0]), jnp.int32)],
        compiler_params=params(),
        cost_estimate=cost(2e9),
    )(departures, innovation, obs_weight, send_rows)


def read_picks(group, core):
    values = group[8 * core : 8 * core + 8].astype(F32)
    return (values[0:4] * 256.0 + values[4:8]).astype(jnp.int32)


def pick(tables, picks):
    high = lax.shift_right_arithmetic(picks, 9)
    low = jnp.where(picks >= 0, jnp.bitwise_and(picks, LOW - 1), -1)
    one_hot = (lax.broadcasted_iota(jnp.int32, (LOW, 256), 0) == low).astype(BF16)
    found = [jnp.dot(part, one_hot, preferred_element_type=F32) for part in tables]
    blocks = []
    for part in found:
        blocks += [part[i * K : (i + 1) * K] for i in range(part.shape[0] // K)]
    tail = found[-1][-16:]
    members, innov = blocks[0], tail[0:1]
    for block in range(1, BLOCKS):
        here = high == block
        members = jnp.where(here, blocks[block], members)
        innov = jnp.where(here, tail[block : block + 1], innov)
    return jnp.concatenate([members, jnp.broadcast_to(innov, (16, 256))], axis=0).astype(BF16)


def grams(first, second, first_picks, second_picks):
    a, b = pick(first, first_picks), pick(second, second_picks)
    even = lax.broadcasted_iota(jnp.int32, (K, 256), 1) % K < K // 2
    totals = []
    for half in range(2):
        span = slice(half * K, (half + 1) * K)
        both = jnp.concatenate([a[:, span], b[:, span]], axis=1)
        rows = both[:K]
        none = jnp.zeros_like(rows)
        split = jnp.concatenate([jnp.where(even, rows, none), jnp.where(even, none, rows)], axis=0)
        totals.append(lax.dot_general(both, split, dims(1, 1), preferred_element_type=F32))
    return totals


def partial_kernel(starts, cores, first, second, *rest):
    out = rest[-1]
    messages = (first, second)
    picks = [
        read_picks(ref[at : at + 16, :], core)
        for ref, (_, at), core in zip(messages, starts, cores)
    ]
    for step in range(2 * Y):
        y, span = step // 2, slice(step % 2 * 256, step % 2 * 256 + 256)
        tables = [[ref[at : at + TABLE, :]] for ref, (at, _) in zip(messages, starts)]
        totals = grams(*tables, picks[0][y : y + 1, span], picks[1][y : y + 1, span])
        for half in range(2):
            if len(rest) > 1:
                out[step, half] = totals[half] + rest[0][step, half]
            else:
                out[step, half] = totals[half]


def partial_grams(starts, cores, *args):
    return pl.pallas_call(
        functools.partial(partial_kernel, starts, cores),
        out_shape=jax.ShapeDtypeStruct((2 * Y, 2, 144, 256), F32),
        in_specs=in_vmem(len(args)),
        out_specs=in_vmem(1)[0],
        compiler_params=params(),
        cost_estimate=cost(4e9),
    )(*args)


def pack(total, side):
    gram = total[0:K, side * K : (side + 1) * K]
    lane = lax.broadcasted_iota(jnp.int32, (32, K), 1)
    fold = jnp.where(lane < 64, pltpu.roll(gram[64:96], 64, 1), gram[96:128])
    return jnp.concatenate([gram[0:64], fold, total[K : K + 16, side * K : (side + 1) * K]], axis=0)


def unpack(packed):
    lane = lax.broadcasted_iota(jnp.int32, (64, K), 1)
    fold = packed[64:96]
    lower = jnp.where(lane >= 64, jnp.concatenate([pltpu.roll(fold, 64, 1), fold], axis=0), 0.0)
    corner = jnp.concatenate([jnp.where(lane >= 64, packed[0:64], 0.0), jnp.zeros_like(lower)], axis=0)
    return jnp.concatenate([packed[0:64], lower], axis=0) + corner.T, packed[96:97]


def last_kernel(shifts, lowest, a_low, a_high, b_low, b_high, before, *rest):
    outs, a_picks, b_picks = rest[:-2], rest[-2], rest[-1]
    place = lax.div(lax.axis_index("grid"), X * CORES)
    a_picks[...] = read_picks(a_low[0:16, :], 0)
    b_picks[...] = read_picks(b_low[0:16, :], 1)
    tables = [[low[16:, :], high[...]] for low, high in ((a_low, a_high), (b_low, b_high))]
    for shift in sorted(set(shifts)):
        y = lax.rem(place + shift, Y)
        for i in range(2):
            span = slice(i * 256, i * 256 + 256)
            picks = [ref[pl.ds(y, 1), :][:, span] for ref in (a_picks, b_picks)]
            totals = grams(*tables, *picks)
            for half in range(2):
                total = totals[half] + before[2 * y + i, half]
                for side in range(2):
                    patch = i + 2 * half + 4 * side
                    for out, its_shift, low in zip(outs, shifts, lowest):
                        if its_shift == shift and low <= patch < low + out.shape[0]:
                            out[patch - low] = pack(total, side).astype(out.dtype)


def last_grams(shifts, lowest, counts, dtype, tables, before):
    return pl.pallas_call(
        functools.partial(last_kernel, shifts, lowest),
        out_shape=[jax.ShapeDtypeStruct((count, PACK, K), dtype) for count in counts],
        in_specs=in_vmem(5),
        out_specs=in_vmem(len(counts)),
        scratch_shapes=[pltpu.VMEM((Y, LOW), jnp.int32)] * 2,
        compiler_params=params(),
        cost_estimate=cost(1e9 * len(set(shifts))),
    )(*tables, before)


def relay_kernel(up, down, from_up, from_down, out_up, out_down):
    half = from_up.shape[0]
    out_up[:half] = (up[:half] + from_up[...].astype(F32)).astype(BF16)
    out_up[half:] = up[half:].astype(BF16)
    out_down[:half] = down[:half].astype(BF16)
    out_down[half:] = (down[half:] + from_down[...].astype(F32)).astype(BF16)


def relay(*args):
    return pl.pallas_call(
        relay_kernel,
        out_shape=[jax.ShapeDtypeStruct(args[0].shape, BF16)] * 2,
        in_specs=in_vmem(4),
        out_specs=in_vmem(2),
        compiler_params=params(),
        cost_estimate=cost(5e8),
    )(*args)


def sum_kernel(own, a, b, out):
    out[...] = (own[...] + a[...].astype(F32) + b[...].astype(F32)).astype(BF16)


def sum_parts(*args):
    return pl.pallas_call(
        sum_kernel,
        out_shape=jax.ShapeDtypeStruct(args[0].shape, BF16),
        in_specs=in_vmem(3),
        out_specs=in_vmem(1)[0],
        compiler_params=params(),
        cost_estimate=cost(5e8),
    )(*args)


def split(value):
    high = value.astype(BF16)
    return high, (value - high.astype(F32)).astype(BF16)


def product(left, right):
    lh, ll = split(left)
    rh, rl = split(right)
    return jnp.dot(
        jnp.concatenate([lh, lh, ll], axis=1),
        jnp.concatenate([rh, rl, rh], axis=0),
        preferred_element_type=F32,
    )


def weights_kernel(parts, out):
    gram, pull = unpack(jnp.sum(parts[...].astype(F32), axis=0))
    row = lax.broadcasted_iota(jnp.int32, (K, K), 0)
    col = lax.broadcasted_iota(jnp.int32, (K, K), 1)
    identity = (row == col).astype(F32)
    system = gram + (K - 1.0) * identity
    squares = jnp.sum(jnp.sum(system * system, axis=0, keepdims=True), axis=1, keepdims=True)
    frob = jnp.sqrt(squares)
    iterate = system / frob
    inverse = 1.5 * identity - 0.5 * iterate
    iterate = product(inverse, iterate)
    for sweep in range(1, ITERS):
        newton = 1.5 * identity - 0.5 * product(inverse, iterate)
        if sweep < ITERS - 1:
            both = product(newton, jnp.concatenate([iterate, inverse], axis=1))
            iterate, inverse = both[:, :K], both[:, K:]
        else:
            inverse = product(newton, inverse)
    shift = product(product(jnp.broadcast_to(pull, (16, K)), inverse), inverse)[0:1] / frob
    out[...] = (jnp.sqrt((K - 1.0) / frob) * inverse.T + shift).astype(BF16)


def transposed_weights(parts):
    return pl.pallas_call(
        weights_kernel,
        out_shape=jax.ShapeDtypeStruct((K, K), BF16),
        in_specs=in_vmem(1),
        out_specs=in_vmem(1)[0],
        compiler_params=params(),
        cost_estimate=cost(4e9),
    )(parts)


def analysis_kernel(own, left, right, state, out):
    rows = state.shape[0]
    weights = jnp.concatenate([own[...], left[...], right[...]], axis=0)
    lane = lax.broadcasted_iota(jnp.int32, (1, 2 * K), 1) % K
    position = (lane.astype(F32) + 0.5) / K
    left_coef = jnp.maximum(0.5 - position, 0.0)
    right_coef = jnp.maximum(position - 0.5, 0.0)
    own_coef = 1.0 - left_coef - right_coef
    side_coef = left_coef + right_coef
    is_left = lane < K // 2
    for pair in range(rows // 2):
        values = [state[2 * pair + i].astype(F32) for i in range(2)]
        means = [jnp.mean(value, axis=0, keepdims=True) for value in values]
        mean = jnp.concatenate(means, axis=1)
        perturb = jnp.concatenate(
            [(values[i] - means[i]).astype(BF16) for i in range(2)], axis=1
        )
        sums = jnp.dot(weights, perturb, preferred_element_type=F32)
        side = jnp.where(is_left, sums[K : 2 * K], sums[2 * K :])
        total = (mean + own_coef * sums[:K] + side_coef * side).astype(BF16)
        for i in range(2):
            out[2 * pair + i] = total[:, i * K : (i + 1) * K]


def analyse(own, left, right, state):
    rows = state.shape[0]
    tile = 8
    small = pl.BlockSpec((K, K), lambda i: (0, 0))
    large = pl.BlockSpec((tile, K, K), lambda i: (i, 0, 0))
    return pl.pallas_call(
        analysis_kernel,
        grid=(rows // tile,),
        out_shape=jax.ShapeDtypeStruct(state.shape, BF16),
        in_specs=[small] * 3 + [large],
        out_specs=large,
        compiler_params=params(),
        cost_estimate=pl.CostEstimate(
            flops=6 * rows * K * K * K, bytes_accessed=4 * rows * K * K, transcendentals=0
        ),
    )(own, left, right, state)


def on_device(departures, innovation, obs_weight, send_rows, send_counts, state):
    n_grid = lax.axis_size("grid")
    near, to_right, to_left = make_messages(departures, innovation, obs_weight, send_rows[0].T)
    other = hop(near, 0, 0, 1)
    left = hop(to_right, 0, 1, 0)
    right = hop(to_left, 0, -1, 0)

    at_end, at_middle = (0, TABLE), (16, 16 + TABLE)
    totals = partial_grams((at_end, at_end), (0, 1), near, other)
    left, right, totals = lax.optimization_barrier((left, right, totals))

    far_low = hop(left[:272], 0, 1, 0)
    far_high = hop(right[256:TABLE], 0, -1, 0)
    left_other = hop(left, 0, 0, 1)
    right_other = hop(right, 0, 0, 1)
    totals = partial_grams((at_middle, at_end), (0, 0), left, right, totals)
    far_low, far_high, left_other, right_other, totals = lax.optimization_barrier(
        (far_low, far_high, left_other, right_other, totals)
    )
    far = (far_low, far_high, hop(far_low, 0, 0, 1), hop(far_high, 0, 0, 1))
    totals = partial_grams((at_middle, at_end), (1, 1), left_other, right_other, totals)

    up, down = last_grams((2, 2), (0, 4), (4, 4), BF16, far, totals)
    from_up, from_down = hop(up, 1, 0, 0), hop(down, -1, 0, 0)
    up, down = last_grams((1, 3), (0, 0), (8, 8), F32, far, totals)
    up, down = relay(up, down, from_up, from_down)
    from_up, from_down = hop(up, 1, 0, 0), hop(down, -1, 0, 0)
    own = last_grams((0,), (0,), (8,), F32, far, totals)[0]
    parts = sum_parts(own, from_up, from_down)
    parts = lax.all_to_all(parts, "obs", 0, 0, tiled=True)

    own = transposed_weights(parts)
    low = lax.ppermute(own, "grid", [(j, (j + 1) % n_grid) for j in range(n_grid)])
    high = lax.ppermute(own, "grid", [(j, (j - 1) % n_grid) for j in range(n_grid)])
    return analyse(own, low, high, state)


def solution(mesh):
    in_specs = (
        P(("obs", "grid"), None),
        P(("obs", "grid")),
        P(("obs", "grid")),
        P(("obs", "grid"), None, None),
        P(("obs", "grid"), None),
        P("obs", None, "grid"),
    )
    out_specs = P("obs", None, "grid")
    return jax.shard_map(
        on_device, mesh=mesh, in_specs=in_specs, out_specs=out_specs, check_vma=False
    )
```

```python
import functools

import jax
import jax.numpy as jnp
from jax import lax
from jax.experimental import pallas as pl
from jax.experimental.pallas import tpu as pltpu
from jax.sharding import PartitionSpec as P

ITERS = 6
Y, X, CORES = 4, 4, 2
F32, BF16 = jnp.float32, jnp.bfloat16
K = 128
LOW = 512
BLOCKS = 4
TABLE = BLOCKS * K + 16
PACK = 112
VMEM = 20 * 1024 * 1024


def params():
    return pltpu.CompilerParams(vmem_limit_bytes=VMEM)


def cost(flops):
    return pl.CostEstimate(flops=int(flops), bytes_accessed=4_000_000, transcendentals=0)


def in_vmem(count):
    return [pl.BlockSpec(memory_space=pltpu.VMEM)] * count


def hop(value, dy, dx, dc):
    pairs = []
    for place in range(Y * X * CORES):
        y, x, c = place // (X * CORES), place // CORES % X, place % CORES
        pairs.append((place, ((y + dy) % Y * X + (x + dx) % X) * CORES + (c ^ dc)))
    return lax.ppermute(value, "grid", pairs)


def dims(m, n):
    return (((m,), (n,)), ((), ()))


def message_kernel(*refs):
    sources, (near, to_right, to_left), held = refs[:4], refs[4:7], refs[7:11]
    turned, sems = refs[11:]
    copies = [
        pltpu.make_async_copy(source, place, sems.at[i])
        for i, (source, place) in enumerate(zip(sources, held))
    ]
    for copy in copies[::-1]:
        copy.start()
    departures, innovation, obs_weight, send_rows = held
    copies[3].wait()
    grid = lax.axis_index("grid")
    x, c = lax.rem(lax.div(grid, CORES), X), lax.rem(grid, CORES)
    turned[...] = send_rows[...].T
    groups = []
    for dx in range(X):
        halves = []
        for dc in range(CORES):
            cx = lax.rem(x + dx, X) * CORES + lax.rem(c + dc, CORES)
            lines = []
            for y in range(Y):
                rows = turned[pl.ds(y * X * CORES + cx, 8, stride=Y * X * CORES), :]
                pairs = jnp.concatenate([rows[0:4], rows[4:8]], axis=1)
                fours = jnp.concatenate([pairs[0:2], pairs[2:4]], axis=1)
                lines.append(jnp.concatenate([fours[0:1], fours[1:2]], axis=1))
            picks = jnp.concatenate(lines, axis=0)
            halves.append(lax.shift_right_arithmetic(picks, 8))
            halves.append(jnp.bitwise_and(picks, 255))
        groups.append(jnp.concatenate(halves, axis=0).astype(F32).astype(BF16))
    near[TABLE:, :] = groups[0]
    to_right[:16, :] = groups[2]
    to_right[16 + TABLE :, :] = groups[1]
    to_left[TABLE:, :] = groups[3]
    for copy in copies[:3]:
        copy.wait()
    root = jnp.sqrt(obs_weight[...].reshape(1, BLOCKS * LOW))
    innov = innovation[...].reshape(1, BLOCKS * LOW) * root
    row = lax.broadcasted_iota(jnp.int32, (16, LOW), 0)
    tail = jnp.zeros((16, LOW), F32)
    for block in range(BLOCKS):
        span = slice(block * LOW, (block + 1) * LOW)
        rows = (departures[span, :].astype(F32).T * root[:, span]).astype(BF16)
        near[block * K : (block + 1) * K, :] = rows
        to_right[16 + block * K : 16 + (block + 1) * K, :] = rows
        to_left[block * K : (block + 1) * K, :] = rows
        tail = jnp.where(row == block, innov[:, span], tail)
    tail = tail.astype(BF16)
    near[BLOCKS * K : TABLE, :] = tail
    to_right[16 + BLOCKS * K : 16 + TABLE, :] = tail
    to_left[BLOCKS * K : TABLE, :] = tail


def make_messages(*args):
    return pl.pallas_call(
        message_kernel,
        out_shape=[
            jax.ShapeDtypeStruct((TABLE + extra, LOW), BF16) for extra in (16, 32, 16)
        ],
        in_specs=[pl.BlockSpec(memory_space=pltpu.HBM)] * 4,
        out_specs=in_vmem(3),
        scratch_shapes=[pltpu.VMEM(arg.shape, arg.dtype) for arg in args]
        + [pltpu.VMEM(args[3].shape[::-1], jnp.int32), pltpu.SemaphoreType.DMA((4,))],
        compiler_params=pltpu.CompilerParams(vmem_limit_bytes=60 * 1024 * 1024),
        cost_estimate=cost(2e9),
    )(*args)


def read_picks(group, core):
    values = group[8 * core : 8 * core + 8].astype(F32)
    return (values[0:4] * 256.0 + values[4:8]).astype(jnp.int32)


def pick(tables, picks):
    high = lax.shift_right_arithmetic(picks, 9)
    low = jnp.where(picks >= 0, jnp.bitwise_and(picks, LOW - 1), -1)
    one_hot = (lax.broadcasted_iota(jnp.int32, (LOW, 256), 0) == low).astype(BF16)
    found = [jnp.dot(part, one_hot, preferred_element_type=F32) for part in tables]
    blocks = []
    for part in found:
        blocks += [part[i * K : (i + 1) * K] for i in range(part.shape[0] // K)]
    tail = found[-1][-16:]
    members, innov = blocks[0], tail[0:1]
    for block in range(1, BLOCKS):
        here = high == block
        members = jnp.where(here, blocks[block], members)
        innov = jnp.where(here, tail[block : block + 1], innov)
    return jnp.concatenate([members, jnp.broadcast_to(innov, (16, 256))], axis=0).astype(BF16)


def grams(tables, picks):
    found = [pick(*pair) for pair in zip(tables, picks)]
    lane = lax.broadcasted_iota(jnp.int32, (K, len(found) * K), 1)
    even = lane % K < K // 2
    totals = []
    for half in range(2):
        span = slice(half * K, (half + 1) * K)
        parts = [part[:, span] for part in found]
        joined = jnp.concatenate(parts, axis=1) if len(parts) > 1 else parts[0]
        rows = joined[:K]
        none = jnp.zeros_like(rows)
        split = jnp.concatenate([jnp.where(even, rows, none), jnp.where(even, none, rows)], axis=0)
        totals.append(lax.dot_general(joined, split, dims(1, 1), preferred_element_type=F32))
    return totals


def partial_kernel(sources, chained, *refs):
    out = refs[-1]
    picks = [
        read_picks(refs[which][at : at + 16, :], core) for _, (which, at, core) in sources
    ]
    for step in range(2 * Y):
        y, span = step // 2, slice(step % 2 * 256, step % 2 * 256 + 256)
        tables = [[refs[which][at:end, :] for which, at, end in parts] for parts, _ in sources]
        totals = grams(tables, [values[y : y + 1, span] for values in picks])
        for half in range(2):
            out[step, half] = totals[half] + refs[-2][step, half] if chained else totals[half]


def partial_grams(sources, messages, before=None):
    args = tuple(messages) + (() if before is None else (before,))
    return pl.pallas_call(
        functools.partial(partial_kernel, sources, before is not None),
        out_shape=jax.ShapeDtypeStruct((2 * Y, 2, 144, 256), F32),
        in_specs=in_vmem(len(args)),
        out_specs=in_vmem(1)[0],
        compiler_params=params(),
        cost_estimate=cost(2e9 * len(sources)),
    )(*args)


def pack(total, side):
    gram = total[0:K, side * K : (side + 1) * K]
    lane = lax.broadcasted_iota(jnp.int32, (32, K), 1)
    fold = jnp.where(lane < 64, pltpu.roll(gram[64:96], 64, 1), gram[96:128])
    return jnp.concatenate([gram[0:64], fold, total[K : K + 16, side * K : (side + 1) * K]], axis=0)


def unpack(packed):
    lane = lax.broadcasted_iota(jnp.int32, (64, K), 1)
    fold = packed[64:96]
    lower = jnp.where(lane >= 64, jnp.concatenate([pltpu.roll(fold, 64, 1), fold], axis=0), 0.0)
    corner = jnp.concatenate([jnp.where(lane >= 64, packed[0:64], 0.0), jnp.zeros_like(lower)], axis=0)
    return jnp.concatenate([packed[0:64], lower], axis=0) + corner.T, packed[96:97]


def last_kernel(shifts, lowest, low, high, before, *rest):
    outs, picks = rest[:-1], rest[-1]
    place = lax.div(lax.axis_index("grid"), X * CORES)
    picks[...] = read_picks(low[0:16, :], 1)
    table = [low[16:, :], high[...]]
    for shift in sorted(set(shifts)):
        y = lax.rem(place + shift, Y)
        for i in range(2):
            span = slice(i * 256, i * 256 + 256)
            totals = grams([table], [picks[pl.ds(y, 1), :][:, span]])
            for half in range(2):
                total = totals[half] + before[2 * y + i, half]
                for side in range(2):
                    patch = i + 2 * half + 4 * side
                    for out, its_shift, first in zip(outs, shifts, lowest):
                        if its_shift == shift and first <= patch < first + out.shape[0]:
                            out[patch - first] = pack(total, side).astype(out.dtype)


def last_grams(shifts, lowest, counts, dtype, low, high, before):
    return pl.pallas_call(
        functools.partial(last_kernel, shifts, lowest),
        out_shape=[jax.ShapeDtypeStruct((count, PACK, K), dtype) for count in counts],
        in_specs=in_vmem(3),
        out_specs=in_vmem(len(counts)),
        scratch_shapes=[pltpu.VMEM((Y, LOW), jnp.int32)],
        compiler_params=params(),
        cost_estimate=cost(5e8 * len(set(shifts))),
    )(low, high, before)


def relay_kernel(up, down, from_up, from_down, out_up, out_down):
    half = from_up.shape[0]
    out_up[:half] = (up[:half] + from_up[...].astype(F32)).astype(BF16)
    out_up[half:] = up[half:].astype(BF16)
    out_down[:half] = down[:half].astype(BF16)
    out_down[half:] = (down[half:] + from_down[...].astype(F32)).astype(BF16)


def relay(*args):
    return pl.pallas_call(
        relay_kernel,
        out_shape=[jax.ShapeDtypeStruct(args[0].shape, BF16)] * 2,
        in_specs=in_vmem(4),
        out_specs=in_vmem(2),
        compiler_params=params(),
        cost_estimate=cost(5e8),
    )(*args)


def sum_kernel(own, a, b, out):
    out[...] = (own[...] + a[...].astype(F32) + b[...].astype(F32)).astype(BF16)


def sum_parts(*args):
    return pl.pallas_call(
        sum_kernel,
        out_shape=jax.ShapeDtypeStruct(args[0].shape, BF16),
        in_specs=in_vmem(3),
        out_specs=in_vmem(1)[0],
        compiler_params=params(),
        cost_estimate=cost(5e8),
    )(*args)


def split(value):
    high = value.astype(BF16)
    return high, (value - high.astype(F32)).astype(BF16)


def product(left, right):
    lh, ll = split(left)
    rh, rl = split(right)
    return jnp.dot(
        jnp.concatenate([lh, lh, ll], axis=1),
        jnp.concatenate([rh, rl, rh], axis=0),
        preferred_element_type=F32,
    )


def weights_kernel(parts, out):
    gram, pull = unpack(jnp.sum(parts[...].astype(F32), axis=0))
    row = lax.broadcasted_iota(jnp.int32, (K, K), 0)
    col = lax.broadcasted_iota(jnp.int32, (K, K), 1)
    identity = (row == col).astype(F32)
    system = gram + (K - 1.0) * identity
    squares = jnp.sum(jnp.sum(system * system, axis=0, keepdims=True), axis=1, keepdims=True)
    frob = jnp.sqrt(squares)
    iterate = system / frob
    inverse = 1.5 * identity - 0.5 * iterate
    iterate = product(inverse, iterate)
    for sweep in range(1, ITERS):
        newton = 1.5 * identity - 0.5 * product(inverse, iterate)
        if sweep < ITERS - 1:
            both = product(newton, jnp.concatenate([iterate, inverse], axis=1))
            iterate, inverse = both[:, :K], both[:, K:]
        else:
            inverse = product(newton, inverse)
    shift = product(product(jnp.broadcast_to(pull, (16, K)), inverse), inverse)[0:1] / frob
    out[...] = (jnp.sqrt((K - 1.0) / frob) * inverse.T + shift).astype(BF16)


def transposed_weights(parts):
    return pl.pallas_call(
        weights_kernel,
        out_shape=jax.ShapeDtypeStruct((K, K), BF16),
        in_specs=in_vmem(1),
        out_specs=in_vmem(1)[0],
        compiler_params=params(),
        cost_estimate=cost(4e9),
    )(parts)


def perturb_kernel(state, mean, perturb):
    for pair in range(mean.shape[0]):
        for i in range(2):
            span = slice(i * K, (i + 1) * K)
            values = state[2 * pair + i].astype(F32)
            average = jnp.mean(values, axis=0, keepdims=True)
            mean[pair : pair + 1, span] = average
            perturb[pair, :, span] = (values - average).astype(BF16)


def perturbations(state):
    pairs = state.shape[0] // 2
    return pl.pallas_call(
        perturb_kernel,
        out_shape=[
            jax.ShapeDtypeStruct((pairs, 2 * K), F32),
            jax.ShapeDtypeStruct((pairs, K, 2 * K), BF16),
        ],
        in_specs=in_vmem(1),
        out_specs=in_vmem(2),
        compiler_params=params(),
        cost_estimate=cost(2e9),
    )(state)


def column_coefs():
    lane = lax.broadcasted_iota(jnp.int32, (1, 2 * K), 1) % K
    position = (lane.astype(F32) + 0.5) / K
    return lane, jnp.maximum(0.5 - position, 0.0), jnp.maximum(position - 0.5, 0.0)


def own_kernel(own, mean, perturb, out):
    _, left_coef, right_coef = column_coefs()
    own_coef = 1.0 - left_coef - right_coef
    for pair in range(mean.shape[0]):
        sums = jnp.dot(own[...], perturb[pair], preferred_element_type=F32)
        out[pair] = mean[pair : pair + 1] + own_coef * sums


def own_part(own, mean, perturb):
    return pl.pallas_call(
        own_kernel,
        out_shape=jax.ShapeDtypeStruct(perturb.shape, F32),
        in_specs=in_vmem(3),
        out_specs=in_vmem(1)[0],
        compiler_params=params(),
        cost_estimate=cost(2e9),
    )(own, mean, perturb)


def side_kernel(left, right, part, perturb, out, held, sems):
    lane, left_coef, right_coef = column_coefs()
    coef = left_coef + right_coef
    weights = jnp.concatenate([left[...], right[...]], axis=0)
    chunks = sems.shape[0]
    pairs = perturb.shape[0] // chunks
    copies = []
    for chunk in range(chunks):
        for pair in range(chunk * pairs, (chunk + 1) * pairs):
            sums = jnp.dot(weights, perturb[pair], preferred_element_type=F32)
            side = jnp.where(lane < K // 2, sums[:K], sums[K:])
            total = (part[pair] + coef * side).astype(BF16)
            for i in range(2):
                held[2 * pair + i] = total[:, i * K : (i + 1) * K]
        rows = pl.ds(2 * chunk * pairs, 2 * pairs)
        copies.append(pltpu.make_async_copy(held.at[rows], out.at[rows], sems.at[chunk]))
        copies[-1].start()
    for copy in copies:
        copy.wait()


def add_sides(left, right, part, perturb):
    shape = (2 * perturb.shape[0], K, K)
    return pl.pallas_call(
        side_kernel,
        out_shape=jax.ShapeDtypeStruct(shape, BF16),
        in_specs=in_vmem(4),
        out_specs=pl.BlockSpec(memory_space=pltpu.HBM),
        scratch_shapes=[pltpu.VMEM(shape, BF16), pltpu.SemaphoreType.DMA((6,))],
        compiler_params=params(),
        cost_estimate=cost(2e9),
    )(left, right, part, perturb)


def on_device(departures, innovation, obs_weight, send_rows, send_counts, state):
    n_grid = lax.axis_size("grid")
    near, to_right, to_left = make_messages(departures, innovation, obs_weight, send_rows[0].T)
    other = hop(near, 0, 0, 1)
    left = hop(to_right, 0, 1, 0)
    right = hop(to_left, 0, -1, 0)

    def at_end(which, core):
        return (((which, 0, TABLE),), (which, TABLE, core))

    def at_middle(which, core):
        return (((which, 16, 16 + TABLE),), (which, 16 + TABLE, core))

    totals = partial_grams((at_end(0, 0), at_end(1, 1)), (near, other))
    mean, perturb = perturbations(state)
    left, right, totals, mean, perturb = lax.optimization_barrier(
        (left, right, totals, mean, perturb)
    )
    far_low, far_high = left[:272], right[256:TABLE]
    far_low, far_high, left, right = lax.optimization_barrier((far_low, far_high, left, right))

    far_low = hop(far_low, 0, 1, 0)
    far_high = hop(far_high, 0, -1, 0)
    left_other = hop(left, 0, 0, 1)
    right_other = hop(right, 0, 0, 1)
    totals = partial_grams((at_middle(0, 0), at_end(1, 0)), (left, right), totals)
    totals = partial_grams((at_middle(0, 1), at_end(1, 1)), (left_other, right_other), totals)
    far_low, far_high, totals = lax.optimization_barrier((far_low, far_high, totals))
    far_low_other = hop(far_low, 0, 0, 1)
    far_high_other = hop(far_high, 0, 0, 1)
    source = (((0, 16, 272), (1, 0, 272)), (0, 0, 0))
    totals = partial_grams((source,), (far_low, far_high), totals)
    last = (far_low_other, far_high_other, totals)

    up, down = last_grams((2, 2), (0, 4), (4, 4), BF16, *last)
    from_up, from_down = hop(up, 1, 0, 0), hop(down, -1, 0, 0)
    up, down = last_grams((1, 3), (0, 0), (8, 8), F32, *last)
    up, down = relay(up, down, from_up, from_down)
    from_up, from_down = hop(up, 1, 0, 0), hop(down, -1, 0, 0)
    own = last_grams((0,), (0,), (8,), F32, *last)[0]
    parts = sum_parts(own, from_up, from_down)
    parts = lax.all_to_all(parts, "obs", 0, 0, tiled=True)

    own = transposed_weights(parts)
    low = lax.ppermute(own, "grid", [(j, (j + 1) % n_grid) for j in range(n_grid)])
    high = lax.ppermute(own, "grid", [(j, (j - 1) % n_grid) for j in range(n_grid)])
    part = own_part(own, mean, perturb)
    return add_sides(low, high, part, perturb)


def solution(mesh):
    in_specs = (
        P(("obs", "grid"), None),
        P(("obs", "grid")),
        P(("obs", "grid")),
        P(("obs", "grid"), None, None),
        P(("obs", "grid"), None),
        P("obs", None, "grid"),
    )
    out_specs = P("obs", None, "grid")
    return jax.shard_map(
        on_device, mesh=mesh, in_specs=in_specs, out_specs=out_specs, check_vma=False
    )
```

```python
import functools

import jax
import jax.numpy as jnp
from jax import lax
from jax.experimental import pallas as pl
from jax.experimental.pallas import tpu as pltpu
from jax.sharding import PartitionSpec as P

ITERS = 6
Y, X, CORES = 4, 4, 2
F32, BF16 = jnp.float32, jnp.bfloat16
K = 128
LOW = 512
BLOCKS = 4
HALF = 2 * K + 16
PACK = 112
VMEM = 20 * 1024 * 1024


def params():
    return pltpu.CompilerParams(vmem_limit_bytes=VMEM)


LONG, MID, SHORT = 6e10, 6e10, 1e6


def cost(flops):
    return pl.CostEstimate(flops=int(flops), bytes_accessed=100_000, transcendentals=0)


def in_vmem(count):
    return [pl.BlockSpec(memory_space=pltpu.VMEM)] * count


def hop(value, dy, dx, dc):
    pairs = []
    for place in range(Y * X * CORES):
        y, x, c = place // (X * CORES), place // CORES % X, place % CORES
        pairs.append((place, ((y + dy) % Y * X + (x + dx) % X) * CORES + (c ^ dc)))
    return lax.ppermute(value, "grid", pairs)


def dims(m, n):
    return (((m,), (n,)), ((), ()))


def message_kernel(*refs):
    sources, (near, right_first, right_second, left_first, left_second) = refs[:4], refs[4:9]
    held, (turned, sems) = refs[9:13], refs[13:]
    copies = [
        pltpu.make_async_copy(source, place, sems.at[i])
        for i, (source, place) in enumerate(zip(sources, held))
    ]
    for copy in copies[::-1]:
        copy.start()
    departures, innovation, obs_weight, send_rows = held
    copies[3].wait()
    grid = lax.axis_index("grid")
    x, c = lax.rem(lax.div(grid, CORES), X), lax.rem(grid, CORES)
    turned[...] = send_rows[...].T
    groups = []
    for dx in range(X):
        halves = []
        for dc in range(CORES):
            cx = lax.rem(x + dx, X) * CORES + lax.rem(c + dc, CORES)
            lines = []
            for y in range(Y):
                rows = turned[pl.ds(y * X * CORES + cx, 8, stride=Y * X * CORES), :]
                pair = [rows[0:4], rows[4:8]]
                pairs = jnp.concatenate(pair[::-1] if dc else pair, axis=1)
                fours = jnp.concatenate([pairs[0:2], pairs[2:4]], axis=1)
                lines.append(jnp.concatenate([fours[0:1], fours[1:2]], axis=1))
            picks = jnp.concatenate(lines, axis=0)
            halves.append(lax.shift_right_arithmetic(picks, 8))
            halves.append(jnp.bitwise_and(picks, 255))
        groups.append(jnp.concatenate(halves, axis=0).astype(F32).astype(BF16))
    near[2 * HALF :, :] = groups[0]
    right_first[:16, :] = groups[1]
    right_first[16:32, :] = groups[2]
    left_first[:16, :] = groups[3]
    for copy in copies[:3]:
        copy.wait()
    root = jnp.sqrt(obs_weight[...].reshape(1, BLOCKS * LOW))
    innov = innovation[...].reshape(1, BLOCKS * LOW) * root
    row = lax.broadcasted_iota(jnp.int32, (16, LOW), 0)
    places = (
        ((near, 0), (right_first, 32), (left_second, 0)),
        ((near, HALF), (left_first, 16), (right_second, 0)),
    )
    for half in range(2):
        tail = jnp.zeros((16, LOW), F32)
        for block in range(2):
            start = (2 * half + block) * LOW
            span = slice(start, start + LOW)
            rows = (departures[span, :].astype(F32).T * root[:, span]).astype(BF16)
            for ref, at in places[half]:
                ref[at + block * K : at + (block + 1) * K, :] = rows
            tail = jnp.where(row == block, innov[:, span], tail)
        for ref, at in places[half]:
            ref[at + 2 * K : at + HALF, :] = tail.astype(BF16)


def make_messages(*args):
    rows = (2 * HALF + 16, HALF + 32, HALF, HALF + 16, HALF)
    return pl.pallas_call(
        message_kernel,
        out_shape=[jax.ShapeDtypeStruct((count, LOW), BF16) for count in rows],
        in_specs=[pl.BlockSpec(memory_space=pltpu.HBM)] * 4,
        out_specs=in_vmem(len(rows)),
        scratch_shapes=[pltpu.VMEM(arg.shape, arg.dtype) for arg in args]
        + [pltpu.VMEM(args[3].shape[::-1], jnp.int32), pltpu.SemaphoreType.DMA((4,))],
        compiler_params=pltpu.CompilerParams(vmem_limit_bytes=60 * 1024 * 1024),
        cost_estimate=cost(2e9),
    )(*args)


def read_picks(group, core):
    values = group[8 * core : 8 * core + 8].astype(F32)
    return (values[0:4] * 256.0 + values[4:8]).astype(jnp.int32)


def pick(parts, picks):
    high = lax.shift_right_arithmetic(picks, 9)
    first = parts[0][0]
    live = picks >= 0 if len(parts) == 2 else lax.shift_right_arithmetic(high, 1) == first
    low = jnp.where(live, jnp.bitwise_and(picks, LOW - 1), -1)
    one_hot = (lax.broadcasted_iota(jnp.int32, (LOW, 256), 0) == low).astype(BF16)
    blocks, innovs = [], []
    for _, rows in parts:
        found = jnp.dot(rows, one_hot, preferred_element_type=F32)
        blocks += [found[:K], found[K : 2 * K]]
        innovs += [found[2 * K : 2 * K + 1], found[2 * K + 1 : 2 * K + 2]]
    members, innov = blocks[0], innovs[0]
    for block in range(1, len(blocks)):
        here = high == 2 * first + block
        members = jnp.where(here, blocks[block], members)
        innov = jnp.where(here, innovs[block], innov)
    return jnp.concatenate([members, jnp.broadcast_to(innov, (16, 256))], axis=0).astype(BF16)


def pick_kernel(sources, count, *refs):
    outs = refs[count:]
    picks = [read_picks(refs[which][at : at + 16, :], core) for _, (which, at, core), _ in sources]
    for step in range(2 * Y):
        y, span = step // 2, slice(step % 2 * 256, step % 2 * 256 + 256)
        for out, (parts, _, before), values in zip(outs, sources, picks):
            tables = [(half, refs[which][at : at + HALF, :]) for half, which, at in parts]
            found = pick(tables, values[y : y + 1, span])
            out[step] = found if before is None else found + refs[before][step]


def pick_rows(sources, flops, *args):
    return pl.pallas_call(
        functools.partial(pick_kernel, sources, len(args)),
        out_shape=[jax.ShapeDtypeStruct((2 * Y, 144, 256), BF16)] * len(sources),
        in_specs=in_vmem(len(args)),
        out_specs=in_vmem(len(sources)),
        compiler_params=params(),
        cost_estimate=cost(flops),
    )(*args)


def join(first, second):
    low = lax.broadcasted_iota(jnp.int32, first.shape, 1) < K // 2
    return jnp.where(low, first, second), jnp.where(low, second, first)


def pack(total):
    gram = total[0:K]
    lane = lax.broadcasted_iota(jnp.int32, (32, K), 1)
    fold = jnp.where(lane < 64, pltpu.roll(gram[64:96], 64, 1), gram[96:128])
    return jnp.concatenate([gram[0:64], fold, total[K : K + 16]], axis=0)


def unpack(packed):
    lane = lax.broadcasted_iota(jnp.int32, (64, K), 1)
    fold = packed[64:96]
    lower = jnp.where(lane >= 64, jnp.concatenate([pltpu.roll(fold, 64, 1), fold], axis=0), 0.0)
    corner = jnp.concatenate([jnp.where(lane >= 64, packed[0:64], 0.0), jnp.zeros_like(lower)], axis=0)
    return jnp.concatenate([packed[0:64], lower], axis=0) + corner.T, packed[96:97]


def last_kernel(shifts, lowest, low, high, same, *rest):
    found, outs, picks = rest[:6], rest[6:-1], rest[-1]
    place = lax.div(lax.axis_index("grid"), X * CORES)
    picks[...] = read_picks(low[16:32, :], 1)
    table = ((0, low[32:, :]), (1, high[16:, :]))
    for shift in sorted(set(shifts)):
        y = lax.rem(place + shift, Y)
        for i in range(2):
            span = slice(i * 256, i * 256 + 256)
            last = pick(table, picks[pl.ds(y, 1), :][:, span])
            shards = [ref[2 * y + i] for ref in (*found, same)] + [last]
            for half in range(2):
                span = slice(half * K, half * K + K)
                pairs = [
                    join(shards[n][:, span], shards[n + 1][:, span])
                    for n in range(0, len(shards), 2)
                ]
                for side in range(2):
                    rows = jnp.concatenate([pair[side] for pair in pairs], axis=1)
                    total = lax.dot_general(rows, rows[:K], dims(1, 1), preferred_element_type=F32)
                    patch = i + 2 * half + 4 * side
                    for out, its_shift, first in zip(outs, shifts, lowest):
                        if its_shift == shift and first <= patch < first + out.shape[0]:
                            out[patch - first] = pack(total).astype(out.dtype)


def last_grams(shifts, lowest, counts, dtype, *args):
    return pl.pallas_call(
        functools.partial(last_kernel, shifts, lowest),
        out_shape=[jax.ShapeDtypeStruct((count, PACK, K), dtype) for count in counts],
        in_specs=in_vmem(len(args)),
        out_specs=in_vmem(len(counts)),
        scratch_shapes=[pltpu.VMEM((Y, LOW), jnp.int32)],
        compiler_params=params(),
        cost_estimate=cost(1e9 * len(set(shifts))),
    )(*args)


def relay_kernel(up, down, from_up, from_down, out_up, out_down):
    half = from_up.shape[0]
    out_up[:half] = (up[:half] + from_up[...].astype(F32)).astype(BF16)
    out_up[half:] = up[half:].astype(BF16)
    out_down[:half] = down[:half].astype(BF16)
    out_down[half:] = (down[half:] + from_down[...].astype(F32)).astype(BF16)


def relay(*args):
    return pl.pallas_call(
        relay_kernel,
        out_shape=[jax.ShapeDtypeStruct(args[0].shape, BF16)] * 2,
        in_specs=in_vmem(4),
        out_specs=in_vmem(2),
        compiler_params=params(),
        cost_estimate=cost(5e8),
    )(*args)


def sum_kernel(own, a, b, out):
    out[...] = (own[...] + a[...].astype(F32) + b[...].astype(F32)).astype(BF16)


def sum_parts(*args):
    return pl.pallas_call(
        sum_kernel,
        out_shape=jax.ShapeDtypeStruct(args[0].shape, BF16),
        in_specs=in_vmem(3),
        out_specs=in_vmem(1)[0],
        compiler_params=params(),
        cost_estimate=cost(5e8),
    )(*args)


def split(value):
    high = value.astype(BF16)
    return high, (value - high.astype(F32)).astype(BF16)


def product(left, right):
    lh, ll = split(left)
    rh, rl = split(right)
    return jnp.dot(
        jnp.concatenate([lh, lh, ll], axis=1),
        jnp.concatenate([rh, rl, rh], axis=0),
        preferred_element_type=F32,
    )


def weights_kernel(parts, out):
    gram, pull = unpack(jnp.sum(parts[...].astype(F32), axis=0))
    row = lax.broadcasted_iota(jnp.int32, (K, K), 0)
    col = lax.broadcasted_iota(jnp.int32, (K, K), 1)
    identity = (row == col).astype(F32)
    system = gram + (K - 1.0) * identity
    squares = jnp.sum(jnp.sum(system * system, axis=0, keepdims=True), axis=1, keepdims=True)
    frob = jnp.sqrt(squares)
    iterate = system / frob
    inverse = 1.5 * identity - 0.5 * iterate
    iterate = product(inverse, iterate)
    for sweep in range(1, ITERS):
        newton = 1.5 * identity - 0.5 * product(inverse, iterate)
        if sweep < ITERS - 1:
            both = product(newton, jnp.concatenate([iterate, inverse], axis=1))
            iterate, inverse = both[:, :K], both[:, K:]
        else:
            inverse = product(newton, inverse)
    shift = product(product(jnp.broadcast_to(pull, (16, K)), inverse), inverse)[0:1] / frob
    out[...] = (jnp.sqrt((K - 1.0) / frob) * inverse.T + shift).astype(BF16)


def transposed_weights(parts):
    return pl.pallas_call(
        weights_kernel,
        out_shape=jax.ShapeDtypeStruct((K, K), BF16),
        in_specs=in_vmem(1),
        out_specs=in_vmem(1)[0],
        compiler_params=params(),
        cost_estimate=cost(4e9),
    )(parts)


def perturb_kernel(state, mean, perturb):
    for pair in range(mean.shape[0]):
        for i in range(2):
            span = slice(i * K, (i + 1) * K)
            values = state[2 * pair + i].astype(F32)
            average = jnp.mean(values, axis=0, keepdims=True)
            mean[pair : pair + 1, span] = average
            perturb[pair, :, span] = (values - average).astype(BF16)


def perturbations(state):
    pairs = state.shape[0] // 2
    return pl.pallas_call(
        perturb_kernel,
        out_shape=[
            jax.ShapeDtypeStruct((pairs, 2 * K), F32),
            jax.ShapeDtypeStruct((pairs, K, 2 * K), BF16),
        ],
        in_specs=in_vmem(1),
        out_specs=in_vmem(2),
        compiler_params=params(),
        cost_estimate=cost(2e9),
    )(state)


def column_coefs():
    lane = lax.broadcasted_iota(jnp.int32, (1, 2 * K), 1) % K
    position = (lane.astype(F32) + 0.5) / K
    return lane, jnp.maximum(0.5 - position, 0.0), jnp.maximum(position - 0.5, 0.0)


def own_kernel(own, mean, perturb, out):
    _, left_coef, right_coef = column_coefs()
    own_coef = 1.0 - left_coef - right_coef
    for pair in range(mean.shape[0]):
        sums = jnp.dot(own[...], perturb[pair], preferred_element_type=F32)
        out[pair] = mean[pair : pair + 1] + own_coef * sums


def own_part(own, mean, perturb):
    return pl.pallas_call(
        own_kernel,
        out_shape=jax.ShapeDtypeStruct(perturb.shape, F32),
        in_specs=in_vmem(3),
        out_specs=in_vmem(1)[0],
        compiler_params=params(),
        cost_estimate=cost(2e9),
    )(own, mean, perturb)


def side_kernel(left, right, part, perturb, out, held, sems):
    lane, left_coef, right_coef = column_coefs()
    coef = left_coef + right_coef
    weights = jnp.concatenate([left[...], right[...]], axis=0)
    chunks = sems.shape[0]
    pairs = perturb.shape[0] // chunks
    copies = []
    for chunk in range(chunks):
        for pair in range(chunk * pairs, (chunk + 1) * pairs):
            sums = jnp.dot(weights, perturb[pair], preferred_element_type=F32)
            side = jnp.where(lane < K // 2, sums[:K], sums[K:])
            total = (part[pair] + coef * side).astype(BF16)
            for i in range(2):
                held[2 * pair + i] = total[:, i * K : (i + 1) * K]
        rows = pl.ds(2 * chunk * pairs, 2 * pairs)
        copies.append(pltpu.make_async_copy(held.at[rows], out.at[rows], sems.at[chunk]))
        copies[-1].start()
    for copy in copies:
        copy.wait()


def add_sides(left, right, part, perturb):
    shape = (2 * perturb.shape[0], K, K)
    return pl.pallas_call(
        side_kernel,
        out_shape=jax.ShapeDtypeStruct(shape, BF16),
        in_specs=in_vmem(4),
        out_specs=pl.BlockSpec(memory_space=pltpu.HBM),
        scratch_shapes=[pltpu.VMEM(shape, BF16), pltpu.SemaphoreType.DMA((6,))],
        compiler_params=params(),
        cost_estimate=cost(2e9),
    )(left, right, part, perturb)


def on_device(departures, innovation, obs_weight, send_rows, send_counts, state):
    n_grid = lax.axis_size("grid")
    near, right_first, right_second, left_first, left_second = make_messages(
        departures, innovation, obs_weight, send_rows[0].T
    )
    left = hop(right_first, 0, 1, 0)
    right = hop(left_first, 0, -1, 0)
    other = hop(near, 0, 0, 1)
    left_more = hop(right_second, 0, 1, 0)
    right_more = hop(left_second, 0, -1, 0)

    whole = lambda which: ((0, which, 0), (1, which, HALF))
    at_end = 2 * HALF
    found = pick_rows(
        ((whole(0), (0, at_end, 0), None), (whole(1), (1, at_end, 1), None)), SHORT, near, other
    )
    mean, perturb = perturbations(state)
    left, right, found, mean, perturb = lax.optimization_barrier(
        (left, right, found, mean, perturb)
    )
    far_low, far_high = hop(left, 0, 1, 0), hop(right, 0, -1, 0)

    def firsts(core):
        return (((0, 0, 32),), (0, 0, core), None), (((1, 1, 16),), (1, 0, core), None)

    def seconds(core):
        return (((1, 2, 0),), (0, 0, core), 4), (((0, 3, 0),), (1, 0, core), 5)

    same = pick_rows(firsts(0), LONG, left, right)
    left, right, same = lax.optimization_barrier((left, right, same))
    left_other, right_other = hop(left, 0, 0, 1), hop(right, 0, 0, 1)
    same = pick_rows(seconds(0), MID, left, right, left_more, right_more, *same)
    left_more, right_more, same = lax.optimization_barrier((left_more, right_more, same))
    left_more_other, right_more_other = hop(left_more, 0, 0, 1), hop(right_more, 0, 0, 1)
    cross = pick_rows(firsts(1), SHORT, left_other, right_other)
    far_low, far_high, cross, left_more_other, right_more_other = lax.optimization_barrier(
        (far_low, far_high, cross, left_more_other, right_more_other)
    )
    far_low_other, far_high_other = hop(far_low, 0, 0, 1), hop(far_high, 0, 0, 1)
    cross = pick_rows(
        seconds(1), SHORT, left_other, right_other, left_more_other, right_more_other, *cross
    )
    far = pick_rows(((((0, 0, 32), (1, 1, 16)), (0, 16, 0), None),), SHORT, far_low, far_high)[0]
    last = (far_low_other, far_high_other, far, *found, same[0], cross[0], same[1], cross[1])

    up, down = last_grams((2, 2), (0, 4), (4, 4), BF16, *last)
    from_up, from_down = hop(up, 1, 0, 0), hop(down, -1, 0, 0)
    up, down = last_grams((1, 3), (0, 0), (8, 8), F32, *last)
    up, down = relay(up, down, from_up, from_down)
    from_up, from_down = hop(up, 1, 0, 0), hop(down, -1, 0, 0)
    own = last_grams((0,), (0,), (8,), F32, *last)[0]
    parts = sum_parts(own, from_up, from_down)
    parts = lax.all_to_all(parts, "obs", 0, 0, tiled=True)

    own = transposed_weights(parts)
    low = lax.ppermute(own, "grid", [(j, (j + 1) % n_grid) for j in range(n_grid)])
    high = lax.ppermute(own, "grid", [(j, (j - 1) % n_grid) for j in range(n_grid)])
    part = own_part(own, mean, perturb)
    return add_sides(low, high, part, perturb)


def solution(mesh):
    in_specs = (
        P(("obs", "grid"), None),
        P(("obs", "grid")),
        P(("obs", "grid")),
        P(("obs", "grid"), None, None),
        P(("obs", "grid"), None),
        P("obs", None, "grid"),
    )
    out_specs = P("obs", None, "grid")
    return jax.shard_map(
        on_device, mesh=mesh, in_specs=in_specs, out_specs=out_specs, check_vma=False
    )
```

```python
import functools

import jax
import jax.numpy as jnp
from jax import lax
from jax.experimental import pallas as pl
from jax.experimental.pallas import tpu as pltpu
from jax.sharding import PartitionSpec as P

ITERS = 6
Y, X, CORES = 4, 4, 2
F32, BF16 = jnp.float32, jnp.bfloat16
K = 128
LOW = 512
BLOCKS = 4
HALF = 2 * K + 16
PACK = 80
VMEM = 20 * 1024 * 1024


def params():
    return pltpu.CompilerParams(vmem_limit_bytes=VMEM)


LONG, MID, SHORT = 6e10, 6e10, 1e6


def cost(flops):
    return pl.CostEstimate(flops=int(flops), bytes_accessed=100_000, transcendentals=0)


def in_vmem(count):
    return [pl.BlockSpec(memory_space=pltpu.VMEM)] * count


def hop(value, dy, dx, dc):
    pairs = []
    for place in range(Y * X * CORES):
        y, x, c = place // (X * CORES), place // CORES % X, place % CORES
        pairs.append((place, ((y + dy) % Y * X + (x + dx) % X) * CORES + (c ^ dc)))
    return lax.ppermute(value, "grid", pairs)


def dims(m, n):
    return (((m,), (n,)), ((), ()))


def message_kernel(*refs):
    sources, (near, right_first, right_second, left_first, left_second) = refs[:4], refs[4:9]
    held, (turned, sems) = refs[9:13], refs[13:]
    copies = [
        pltpu.make_async_copy(source, place, sems.at[i])
        for i, (source, place) in enumerate(zip(sources, held))
    ]
    for copy in copies[::-1]:
        copy.start()
    departures, innovation, obs_weight, send_rows = held
    copies[3].wait()
    grid = lax.axis_index("grid")
    x, c = lax.rem(lax.div(grid, CORES), X), lax.rem(grid, CORES)
    turned[...] = send_rows[...].T
    groups = []
    for dx in range(X):
        halves = []
        for dc in range(CORES):
            cx = lax.rem(x + dx, X) * CORES + lax.rem(c + dc, CORES)
            lines = []
            for y in range(Y):
                rows = turned[pl.ds(y * X * CORES + cx, 8, stride=Y * X * CORES), :]
                pair = [rows[0:4], rows[4:8]]
                pairs = jnp.concatenate(pair[::-1] if dc else pair, axis=1)
                fours = jnp.concatenate([pairs[0:2], pairs[2:4]], axis=1)
                lines.append(jnp.concatenate([fours[0:1], fours[1:2]], axis=1))
            picks = jnp.concatenate(lines, axis=0)
            halves.append(lax.shift_right_arithmetic(picks, 8))
            halves.append(jnp.bitwise_and(picks, 255))
        groups.append(jnp.concatenate(halves, axis=0).astype(F32).astype(BF16))
    near[2 * HALF :, :] = groups[0]
    right_first[:16, :] = groups[1]
    right_first[16:32, :] = groups[2]
    left_first[:16, :] = groups[3]
    for copy in copies[:3]:
        copy.wait()
    root = jnp.sqrt(obs_weight[...].reshape(1, BLOCKS * LOW))
    innov = innovation[...].reshape(1, BLOCKS * LOW) * root
    row = lax.broadcasted_iota(jnp.int32, (16, LOW), 0)
    places = (
        ((near, 0), (right_first, 32), (left_second, 0)),
        ((near, HALF), (left_first, 16), (right_second, 0)),
    )
    for half in range(2):
        tail = jnp.zeros((16, LOW), F32)
        for block in range(2):
            start = (2 * half + block) * LOW
            span = slice(start, start + LOW)
            rows = (departures[span, :].astype(F32).T * root[:, span]).astype(BF16)
            for ref, at in places[half]:
                ref[at + block * K : at + (block + 1) * K, :] = rows
            tail = jnp.where(row == block, innov[:, span], tail)
        for ref, at in places[half]:
            ref[at + 2 * K : at + HALF, :] = tail.astype(BF16)


def make_messages(*args):
    rows = (2 * HALF + 16, HALF + 32, HALF, HALF + 16, HALF)
    return pl.pallas_call(
        message_kernel,
        out_shape=[jax.ShapeDtypeStruct((count, LOW), BF16) for count in rows],
        in_specs=[pl.BlockSpec(memory_space=pltpu.HBM)] * 4,
        out_specs=in_vmem(len(rows)),
        scratch_shapes=[pltpu.VMEM(arg.shape, arg.dtype) for arg in args]
        + [pltpu.VMEM(args[3].shape[::-1], jnp.int32), pltpu.SemaphoreType.DMA((4,))],
        compiler_params=pltpu.CompilerParams(vmem_limit_bytes=60 * 1024 * 1024),
        cost_estimate=cost(2e9),
    )(*args)


def read_picks(group, core):
    values = group[8 * core : 8 * core + 8].astype(F32)
    return (values[0:4] * 256.0 + values[4:8]).astype(jnp.int32)


def pick(parts, picks):
    high = lax.shift_right_arithmetic(picks, 9)
    first = parts[0][0]
    live = picks >= 0 if len(parts) == 2 else lax.shift_right_arithmetic(high, 1) == first
    low = jnp.where(live, jnp.bitwise_and(picks, LOW - 1), -1)
    one_hot = (lax.broadcasted_iota(jnp.int32, (LOW, 256), 0) == low).astype(BF16)
    blocks, innovs = [], []
    for _, rows in parts:
        found = jnp.dot(rows, one_hot, preferred_element_type=F32)
        blocks += [found[:K], found[K : 2 * K]]
        innovs += [found[2 * K : 2 * K + 1], found[2 * K + 1 : 2 * K + 2]]
    members, innov = blocks[0], innovs[0]
    for block in range(1, len(blocks)):
        here = high == 2 * first + block
        members = jnp.where(here, blocks[block], members)
        innov = jnp.where(here, innovs[block], innov)
    return jnp.concatenate([members, jnp.broadcast_to(innov, (16, 256))], axis=0).astype(BF16)


def pick_kernel(sources, count, *refs):
    outs = refs[count:]
    picks = [read_picks(refs[which][at : at + 16, :], core) for _, (which, at, core), _ in sources]
    for step in range(2 * Y):
        y, span = step // 2, slice(step % 2 * 256, step % 2 * 256 + 256)
        for out, (parts, _, before), values in zip(outs, sources, picks):
            tables = [(half, refs[which][at : at + HALF, :]) for half, which, at in parts]
            found = pick(tables, values[y : y + 1, span])
            out[step] = found if before is None else found + refs[before][step]


def pick_rows(sources, flops, *args):
    return pl.pallas_call(
        functools.partial(pick_kernel, sources, len(args)),
        out_shape=[jax.ShapeDtypeStruct((2 * Y, 144, 256), BF16)] * len(sources),
        in_specs=in_vmem(len(args)),
        out_specs=in_vmem(len(sources)),
        compiler_params=params(),
        cost_estimate=cost(flops),
    )(*args)


def join(first, second):
    low = lax.broadcasted_iota(jnp.int32, first.shape, 1) < K // 2
    return jnp.where(low, first, second), jnp.where(low, second, first)


def pack(total):
    row = lax.broadcasted_iota(jnp.int32, (64, K), 0)
    lane = lax.broadcasted_iota(jnp.int32, (64, K), 1)
    lower = total[64:K]
    upper = jnp.where(lane < row, pltpu.roll(lower, 64, 1), total[0:64])
    diagonal = jnp.sum(jnp.where(lane == row + 64, lower, 0.0), axis=0, keepdims=True)
    tail = jnp.where(lax.broadcasted_iota(jnp.int32, (16, K), 0) == 0, diagonal, total[K:])
    return jnp.concatenate([upper, tail], axis=0)


def unpack(packed):
    row = lax.broadcasted_iota(jnp.int32, (64, K), 0)
    lane = lax.broadcasted_iota(jnp.int32, (64, K), 1)
    upper = packed[0:64]
    above = jnp.where(lane > row, upper, 0.0)
    below = pltpu.roll(jnp.where(lane < row, upper, 0.0), 64, 1)
    off = jnp.concatenate([above, below], axis=0)
    low = jnp.where(lane == row + 64, packed[64:65], 0.0)
    diagonal = jnp.concatenate([jnp.where(lane == row, upper, 0.0), low], axis=0)
    return off + off.T + diagonal, packed[65:66]


def last_kernel(shifts, lowest, low, high, same, *rest):
    found, outs, picks = rest[:6], rest[6:-1], rest[-1]
    place = lax.div(lax.axis_index("grid"), X * CORES)
    picks[...] = read_picks(low[16:32, :], 1)
    table = ((0, low[32:, :]), (1, high[16:, :]))
    for shift in sorted(set(shifts)):
        y = lax.rem(place + shift, Y)
        for i in range(2):
            span = slice(i * 256, i * 256 + 256)
            last = pick(table, picks[pl.ds(y, 1), :][:, span])
            shards = [ref[2 * y + i] for ref in (*found, same)] + [last]
            for half in range(2):
                span = slice(half * K, half * K + K)
                pairs = [
                    join(shards[n][:, span], shards[n + 1][:, span])
                    for n in range(0, len(shards), 2)
                ]
                for side in range(2):
                    rows = jnp.concatenate([pair[side] for pair in pairs], axis=1)
                    total = lax.dot_general(rows, rows[:K], dims(1, 1), preferred_element_type=F32)
                    patch = i + 2 * half + 4 * side
                    for out, its_shift, first in zip(outs, shifts, lowest):
                        if its_shift == shift and first <= patch < first + out.shape[0]:
                            out[patch - first] = pack(total).astype(out.dtype)


def last_grams(shifts, lowest, counts, dtype, *args):
    return pl.pallas_call(
        functools.partial(last_kernel, shifts, lowest),
        out_shape=[jax.ShapeDtypeStruct((count, PACK, K), dtype) for count in counts],
        in_specs=in_vmem(len(args)),
        out_specs=in_vmem(len(counts)),
        scratch_shapes=[pltpu.VMEM((Y, LOW), jnp.int32)],
        compiler_params=params(),
        cost_estimate=cost(1e9 * len(set(shifts))),
    )(*args)


def relay_kernel(up, down, from_up, from_down, out_up, out_down):
    half = from_up.shape[0]
    out_up[:half] = (up[:half] + from_up[...].astype(F32)).astype(BF16)
    out_up[half:] = up[half:].astype(BF16)
    out_down[:half] = down[:half].astype(BF16)
    out_down[half:] = (down[half:] + from_down[...].astype(F32)).astype(BF16)


def relay(*args):
    return pl.pallas_call(
        relay_kernel,
        out_shape=[jax.ShapeDtypeStruct(args[0].shape, BF16)] * 2,
        in_specs=in_vmem(4),
        out_specs=in_vmem(2),
        compiler_params=params(),
        cost_estimate=cost(5e8),
    )(*args)


def sum_kernel(own, a, b, out):
    out[...] = (own[...] + a[...].astype(F32) + b[...].astype(F32)).astype(BF16)


def sum_parts(*args):
    return pl.pallas_call(
        sum_kernel,
        out_shape=jax.ShapeDtypeStruct(args[0].shape, BF16),
        in_specs=in_vmem(3),
        out_specs=in_vmem(1)[0],
        compiler_params=params(),
        cost_estimate=cost(5e8),
    )(*args)


def split(value):
    high = value.astype(BF16)
    return high, (value - high.astype(F32)).astype(BF16)


def product(left, right):
    lh, ll = split(left)
    rh, rl = split(right)
    return jnp.dot(
        jnp.concatenate([lh, lh, ll], axis=1),
        jnp.concatenate([rh, rl, rh], axis=0),
        preferred_element_type=F32,
    )


def weights_kernel(parts, out):
    gram, pull = unpack(jnp.sum(parts[...].astype(F32), axis=0))
    row = lax.broadcasted_iota(jnp.int32, (K, K), 0)
    col = lax.broadcasted_iota(jnp.int32, (K, K), 1)
    identity = (row == col).astype(F32)
    system = gram + (K - 1.0) * identity
    squares = jnp.sum(jnp.sum(system * system, axis=0, keepdims=True), axis=1, keepdims=True)
    frob = jnp.sqrt(squares)
    iterate = system / frob
    inverse = 1.5 * identity - 0.5 * iterate
    iterate = product(inverse, iterate)
    for sweep in range(1, ITERS):
        newton = 1.5 * identity - 0.5 * product(inverse, iterate)
        if sweep < ITERS - 1:
            both = product(newton, jnp.concatenate([iterate, inverse], axis=1))
            iterate, inverse = both[:, :K], both[:, K:]
        else:
            inverse = product(newton, inverse)
    shift = product(product(jnp.broadcast_to(pull, (16, K)), inverse), inverse)[0:1] / frob
    out[...] = (jnp.sqrt((K - 1.0) / frob) * inverse.T + shift).astype(BF16)


def transposed_weights(parts):
    return pl.pallas_call(
        weights_kernel,
        out_shape=jax.ShapeDtypeStruct((K, K), BF16),
        in_specs=in_vmem(1),
        out_specs=in_vmem(1)[0],
        compiler_params=params(),
        cost_estimate=cost(4e9),
    )(parts)


def perturb_kernel(state, mean, perturb):
    for pair in range(mean.shape[0]):
        for i in range(2):
            span = slice(i * K, (i + 1) * K)
            values = state[2 * pair + i].astype(F32)
            average = jnp.mean(values, axis=0, keepdims=True)
            mean[pair : pair + 1, span] = average
            perturb[pair, :, span] = (values - average).astype(BF16)


def perturbations(state):
    pairs = state.shape[0] // 2
    return pl.pallas_call(
        perturb_kernel,
        out_shape=[
            jax.ShapeDtypeStruct((pairs, 2 * K), F32),
            jax.ShapeDtypeStruct((pairs, K, 2 * K), BF16),
        ],
        in_specs=in_vmem(1),
        out_specs=in_vmem(2),
        compiler_params=params(),
        cost_estimate=cost(2e9),
    )(state)


def column_coefs():
    lane = lax.broadcasted_iota(jnp.int32, (1, 2 * K), 1) % K
    position = (lane.astype(F32) + 0.5) / K
    return lane, jnp.maximum(0.5 - position, 0.0), jnp.maximum(position - 0.5, 0.0)


def own_kernel(own, mean, perturb, out):
    _, left_coef, right_coef = column_coefs()
    own_coef = 1.0 - left_coef - right_coef
    for pair in range(mean.shape[0]):
        sums = jnp.dot(own[...], perturb[pair], preferred_element_type=F32)
        out[pair] = mean[pair : pair + 1] + own_coef * sums


def own_part(own, mean, perturb):
    return pl.pallas_call(
        own_kernel,
        out_shape=jax.ShapeDtypeStruct(perturb.shape, F32),
        in_specs=in_vmem(3),
        out_specs=in_vmem(1)[0],
        compiler_params=params(),
        cost_estimate=cost(2e9),
    )(own, mean, perturb)


def side_kernel(left, right, part, perturb, out, held, sems):
    lane, left_coef, right_coef = column_coefs()
    coef = left_coef + right_coef
    weights = jnp.concatenate([left[...], right[...]], axis=0)
    chunks = sems.shape[0]
    pairs = perturb.shape[0] // chunks
    copies = []
    for chunk in range(chunks):
        for pair in range(chunk * pairs, (chunk + 1) * pairs):
            sums = jnp.dot(weights, perturb[pair], preferred_element_type=F32)
            side = jnp.where(lane < K // 2, sums[:K], sums[K:])
            total = (part[pair] + coef * side).astype(BF16)
            for i in range(2):
                held[2 * pair + i] = total[:, i * K : (i + 1) * K]
        rows = pl.ds(2 * chunk * pairs, 2 * pairs)
        copies.append(pltpu.make_async_copy(held.at[rows], out.at[rows], sems.at[chunk]))
        copies[-1].start()
    for copy in copies:
        copy.wait()


def add_sides(left, right, part, perturb):
    shape = (2 * perturb.shape[0], K, K)
    return pl.pallas_call(
        side_kernel,
        out_shape=jax.ShapeDtypeStruct(shape, BF16),
        in_specs=in_vmem(4),
        out_specs=pl.BlockSpec(memory_space=pltpu.HBM),
        scratch_shapes=[pltpu.VMEM(shape, BF16), pltpu.SemaphoreType.DMA((6,))],
        compiler_params=params(),
        cost_estimate=cost(2e9),
    )(left, right, part, perturb)


def on_device(departures, innovation, obs_weight, send_rows, send_counts, state):
    n_grid = lax.axis_size("grid")
    near, right_first, right_second, left_first, left_second = make_messages(
        departures, innovation, obs_weight, send_rows[0].T
    )
    left = hop(right_first, 0, 1, 0)
    right = hop(left_first, 0, -1, 0)
    other = hop(near, 0, 0, 1)
    left_more = hop(right_second, 0, 1, 0)
    right_more = hop(left_second, 0, -1, 0)

    whole = lambda which: ((0, which, 0), (1, which, HALF))
    at_end = 2 * HALF
    found = pick_rows(
        ((whole(0), (0, at_end, 0), None), (whole(1), (1, at_end, 1), None)), SHORT, near, other
    )
    mean, perturb = perturbations(state)
    left, right, found, mean, perturb = lax.optimization_barrier(
        (left, right, found, mean, perturb)
    )
    far_low, far_high = hop(left, 0, 1, 0), hop(right, 0, -1, 0)

    def firsts(core):
        return (((0, 0, 32),), (0, 0, core), None), (((1, 1, 16),), (1, 0, core), None)

    def seconds(core):
        return (((1, 2, 0),), (0, 0, core), 4), (((0, 3, 0),), (1, 0, core), 5)

    same = pick_rows(firsts(0), LONG, left, right)
    left, right, same = lax.optimization_barrier((left, right, same))
    left_other, right_other = hop(left, 0, 0, 1), hop(right, 0, 0, 1)
    same = pick_rows(seconds(0), MID, left, right, left_more, right_more, *same)
    left_more, right_more, same = lax.optimization_barrier((left_more, right_more, same))
    left_more_other, right_more_other = hop(left_more, 0, 0, 1), hop(right_more, 0, 0, 1)
    cross = pick_rows(firsts(1), SHORT, left_other, right_other)
    cross = pick_rows(
        seconds(1), SHORT, left_other, right_other, left_more_other, right_more_other, *cross
    )
    far_low, far_high, cross = lax.optimization_barrier((far_low, far_high, cross))
    far_low_other, far_high_other = hop(far_low, 0, 0, 1), hop(far_high, 0, 0, 1)
    far = pick_rows(((((0, 0, 32), (1, 1, 16)), (0, 16, 0), None),), SHORT, far_low, far_high)[0]
    last = (far_low_other, far_high_other, far, *found, same[0], cross[0], same[1], cross[1])

    up, down = last_grams((2, 2), (0, 4), (4, 4), BF16, *last)
    from_up, from_down = hop(up, 1, 0, 0), hop(down, -1, 0, 0)
    up, down = last_grams((1, 3), (0, 0), (8, 8), F32, *last)
    up, down = relay(up, down, from_up, from_down)
    from_up, from_down = hop(up, 1, 0, 0), hop(down, -1, 0, 0)
    own = last_grams((0,), (0,), (8,), F32, *last)[0]
    parts = sum_parts(own, from_up, from_down)
    parts = lax.all_to_all(parts, "obs", 0, 0, tiled=True)

    own = transposed_weights(parts)
    low = lax.ppermute(own, "grid", [(j, (j + 1) % n_grid) for j in range(n_grid)])
    high = lax.ppermute(own, "grid", [(j, (j - 1) % n_grid) for j in range(n_grid)])
    part = own_part(own, mean, perturb)
    return add_sides(low, high, part, perturb)


def solution(mesh):
    in_specs = (
        P(("obs", "grid"), None),
        P(("obs", "grid")),
        P(("obs", "grid")),
        P(("obs", "grid"), None, None),
        P(("obs", "grid"), None),
        P("obs", None, "grid"),
    )
    out_specs = P("obs", None, "grid")
    return jax.shard_map(
        on_device, mesh=mesh, in_specs=in_specs, out_specs=out_specs, check_vma=False
    )
```

```python
import functools

import jax
import jax.numpy as jnp
from jax import lax
from jax.experimental import pallas as pl
from jax.experimental.pallas import tpu as pltpu
from jax.sharding import PartitionSpec as P

ITERS = 6
Y, X, CORES = 4, 4, 2
F32, BF16 = jnp.float32, jnp.bfloat16
K = 128
LOW = 512
BLOCKS = 4
HALF = 2 * K + 16
PACK = 80
VMEM = 20 * 1024 * 1024


def params():
    return pltpu.CompilerParams(vmem_limit_bytes=VMEM)


LONG, MID, SHORT = 6e10, 6e10, 1e6


def cost(flops):
    return pl.CostEstimate(flops=int(flops), bytes_accessed=100_000, transcendentals=0)


def in_vmem(count):
    return [pl.BlockSpec(memory_space=pltpu.VMEM)] * count


def hop(value, dy, dx, dc):
    pairs = []
    for place in range(Y * X * CORES):
        y, x, c = place // (X * CORES), place // CORES % X, place % CORES
        pairs.append((place, ((y + dy) % Y * X + (x + dx) % X) * CORES + (c ^ dc)))
    return lax.ppermute(value, "grid", pairs)


def dims(m, n):
    return (((m,), (n,)), ((), ()))


def message_kernel(*refs):
    sources, (near, right_first, right_second, left_first, left_second) = refs[:4], refs[4:9]
    held, (turned, sems) = refs[9:13], refs[13:]
    copies = [
        pltpu.make_async_copy(source, place, sems.at[i])
        for i, (source, place) in enumerate(zip(sources, held))
    ]
    for copy in copies[::-1]:
        copy.start()
    departures, innovation, obs_weight, send_rows = held
    copies[3].wait()
    grid = lax.axis_index("grid")
    x, c = lax.rem(lax.div(grid, CORES), X), lax.rem(grid, CORES)
    turned[...] = send_rows[...].T
    groups = []
    for dx in range(X):
        halves = []
        for dc in range(CORES):
            cx = lax.rem(x + dx, X) * CORES + lax.rem(c + dc, CORES)
            lines = []
            for y in range(Y):
                rows = turned[pl.ds(y * X * CORES + cx, 8, stride=Y * X * CORES), :]
                pair = [rows[0:4], rows[4:8]]
                pairs = jnp.concatenate(pair[::-1] if dc else pair, axis=1)
                fours = jnp.concatenate([pairs[0:2], pairs[2:4]], axis=1)
                lines.append(jnp.concatenate([fours[0:1], fours[1:2]], axis=1))
            picks = jnp.concatenate(lines, axis=0)
            halves.append(lax.shift_right_arithmetic(picks, 8))
            halves.append(jnp.bitwise_and(picks, 255))
        groups.append(jnp.concatenate(halves, axis=0).astype(F32).astype(BF16))
    near[2 * HALF :, :] = groups[0]
    right_first[:16, :] = groups[1]
    right_first[16:32, :] = groups[2]
    left_first[:16, :] = groups[3]
    for copy in copies[:3]:
        copy.wait()
    root = jnp.sqrt(obs_weight[...].reshape(1, BLOCKS * LOW))
    innov = innovation[...].reshape(1, BLOCKS * LOW) * root
    row = lax.broadcasted_iota(jnp.int32, (16, LOW), 0)
    places = (
        ((near, 0), (right_first, 32), (left_second, 0)),
        ((near, HALF), (left_first, 16), (right_second, 0)),
    )
    for half in range(2):
        tail = jnp.zeros((16, LOW), F32)
        for block in range(2):
            start = (2 * half + block) * LOW
            span = slice(start, start + LOW)
            rows = (departures[span, :].astype(F32).T * root[:, span]).astype(BF16)
            for ref, at in places[half]:
                ref[at + block * K : at + (block + 1) * K, :] = rows
            tail = jnp.where(row == block, innov[:, span], tail)
        for ref, at in places[half]:
            ref[at + 2 * K : at + HALF, :] = tail.astype(BF16)


def make_messages(*args):
    rows = (2 * HALF + 16, HALF + 32, HALF, HALF + 16, HALF)
    return pl.pallas_call(
        message_kernel,
        out_shape=[jax.ShapeDtypeStruct((count, LOW), BF16) for count in rows],
        in_specs=[pl.BlockSpec(memory_space=pltpu.HBM)] * 4,
        out_specs=in_vmem(len(rows)),
        scratch_shapes=[pltpu.VMEM(arg.shape, arg.dtype) for arg in args]
        + [pltpu.VMEM(args[3].shape[::-1], jnp.int32), pltpu.SemaphoreType.DMA((4,))],
        compiler_params=pltpu.CompilerParams(vmem_limit_bytes=60 * 1024 * 1024),
        cost_estimate=cost(2e9),
    )(*args)


def read_picks(group, core):
    values = group[8 * core : 8 * core + 8].astype(F32)
    return (values[0:4] * 256.0 + values[4:8]).astype(jnp.int32)


def pick(parts, picks):
    high = lax.shift_right_arithmetic(picks, 9)
    first = parts[0][0]
    live = picks >= 0 if len(parts) == 2 else lax.shift_right_arithmetic(high, 1) == first
    low = jnp.where(live, jnp.bitwise_and(picks, LOW - 1), -1)
    place = lax.broadcasted_iota(jnp.int32, (LOW, 256), 0).astype(jnp.int16)
    low = jnp.broadcast_to(low, (LOW, 256)).astype(jnp.int16)
    one_hot = jnp.where(place == low, jnp.ones((), BF16), jnp.zeros((), BF16))
    blocks, innovs = [], []
    for _, rows in parts:
        found = jnp.dot(rows, one_hot, preferred_element_type=F32)
        blocks += [found[:K], found[K : 2 * K]]
        innovs += [found[2 * K : 2 * K + 1], found[2 * K + 1 : 2 * K + 2]]
    members, innov = blocks[0], innovs[0]
    for block in range(1, len(blocks)):
        here = high == 2 * first + block
        members = jnp.where(here, blocks[block], members)
        innov = jnp.where(here, innovs[block], innov)
    return jnp.concatenate([members, jnp.broadcast_to(innov, (16, 256))], axis=0).astype(BF16)


def pick_kernel(sources, count, *refs):
    outs = refs[count:]
    picks = [read_picks(refs[which][at : at + 16, :], core) for _, (which, at, core), _ in sources]
    for step in range(2 * Y):
        y, span = step // 2, slice(step % 2 * 256, step % 2 * 256 + 256)
        for out, (parts, _, before), values in zip(outs, sources, picks):
            tables = [(half, refs[which][at : at + HALF, :]) for half, which, at in parts]
            found = pick(tables, values[y : y + 1, span])
            out[step] = found if before is None else found + refs[before][step]


def pick_rows(sources, flops, *args):
    return pl.pallas_call(
        functools.partial(pick_kernel, sources, len(args)),
        out_shape=[jax.ShapeDtypeStruct((2 * Y, 144, 256), BF16)] * len(sources),
        in_specs=in_vmem(len(args)),
        out_specs=in_vmem(len(sources)),
        compiler_params=params(),
        cost_estimate=cost(flops),
    )(*args)


def join(first, second):
    low = lax.broadcasted_iota(jnp.int32, first.shape, 1) < K // 2
    return jnp.where(low, first, second), jnp.where(low, second, first)


def pack(total):
    row = lax.broadcasted_iota(jnp.int32, (64, K), 0)
    lane = lax.broadcasted_iota(jnp.int32, (64, K), 1)
    lower = total[64:K]
    upper = jnp.where(lane < row, pltpu.roll(lower, 64, 1), total[0:64])
    diagonal = jnp.sum(jnp.where(lane == row + 64, lower, 0.0), axis=0, keepdims=True)
    tail = jnp.where(lax.broadcasted_iota(jnp.int32, (16, K), 0) == 0, diagonal, total[K:])
    return jnp.concatenate([upper, tail], axis=0)


def unpack(packed):
    row = lax.broadcasted_iota(jnp.int32, (64, K), 0)
    lane = lax.broadcasted_iota(jnp.int32, (64, K), 1)
    upper = packed[0:64]
    above = jnp.where(lane > row, upper, 0.0)
    below = pltpu.roll(jnp.where(lane < row, upper, 0.0), 64, 1)
    off = jnp.concatenate([above, below], axis=0)
    low = jnp.where(lane == row + 64, packed[64:65], 0.0)
    diagonal = jnp.concatenate([jnp.where(lane == row, upper, 0.0), low], axis=0)
    return off + off.T + diagonal, packed[65:66]


def last_kernel(shifts, low, high, same, *rest):
    found, outs, picks = rest[:6], rest[6:-1], rest[-1]
    place = lax.div(lax.axis_index("grid"), X * CORES)
    picks[...] = read_picks(low[16:32, :], 1)
    table = ((0, low[32:, :]), (1, high[16:, :]))
    for out, shift in zip(outs, shifts):
        y = lax.rem(place + shift, Y)
        for i in range(2):
            span = slice(i * 256, i * 256 + 256)
            last = pick(table, picks[pl.ds(y, 1), :][:, span])
            shards = [ref[2 * y + i] for ref in (*found, same)] + [last]
            for half in range(2):
                span = slice(half * K, half * K + K)
                pairs = [
                    join(shards[n][:, span], shards[n + 1][:, span])
                    for n in range(0, len(shards), 2)
                ]
                for side in range(2):
                    rows = jnp.concatenate([pair[side] for pair in pairs], axis=1)
                    total = lax.dot_general(rows, rows[:K], dims(1, 1), preferred_element_type=F32)
                    out[i + 2 * half + 4 * side] = pack(total).astype(out.dtype)


def last_grams(shifts, dtype, *args):
    return pl.pallas_call(
        functools.partial(last_kernel, shifts),
        out_shape=[jax.ShapeDtypeStruct((8, PACK, K), dtype)] * len(shifts),
        in_specs=in_vmem(len(args)),
        out_specs=in_vmem(len(shifts)),
        scratch_shapes=[pltpu.VMEM((Y, LOW), jnp.int32)],
        compiler_params=params(),
        cost_estimate=cost(1e9 * len(shifts)),
    )(*args)


def sum_kernel(own, a, b, c, out):
    others = a[...].astype(F32) + b[...].astype(F32) + c[...].astype(F32)
    out[...] = (own[...] + others).astype(BF16)


def sum_parts(*args):
    return pl.pallas_call(
        sum_kernel,
        out_shape=jax.ShapeDtypeStruct(args[0].shape, BF16),
        in_specs=in_vmem(4),
        out_specs=in_vmem(1)[0],
        compiler_params=params(),
        cost_estimate=cost(5e8),
    )(*args)


def split(value):
    high = value.astype(BF16)
    return high, (value - high.astype(F32)).astype(BF16)


def product(left, right):
    lh, ll = split(left)
    rh, rl = split(right)
    return jnp.dot(
        jnp.concatenate([lh, lh, ll], axis=1),
        jnp.concatenate([rh, rl, rh], axis=0),
        preferred_element_type=F32,
    )


def weights_kernel(parts, out):
    gram, pull = unpack(jnp.sum(parts[...].astype(F32), axis=0))
    row = lax.broadcasted_iota(jnp.int32, (K, K), 0)
    col = lax.broadcasted_iota(jnp.int32, (K, K), 1)
    identity = (row == col).astype(F32)
    system = gram + (K - 1.0) * identity
    squares = jnp.sum(jnp.sum(system * system, axis=0, keepdims=True), axis=1, keepdims=True)
    frob = jnp.sqrt(squares)
    iterate = system / frob
    inverse = 1.5 * identity - 0.5 * iterate
    iterate = product(inverse, iterate)
    for sweep in range(1, ITERS):
        newton = 1.5 * identity - 0.5 * product(inverse, iterate)
        if sweep < ITERS - 1:
            both = product(newton, jnp.concatenate([iterate, inverse], axis=1))
            iterate, inverse = both[:, :K], both[:, K:]
        else:
            inverse = product(newton, inverse)
    shift = product(product(jnp.broadcast_to(pull, (16, K)), inverse), inverse)[0:1] / frob
    out[...] = (jnp.sqrt((K - 1.0) / frob) * inverse.T + shift).astype(BF16)


def transposed_weights(parts):
    return pl.pallas_call(
        weights_kernel,
        out_shape=jax.ShapeDtypeStruct((K, K), BF16),
        in_specs=in_vmem(1),
        out_specs=in_vmem(1)[0],
        compiler_params=params(),
        cost_estimate=cost(4e9),
    )(parts)


def perturb_kernel(state, mean, perturb):
    for pair in range(mean.shape[0]):
        for i in range(2):
            span = slice(i * K, (i + 1) * K)
            values = state[2 * pair + i].astype(F32)
            average = jnp.mean(values, axis=0, keepdims=True)
            mean[pair : pair + 1, span] = average
            perturb[pair, :, span] = (values - average).astype(BF16)


def perturbations(state):
    pairs = state.shape[0] // 2
    return pl.pallas_call(
        perturb_kernel,
        out_shape=[
            jax.ShapeDtypeStruct((pairs, 2 * K), F32),
            jax.ShapeDtypeStruct((pairs, K, 2 * K), BF16),
        ],
        in_specs=in_vmem(1),
        out_specs=in_vmem(2),
        compiler_params=params(),
        cost_estimate=cost(2e9),
    )(state)


def column_coefs():
    lane = lax.broadcasted_iota(jnp.int32, (1, 2 * K), 1) % K
    position = (lane.astype(F32) + 0.5) / K
    return lane, jnp.maximum(0.5 - position, 0.0), jnp.maximum(position - 0.5, 0.0)


def own_kernel(own, mean, perturb, out):
    _, left_coef, right_coef = column_coefs()
    own_coef = 1.0 - left_coef - right_coef
    for pair in range(mean.shape[0]):
        sums = jnp.dot(own[...], perturb[pair], preferred_element_type=F32)
        out[pair] = mean[pair : pair + 1] + own_coef * sums


def own_part(own, mean, perturb):
    return pl.pallas_call(
        own_kernel,
        out_shape=jax.ShapeDtypeStruct(perturb.shape, F32),
        in_specs=in_vmem(3),
        out_specs=in_vmem(1)[0],
        compiler_params=params(),
        cost_estimate=cost(2e9),
    )(own, mean, perturb)


def side_kernel(left, right, part, perturb, out, held, sems):
    lane, left_coef, right_coef = column_coefs()
    coef = left_coef + right_coef
    weights = jnp.concatenate([left[...], right[...]], axis=0)
    chunks = sems.shape[0]
    pairs = perturb.shape[0] // chunks
    copies = []
    for chunk in range(chunks):
        for pair in range(chunk * pairs, (chunk + 1) * pairs):
            sums = jnp.dot(weights, perturb[pair], preferred_element_type=F32)
            side = jnp.where(lane < K // 2, sums[:K], sums[K:])
            total = (part[pair] + coef * side).astype(BF16)
            for i in range(2):
                held[2 * pair + i] = total[:, i * K : (i + 1) * K]
        rows = pl.ds(2 * chunk * pairs, 2 * pairs)
        copies.append(pltpu.make_async_copy(held.at[rows], out.at[rows], sems.at[chunk]))
        copies[-1].start()
    for copy in copies:
        copy.wait()


def add_sides(left, right, part, perturb):
    shape = (2 * perturb.shape[0], K, K)
    return pl.pallas_call(
        side_kernel,
        out_shape=jax.ShapeDtypeStruct(shape, BF16),
        in_specs=in_vmem(4),
        out_specs=pl.BlockSpec(memory_space=pltpu.HBM),
        scratch_shapes=[pltpu.VMEM(shape, BF16), pltpu.SemaphoreType.DMA((6,))],
        compiler_params=params(),
        cost_estimate=cost(2e9),
    )(left, right, part, perturb)


def on_device(departures, innovation, obs_weight, send_rows, send_counts, state):
    n_grid = lax.axis_size("grid")
    near, right_first, right_second, left_first, left_second = make_messages(
        departures, innovation, obs_weight, send_rows[0].T
    )
    left = hop(right_first, 0, 1, 0)
    right = hop(left_first, 0, -1, 0)
    other = hop(near, 0, 0, 1)
    left_more = hop(right_second, 0, 1, 0)
    right_more = hop(left_second, 0, -1, 0)

    whole = lambda which: ((0, which, 0), (1, which, HALF))
    at_end = 2 * HALF
    found = pick_rows(
        ((whole(0), (0, at_end, 0), None), (whole(1), (1, at_end, 1), None)), SHORT, near, other
    )
    mean, perturb = perturbations(state)
    left, right, found, mean, perturb = lax.optimization_barrier(
        (left, right, found, mean, perturb)
    )
    far_low, far_high = hop(left, 0, 1, 0), hop(right, 0, -1, 0)

    def firsts(core):
        return (((0, 0, 32),), (0, 0, core), None), (((1, 1, 16),), (1, 0, core), None)

    def seconds(core):
        return (((1, 2, 0),), (0, 0, core), 4), (((0, 3, 0),), (1, 0, core), 5)

    same = pick_rows(firsts(0), LONG, left, right)
    left, right, same = lax.optimization_barrier((left, right, same))
    left_other, right_other = hop(left, 0, 0, 1), hop(right, 0, 0, 1)
    same = pick_rows(seconds(0), MID, left, right, left_more, right_more, *same)
    left_more, right_more, same = lax.optimization_barrier((left_more, right_more, same))
    left_more_other, right_more_other = hop(left_more, 0, 0, 1), hop(right_more, 0, 0, 1)
    cross = pick_rows(firsts(1), SHORT, left_other, right_other)
    cross = pick_rows(
        seconds(1), SHORT, left_other, right_other, left_more_other, right_more_other, *cross
    )
    far_low, far_high, cross = lax.optimization_barrier((far_low, far_high, cross))
    far_low_other, far_high_other = hop(far_low, 0, 0, 1), hop(far_high, 0, 0, 1)
    far = pick_rows(((((0, 0, 32), (1, 1, 16)), (0, 16, 0), None),), SHORT, far_low, far_high)[0]
    last = (far_low_other, far_high_other, far, *found, same[0], cross[0], same[1], cross[1])

    across = last_grams((2,), BF16, *last)[0]
    from_across = hop(across, 2, 0, 0)
    up, down = last_grams((1, 3), BF16, *last)
    from_up, from_down = hop(up, 1, 0, 0), hop(down, -1, 0, 0)
    own = last_grams((0,), F32, *last)[0]
    parts = sum_parts(own, from_across, from_up, from_down)
    parts = lax.all_to_all(parts, "obs", 0, 0, tiled=True)

    own = transposed_weights(parts)
    low = lax.ppermute(own, "grid", [(j, (j + 1) % n_grid) for j in range(n_grid)])
    high = lax.ppermute(own, "grid", [(j, (j - 1) % n_grid) for j in range(n_grid)])
    part = own_part(own, mean, perturb)
    return add_sides(low, high, part, perturb)


def solution(mesh):
    in_specs = (
        P(("obs", "grid"), None),
        P(("obs", "grid")),
        P(("obs", "grid")),
        P(("obs", "grid"), None, None),
        P(("obs", "grid"), None),
        P("obs", None, "grid"),
    )
    out_specs = P("obs", None, "grid")
    return jax.shard_map(
        on_device, mesh=mesh, in_specs=in_specs, out_specs=out_specs, check_vma=False
    )
```

```python
import functools

import jax
import jax.numpy as jnp
from jax import lax
from jax.experimental import pallas as pl
from jax.experimental.pallas import tpu as pltpu
from jax.sharding import PartitionSpec as P

ITERS = 6
Y, X, CORES = 4, 4, 2
F32, BF16 = jnp.float32, jnp.bfloat16
K = 128
LOW = 512
BLOCKS = 4
HALF = 2 * K + 16
PACK = 80
VMEM = 20 * 1024 * 1024


def params():
    return pltpu.CompilerParams(vmem_limit_bytes=VMEM)


LONG, SHORT = 6e10, 1e6


def cost(flops):
    return pl.CostEstimate(flops=int(flops), bytes_accessed=100_000, transcendentals=0)


def in_vmem(count):
    return [pl.BlockSpec(memory_space=pltpu.VMEM)] * count


def hop(value, dy, dx, dc):
    pairs = []
    for place in range(Y * X * CORES):
        y, x, c = place // (X * CORES), place // CORES % X, place % CORES
        pairs.append((place, ((y + dy) % Y * X + (x + dx) % X) * CORES + (c ^ dc)))
    return lax.ppermute(value, "grid", pairs)


def dims(m, n):
    return (((m,), (n,)), ((), ()))


def send_picks(turned, cx, swapped):
    lines = []
    for y in range(Y):
        rows = turned[pl.ds(y * X * CORES + cx, 8, stride=Y * X * CORES), :]
        pair = [rows[0:4], rows[4:8]]
        pairs = jnp.concatenate(pair[::-1] if swapped else pair, axis=1)
        fours = jnp.concatenate([pairs[0:2], pairs[2:4]], axis=1)
        lines.append(jnp.concatenate([fours[0:1], fours[1:2]], axis=1))
    picks = jnp.concatenate(lines, axis=0)
    power = jnp.maximum(lax.shift_right_arithmetic(picks, 7), 0)
    code = lax.shift_left(128 + jnp.bitwise_and(picks, 127), power)
    return jnp.where(picks >= 0, code, 0).astype(F32)


def read_picks(rows):
    left = rows.astype(F32)
    high = jnp.zeros_like(left)
    for step in (8, 4, 2, 1):
        large = left >= 128.0 * 2**step
        left = jnp.where(large, left * 0.5**step, left)
        high = jnp.where(large, high + step, high)
    return jnp.where(left > 0.0, left - 128.0 + 128.0 * high, -1.0).astype(jnp.int32)


def message_kernel(departures, innovation, obs_weight, send_rows, *refs):
    outs, (rows, innov, weight, picks, turned) = refs[:3], refs[3:8]
    built, (in_sems, out_sems) = refs[8:11], refs[11:]
    small = ((send_rows, picks), (obs_weight, weight), (innovation, innov))
    small = [pltpu.make_async_copy(*pair, in_sems.at[i]) for i, pair in enumerate(small)]
    large = []
    for block in range(BLOCKS):
        span = pl.ds(block * LOW, LOW)
        large.append(
            pltpu.make_async_copy(departures.at[span], rows.at[span], in_sems.at[3 + block])
        )
    for copy in small + large:
        copy.start()
    small[0].wait()
    grid = lax.axis_index("grid")
    x, c = lax.rem(lax.div(grid, CORES), X), lax.rem(grid, CORES)
    turned[...] = picks[...].T
    groups = []
    for dx in range(X):
        for dc in range(CORES):
            cx = lax.rem(x + dx, X) * CORES + lax.rem(c + dc, CORES)
            groups.append(send_picks(turned, cx, dc == 1))
    small[1].wait()
    small[2].wait()
    root = jnp.sqrt(weight[...].reshape(1, BLOCKS * LOW))
    scaled = innov[...].reshape(1, BLOCKS * LOW) * root
    blank = jnp.zeros((2, LOW), F32)
    both, out_both = built[2], outs[2]
    copies = []
    for half in range(2):
        one, out_one = built[half], outs[half]
        at = half * HALF
        innovs = []
        for block in range(2):
            start = (2 * half + block) * LOW
            span = slice(start, start + LOW)
            large[2 * half + block].wait()
            part = (rows[span, :].astype(F32).T * root[:, span]).astype(BF16)
            one[block * K : (block + 1) * K, :] = part
            both[at + block * K : at + (block + 1) * K, :] = part
            innovs.append(scaled[:, span])
        top = innovs + [blank, groups[4 + half]]
        next_one = groups[2:4] if half == 0 else groups[6:8]
        one[2 * K :, :] = jnp.concatenate(top + next_one, axis=0).astype(BF16)
        both[at + 2 * K : at + HALF, :] = jnp.concatenate(top + groups[0:2], axis=0).astype(BF16)
        copies.append(pltpu.make_async_copy(one, out_one, out_sems.at[half]))
        span = pl.ds(at, HALF)
        copies.append(
            pltpu.make_async_copy(both.at[span], out_both.at[span], out_sems.at[2 + half])
        )
        for copy in copies[-2:]:
            copy.start()
    for copy in copies:
        copy.wait()


def make_messages(*args):
    shapes = [(HALF, LOW), (HALF, LOW), (2 * HALF, LOW)]
    hbm = pl.BlockSpec(memory_space=pltpu.HBM)
    return pl.pallas_call(
        message_kernel,
        out_shape=[jax.ShapeDtypeStruct(shape, BF16) for shape in shapes],
        in_specs=[hbm] * 4,
        out_specs=[hbm] * 3,
        scratch_shapes=[pltpu.VMEM(arg.shape, arg.dtype) for arg in args]
        + [pltpu.VMEM(args[3].shape[::-1], jnp.int32)]
        + [pltpu.VMEM(shape, BF16) for shape in shapes]
        + [pltpu.SemaphoreType.DMA((3 + BLOCKS,)), pltpu.SemaphoreType.DMA((4,))],
        compiler_params=pltpu.CompilerParams(vmem_limit_bytes=60 * 1024 * 1024),
        cost_estimate=cost(2e9),
    )(*args)


def pick(parts, picks):
    high = lax.shift_right_arithmetic(picks, 9)
    first = parts[0][0]
    live = picks >= 0 if len(parts) == 2 else lax.shift_right_arithmetic(high, 1) == first
    low = jnp.where(live, jnp.bitwise_and(picks, LOW - 1), -1)
    place = lax.broadcasted_iota(jnp.int32, (LOW, 256), 0).astype(jnp.int16)
    low = jnp.broadcast_to(low, (LOW, 256)).astype(jnp.int16)
    one_hot = jnp.where(place == low, jnp.ones((), BF16), jnp.zeros((), BF16))
    blocks, innovs = [], []
    for _, rows in parts:
        found = jnp.dot(rows, one_hot, preferred_element_type=F32)
        blocks += [found[:K], found[K : 2 * K]]
        innovs += [found[2 * K : 2 * K + 1], found[2 * K + 1 : 2 * K + 2]]
    members, innov = blocks[0], innovs[0]
    for block in range(1, len(blocks)):
        here = high == 2 * first + block
        members = jnp.where(here, blocks[block], members)
        innov = jnp.where(here, innovs[block], innov)
    return jnp.concatenate([members, jnp.broadcast_to(innov, (16, 256))], axis=0).astype(BF16)


def tail_picks(ref, at, row):
    return read_picks(ref[at + 2 * K : at + HALF, :].astype(F32)[row : row + 4])


def pick_kernel(sources, count, *refs):
    outs = refs[count:]
    picks = [tail_picks(refs[which], at, row) for _, (which, at, row), _ in sources]
    for step in range(2 * Y):
        y, span = step // 2, slice(step % 2 * 256, step % 2 * 256 + 256)
        for out, (parts, _, before), values in zip(outs, sources, picks):
            tables = [(half, refs[which][at : at + HALF, :]) for half, which, at in parts]
            found = pick(tables, values[y : y + 1, span])
            out[step] = found if before is None else found + refs[before][step]


def pick_rows(sources, flops, *args):
    return pl.pallas_call(
        functools.partial(pick_kernel, sources, len(args)),
        out_shape=[jax.ShapeDtypeStruct((2 * Y, 144, 256), BF16)] * len(sources),
        in_specs=in_vmem(len(args)),
        out_specs=in_vmem(len(sources)),
        compiler_params=params(),
        cost_estimate=cost(flops),
    )(*args)


def join(first, second):
    low = lax.broadcasted_iota(jnp.int32, first.shape, 1) < K // 2
    return jnp.where(low, first, second), jnp.where(low, second, first)


def pack(total):
    row = lax.broadcasted_iota(jnp.int32, (64, K), 0)
    lane = lax.broadcasted_iota(jnp.int32, (64, K), 1)
    lower = total[64:K]
    upper = jnp.where(lane < row, pltpu.roll(lower, 64, 1), total[0:64])
    diagonal = jnp.sum(jnp.where(lane == row + 64, lower, 0.0), axis=0, keepdims=True)
    tail = jnp.where(lax.broadcasted_iota(jnp.int32, (16, K), 0) == 0, diagonal, total[K:])
    return jnp.concatenate([upper, tail], axis=0)


def unpack(packed):
    row = lax.broadcasted_iota(jnp.int32, (64, K), 0)
    lane = lax.broadcasted_iota(jnp.int32, (64, K), 1)
    upper = packed[0:64]
    above = jnp.where(lane > row, upper, 0.0)
    below = pltpu.roll(jnp.where(lane < row, upper, 0.0), 64, 1)
    off = jnp.concatenate([above, below], axis=0)
    low = jnp.where(lane == row + 64, packed[64:65], 0.0)
    diagonal = jnp.concatenate([jnp.where(lane == row, upper, 0.0), low], axis=0)
    return off + off.T + diagonal, packed[65:66]


def last_kernel(shifts, low, high, same, *rest):
    found, outs, picks = rest[:6], rest[6:-1], rest[-1]
    place = lax.div(lax.axis_index("grid"), X * CORES)
    picks[...] = tail_picks(high, 0, 4)
    table = ((0, low[...]), (1, high[...]))
    for out, shift in zip(outs, shifts):
        y = lax.rem(place + shift, Y)
        for i in range(2):
            span = slice(i * 256, i * 256 + 256)
            last = pick(table, picks[pl.ds(y, 1), :][:, span])
            shards = [ref[2 * y + i] for ref in (*found, same)] + [last]
            for half in range(2):
                span = slice(half * K, half * K + K)
                pairs = [
                    join(shards[n][:, span], shards[n + 1][:, span])
                    for n in range(0, len(shards), 2)
                ]
                for side in range(2):
                    rows = jnp.concatenate([pair[side] for pair in pairs], axis=1)
                    total = lax.dot_general(rows, rows[:K], dims(1, 1), preferred_element_type=F32)
                    out[i + 2 * half + 4 * side] = pack(total).astype(out.dtype)


def last_grams(shifts, dtype, *args):
    return pl.pallas_call(
        functools.partial(last_kernel, shifts),
        out_shape=[jax.ShapeDtypeStruct((8, PACK, K), dtype)] * len(shifts),
        in_specs=in_vmem(len(args)),
        out_specs=in_vmem(len(shifts)),
        scratch_shapes=[pltpu.VMEM((Y, LOW), jnp.int32)],
        compiler_params=params(),
        cost_estimate=cost(1e9 * len(shifts)),
    )(*args)


def sum_kernel(own, a, b, c, out):
    others = a[...].astype(F32) + b[...].astype(F32) + c[...].astype(F32)
    out[...] = (own[...] + others).astype(BF16)


def sum_parts(*args):
    return pl.pallas_call(
        sum_kernel,
        out_shape=jax.ShapeDtypeStruct(args[0].shape, BF16),
        in_specs=in_vmem(4),
        out_specs=in_vmem(1)[0],
        compiler_params=params(),
        cost_estimate=cost(5e8),
    )(*args)


def split(value):
    high = value.astype(BF16)
    return high, (value - high.astype(F32)).astype(BF16)


def product(left, right):
    lh, ll = split(left)
    rh, rl = split(right)
    return jnp.dot(
        jnp.concatenate([lh, lh, ll], axis=1),
        jnp.concatenate([rh, rl, rh], axis=0),
        preferred_element_type=F32,
    )


def weights_kernel(parts, out):
    gram, pull = unpack(jnp.sum(parts[...].astype(F32), axis=0))
    row = lax.broadcasted_iota(jnp.int32, (K, K), 0)
    col = lax.broadcasted_iota(jnp.int32, (K, K), 1)
    identity = (row == col).astype(F32)
    system = gram + (K - 1.0) * identity
    squares = jnp.sum(jnp.sum(system * system, axis=0, keepdims=True), axis=1, keepdims=True)
    frob = jnp.sqrt(squares)
    iterate = system / frob
    inverse = 1.5 * identity - 0.5 * iterate
    iterate = product(inverse, iterate)
    for sweep in range(1, ITERS):
        newton = 1.5 * identity - 0.5 * product(inverse, iterate)
        if sweep < ITERS - 1:
            both = product(newton, jnp.concatenate([iterate, inverse], axis=1))
            iterate, inverse = both[:, :K], both[:, K:]
        else:
            inverse = product(newton, inverse)
    shift = product(product(jnp.broadcast_to(pull, (16, K)), inverse), inverse)[0:1] / frob
    out[...] = (jnp.sqrt((K - 1.0) / frob) * inverse.T + shift).astype(BF16)


def transposed_weights(parts):
    return pl.pallas_call(
        weights_kernel,
        out_shape=jax.ShapeDtypeStruct((K, K), BF16),
        in_specs=in_vmem(1),
        out_specs=in_vmem(1)[0],
        compiler_params=params(),
        cost_estimate=cost(4e9),
    )(parts)


def perturb_kernel(state, mean, perturb):
    for pair in range(mean.shape[0]):
        for i in range(2):
            span = slice(i * K, (i + 1) * K)
            values = state[2 * pair + i].astype(F32)
            average = jnp.mean(values, axis=0, keepdims=True)
            mean[pair : pair + 1, span] = average
            perturb[pair, :, span] = (values - average).astype(BF16)


def perturbations(state):
    pairs = state.shape[0] // 2
    return pl.pallas_call(
        perturb_kernel,
        out_shape=[
            jax.ShapeDtypeStruct((pairs, 2 * K), F32),
            jax.ShapeDtypeStruct((pairs, K, 2 * K), BF16),
        ],
        in_specs=in_vmem(1),
        out_specs=in_vmem(2),
        compiler_params=params(),
        cost_estimate=cost(SHORT),
    )(state)


def column_coefs():
    lane = lax.broadcasted_iota(jnp.int32, (1, 2 * K), 1) % K
    position = (lane.astype(F32) + 0.5) / K
    return lane, jnp.maximum(0.5 - position, 0.0), jnp.maximum(position - 0.5, 0.0)


def own_kernel(own, mean, perturb, out):
    _, left_coef, right_coef = column_coefs()
    own_coef = 1.0 - left_coef - right_coef
    for pair in range(mean.shape[0]):
        sums = jnp.dot(own[...], perturb[pair], preferred_element_type=F32)
        out[pair] = mean[pair : pair + 1] + own_coef * sums


def own_part(own, mean, perturb):
    return pl.pallas_call(
        own_kernel,
        out_shape=jax.ShapeDtypeStruct(perturb.shape, F32),
        in_specs=in_vmem(3),
        out_specs=in_vmem(1)[0],
        compiler_params=params(),
        cost_estimate=cost(2e9),
    )(own, mean, perturb)


def side_kernel(left, right, part, perturb, out, held, sems):
    lane, left_coef, right_coef = column_coefs()
    coef = left_coef + right_coef
    weights = jnp.concatenate([left[...], right[...]], axis=0)
    chunks = sems.shape[0]
    pairs = perturb.shape[0] // chunks
    copies = []
    for chunk in range(chunks):
        for pair in range(chunk * pairs, (chunk + 1) * pairs):
            sums = jnp.dot(weights, perturb[pair], preferred_element_type=F32)
            side = jnp.where(lane < K // 2, sums[:K], sums[K:])
            total = (part[pair] + coef * side).astype(BF16)
            for i in range(2):
                held[2 * pair + i] = total[:, i * K : (i + 1) * K]
        rows = pl.ds(2 * chunk * pairs, 2 * pairs)
        copies.append(pltpu.make_async_copy(held.at[rows], out.at[rows], sems.at[chunk]))
        copies[-1].start()
    for copy in copies:
        copy.wait()


def add_sides(left, right, part, perturb):
    shape = (2 * perturb.shape[0], K, K)
    return pl.pallas_call(
        side_kernel,
        out_shape=jax.ShapeDtypeStruct(shape, BF16),
        in_specs=in_vmem(4),
        out_specs=pl.BlockSpec(memory_space=pltpu.HBM),
        scratch_shapes=[pltpu.VMEM(shape, BF16), pltpu.SemaphoreType.DMA((6,))],
        compiler_params=params(),
        cost_estimate=cost(2e9),
    )(left, right, part, perturb)


def on_device(departures, innovation, obs_weight, send_rows, send_counts, state):
    n_grid = lax.axis_size("grid")
    low_half, high_half, near = make_messages(
        departures, innovation, obs_weight, send_rows[0].T
    )
    left = hop(low_half, 0, 1, 0)
    right = hop(high_half, 0, -1, 0)
    other = hop(near, 0, 0, 1)
    left_more = hop(high_half, 0, 1, 0)
    right_more = hop(low_half, 0, -1, 0)

    whole = lambda which: ((0, which, 0), (1, which, HALF))
    found = pick_rows(
        ((whole(0), (0, 0, 8), None), (whole(1), (1, 0, 12), None)), SHORT, near, other
    )
    mean, perturb = perturbations(state)
    left, right, found, mean, perturb = lax.optimization_barrier(
        (left, right, found, mean, perturb)
    )
    far_low, far_high = hop(left, 0, 1, 0), hop(right, 0, -1, 0)

    def firsts(core):
        row = 8 + 4 * core
        return (((0, 0, 0),), (0, 0, row), None), (((1, 1, 0),), (1, 0, row), None)

    def seconds(core):
        row = 8 + 4 * core
        return (((1, 2, 0),), (0, 0, row), 4), (((0, 3, 0),), (1, 0, row), 5)

    same = pick_rows(firsts(0), SHORT, left, right)
    left, right, same = lax.optimization_barrier((left, right, same))
    left_other, right_other = hop(left, 0, 0, 1), hop(right, 0, 0, 1)
    same = pick_rows(seconds(0), LONG, left, right, left_more, right_more, *same)
    left_more, right_more, same = lax.optimization_barrier((left_more, right_more, same))
    left_more_other, right_more_other = hop(left_more, 0, 0, 1), hop(right_more, 0, 0, 1)
    cross = pick_rows(firsts(1), LONG, left_other, right_other)
    cross = pick_rows(
        seconds(1), SHORT, left_other, right_other, left_more_other, right_more_other, *cross
    )
    far_low, far_high, cross = lax.optimization_barrier((far_low, far_high, cross))
    far_low_other, far_high_other = hop(far_low, 0, 0, 1), hop(far_high, 0, 0, 1)
    far = pick_rows(((((0, 0, 0), (1, 1, 0)), (0, 0, 4), None),), SHORT, far_low, far_high)[0]
    last = (far_low_other, far_high_other, far, *found, same[0], cross[0], same[1], cross[1])

    across = last_grams((2,), BF16, *last)[0]
    from_across = hop(across, 2, 0, 0)
    up, down = last_grams((1, 3), BF16, *last)
    from_up, from_down = hop(up, 1, 0, 0), hop(down, -1, 0, 0)
    own = last_grams((0,), F32, *last)[0]
    parts = sum_parts(own, from_across, from_up, from_down)
    parts = lax.all_to_all(parts, "obs", 0, 0, tiled=True)

    own = transposed_weights(parts)
    low = lax.ppermute(own, "grid", [(j, (j + 1) % n_grid) for j in range(n_grid)])
    high = lax.ppermute(own, "grid", [(j, (j - 1) % n_grid) for j in range(n_grid)])
    part = own_part(own, mean, perturb)
    return add_sides(low, high, part, perturb)


def solution(mesh):
    in_specs = (
        P(("obs", "grid"), None),
        P(("obs", "grid")),
        P(("obs", "grid")),
        P(("obs", "grid"), None, None),
        P(("obs", "grid"), None),
        P("obs", None, "grid"),
    )
    out_specs = P("obs", None, "grid")
    return jax.shard_map(
        on_device, mesh=mesh, in_specs=in_specs, out_specs=out_specs, check_vma=False
    )
```

```python
import functools

import jax
import jax.numpy as jnp
from jax import lax
from jax.experimental import pallas as pl
from jax.experimental.pallas import tpu as pltpu
from jax.sharding import PartitionSpec as P

ITERS = 6
Y, X, CORES = 4, 4, 2
F32, BF16 = jnp.float32, jnp.bfloat16
K = 128
LOW = 512
BLOCKS = 4
HALF = 2 * K + 16
PACK = 80
VMEM = 20 * 1024 * 1024


def params():
    return pltpu.CompilerParams(vmem_limit_bytes=VMEM)


LONG, SHORT = 6e10, 1e6


def cost(flops):
    return pl.CostEstimate(flops=int(flops), bytes_accessed=100_000, transcendentals=0)


def in_vmem(count):
    return [pl.BlockSpec(memory_space=pltpu.VMEM)] * count


def hop(value, dy, dx, dc):
    pairs = []
    for place in range(Y * X * CORES):
        y, x, c = place // (X * CORES), place // CORES % X, place % CORES
        pairs.append((place, ((y + dy) % Y * X + (x + dx) % X) * CORES + (c ^ dc)))
    return lax.ppermute(value, "grid", pairs)


def dims(m, n):
    return (((m,), (n,)), ((), ()))


def send_picks(turned, cx, swapped):
    lines = []
    for y in range(Y):
        rows = turned[pl.ds(y * X * CORES + cx, 8, stride=Y * X * CORES), :]
        pair = [rows[0:4], rows[4:8]]
        pairs = jnp.concatenate(pair[::-1] if swapped else pair, axis=1)
        fours = jnp.concatenate([pairs[0:2], pairs[2:4]], axis=1)
        lines.append(jnp.concatenate([fours[0:1], fours[1:2]], axis=1))
    picks = jnp.concatenate(lines, axis=0)
    power = jnp.maximum(lax.shift_right_arithmetic(picks, 7), 0)
    code = lax.shift_left(128 + jnp.bitwise_and(picks, 127), power)
    return jnp.where(picks >= 0, code, 0).astype(F32)


def read_picks(rows):
    left = rows.astype(F32)
    high = jnp.zeros_like(left)
    for step in (8, 4, 2, 1):
        large = left >= 128.0 * 2**step
        left = jnp.where(large, left * 0.5**step, left)
        high = jnp.where(large, high + step, high)
    return jnp.where(left > 0.0, left - 128.0 + 128.0 * high, -1.0).astype(jnp.int32)


def message_kernel(departures, innovation, obs_weight, send_rows, *refs):
    outs, (rows, innov, weight, picks, turned) = refs[:3], refs[3:8]
    built, (in_sems, out_sems) = refs[8:11], refs[11:]
    small = ((send_rows, picks), (obs_weight, weight), (innovation, innov))
    small = [pltpu.make_async_copy(*pair, in_sems.at[i]) for i, pair in enumerate(small)]
    large = []
    for block in range(BLOCKS):
        span = pl.ds(block * LOW, LOW)
        large.append(
            pltpu.make_async_copy(departures.at[span], rows.at[span], in_sems.at[3 + block])
        )
    for copy in small + large:
        copy.start()
    small[0].wait()
    grid = lax.axis_index("grid")
    x, c = lax.rem(lax.div(grid, CORES), X), lax.rem(grid, CORES)
    turned[...] = picks[...].T
    groups = []
    for dx in range(X):
        for dc in range(CORES):
            cx = lax.rem(x + dx, X) * CORES + lax.rem(c + dc, CORES)
            groups.append(send_picks(turned, cx, dc == 1))
    small[1].wait()
    small[2].wait()
    root = jnp.sqrt(weight[...].reshape(1, BLOCKS * LOW))
    scaled = innov[...].reshape(1, BLOCKS * LOW) * root
    blank = jnp.zeros((2, LOW), F32)
    both, out_both = built[2], outs[2]
    copies = []
    for half in range(2):
        one, out_one = built[half], outs[half]
        at = half * HALF
        innovs = []
        for block in range(2):
            start = (2 * half + block) * LOW
            span = slice(start, start + LOW)
            large[2 * half + block].wait()
            part = (rows[span, :].astype(F32).T * root[:, span]).astype(BF16)
            one[block * K : (block + 1) * K, :] = part
            both[at + block * K : at + (block + 1) * K, :] = part
            innovs.append(scaled[:, span])
        top = innovs + [blank, groups[4 + half]]
        next_one = groups[2:4] if half == 0 else groups[6:8]
        one[2 * K :, :] = jnp.concatenate(top + next_one, axis=0).astype(BF16)
        both[at + 2 * K : at + HALF, :] = jnp.concatenate(top + groups[0:2], axis=0).astype(BF16)
        copies.append(pltpu.make_async_copy(one, out_one, out_sems.at[half]))
        span = pl.ds(at, HALF)
        copies.append(
            pltpu.make_async_copy(both.at[span], out_both.at[span], out_sems.at[2 + half])
        )
        for copy in copies[-2:]:
            copy.start()
    for copy in copies:
        copy.wait()


def make_messages(*args):
    shapes = [(HALF, LOW), (HALF, LOW), (2 * HALF, LOW)]
    hbm = pl.BlockSpec(memory_space=pltpu.HBM)
    return pl.pallas_call(
        message_kernel,
        out_shape=[jax.ShapeDtypeStruct(shape, BF16) for shape in shapes],
        in_specs=[hbm] * 4,
        out_specs=[hbm] * 3,
        scratch_shapes=[pltpu.VMEM(arg.shape, arg.dtype) for arg in args]
        + [pltpu.VMEM(args[3].shape[::-1], jnp.int32)]
        + [pltpu.VMEM(shape, BF16) for shape in shapes]
        + [pltpu.SemaphoreType.DMA((3 + BLOCKS,)), pltpu.SemaphoreType.DMA((4,))],
        compiler_params=pltpu.CompilerParams(vmem_limit_bytes=60 * 1024 * 1024),
        cost_estimate=cost(2e9),
    )(*args)


def pick(parts, picks):
    high = lax.shift_right_arithmetic(picks, 9)
    first = parts[0][0]
    live = picks >= 0 if len(parts) == 2 else lax.shift_right_arithmetic(high, 1) == first
    low = jnp.where(live, jnp.bitwise_and(picks, LOW - 1), -1)
    place = lax.broadcasted_iota(jnp.int32, (LOW, 256), 0).astype(jnp.int16)
    low = jnp.broadcast_to(low, (LOW, 256)).astype(jnp.int16)
    one_hot = jnp.where(place == low, jnp.ones((), BF16), jnp.zeros((), BF16))
    blocks, innovs = [], []
    for _, rows in parts:
        found = jnp.dot(rows, one_hot, preferred_element_type=F32)
        blocks += [found[:K], found[K : 2 * K]]
        innovs += [found[2 * K : 2 * K + 1], found[2 * K + 1 : 2 * K + 2]]
    members, innov = blocks[0], innovs[0]
    for block in range(1, len(blocks)):
        here = high == 2 * first + block
        members = jnp.where(here, blocks[block], members)
        innov = jnp.where(here, innovs[block], innov)
    return jnp.concatenate([members, jnp.broadcast_to(innov, (16, 256))], axis=0).astype(BF16)


def tail_picks(ref, at, row):
    return read_picks(ref[at + 2 * K : at + HALF, :].astype(F32)[row : row + 4])


def pick_kernel(sources, count, *refs):
    outs = refs[count:]
    picks = [tail_picks(refs[which], at, row) for _, (which, at, row), _ in sources]
    for step in range(2 * Y):
        y, span = step // 2, slice(step % 2 * 256, step % 2 * 256 + 256)
        for out, (parts, _, before), values in zip(outs, sources, picks):
            tables = [(half, refs[which][at : at + HALF, :]) for half, which, at in parts]
            found = pick(tables, values[y : y + 1, span])
            out[step] = found if before is None else found + refs[before][step]


def pick_rows(sources, flops, *args):
    return pl.pallas_call(
        functools.partial(pick_kernel, sources, len(args)),
        out_shape=[jax.ShapeDtypeStruct((2 * Y, 144, 256), BF16)] * len(sources),
        in_specs=in_vmem(len(args)),
        out_specs=in_vmem(len(sources)),
        compiler_params=params(),
        cost_estimate=cost(flops),
    )(*args)


def join(first, second):
    low = lax.broadcasted_iota(jnp.int32, first.shape, 1) < K // 2
    return jnp.where(low, first, second), jnp.where(low, second, first)


def pack(total):
    row = lax.broadcasted_iota(jnp.int32, (64, K), 0)
    lane = lax.broadcasted_iota(jnp.int32, (64, K), 1)
    lower = total[64:K]
    upper = jnp.where(lane < row, pltpu.roll(lower, 64, 1), total[0:64])
    diagonal = jnp.sum(jnp.where(lane == row + 64, lower, 0.0), axis=0, keepdims=True)
    tail = jnp.where(lax.broadcasted_iota(jnp.int32, (16, K), 0) == 0, diagonal, total[K:])
    return jnp.concatenate([upper, tail], axis=0)


def unpack(packed):
    row = lax.broadcasted_iota(jnp.int32, (64, K), 0)
    lane = lax.broadcasted_iota(jnp.int32, (64, K), 1)
    upper = packed[0:64]
    above = jnp.where(lane > row, upper, 0.0)
    below = pltpu.roll(jnp.where(lane < row, upper, 0.0), 64, 1)
    off = jnp.concatenate([above, below], axis=0)
    low = jnp.where(lane == row + 64, packed[64:65], 0.0)
    diagonal = jnp.concatenate([jnp.where(lane == row, upper, 0.0), low], axis=0)
    return off + off.T + diagonal, packed[65:66]


def last_kernel(shifts, low, high, same, *rest):
    found, outs, picks = rest[:6], rest[6:-1], rest[-1]
    place = lax.div(lax.axis_index("grid"), X * CORES)
    picks[...] = tail_picks(high, 0, 4)
    table = ((0, low[...]), (1, high[...]))
    for out, shift in zip(outs, shifts):
        y = lax.rem(place + shift, Y)
        for i in range(2):
            span = slice(i * 256, i * 256 + 256)
            last = pick(table, picks[pl.ds(y, 1), :][:, span])
            shards = [ref[2 * y + i] for ref in (*found, same)] + [last]
            for half in range(2):
                span = slice(half * K, half * K + K)
                pairs = [
                    join(shards[n][:, span], shards[n + 1][:, span])
                    for n in range(0, len(shards), 2)
                ]
                for side in range(2):
                    rows = jnp.concatenate([pair[side] for pair in pairs], axis=1)
                    total = lax.dot_general(rows, rows[:K], dims(1, 1), preferred_element_type=F32)
                    out[i + 2 * half + 4 * side] = pack(total).astype(out.dtype)


def last_grams(shifts, dtype, *args):
    return pl.pallas_call(
        functools.partial(last_kernel, shifts),
        out_shape=[jax.ShapeDtypeStruct((8, PACK, K), dtype)] * len(shifts),
        in_specs=in_vmem(len(args)),
        out_specs=in_vmem(len(shifts)),
        scratch_shapes=[pltpu.VMEM((Y, LOW), jnp.int32)],
        compiler_params=params(),
        cost_estimate=cost(1e9 * len(shifts)),
    )(*args)


def sum_kernel(own, a, b, c, out):
    others = a[...].astype(F32) + b[...].astype(F32) + c[...].astype(F32)
    out[...] = (own[...] + others).astype(BF16)


def sum_parts(*args):
    return pl.pallas_call(
        sum_kernel,
        out_shape=jax.ShapeDtypeStruct(args[0].shape, BF16),
        in_specs=in_vmem(4),
        out_specs=in_vmem(1)[0],
        compiler_params=params(),
        cost_estimate=cost(5e8),
    )(*args)


def split(value):
    high = value.astype(BF16)
    return high, (value - high.astype(F32)).astype(BF16)


def product(left, right):
    lh, ll = split(left)
    rh, rl = split(right)
    return jnp.dot(
        jnp.concatenate([lh, lh, ll], axis=1),
        jnp.concatenate([rh, rl, rh], axis=0),
        preferred_element_type=F32,
    )


def weights_kernel(parts, out):
    gram, pull = unpack(jnp.sum(parts[...].astype(F32), axis=0))
    row = lax.broadcasted_iota(jnp.int32, (K, K), 0)
    col = lax.broadcasted_iota(jnp.int32, (K, K), 1)
    identity = (row == col).astype(F32)
    system = gram + (K - 1.0) * identity
    squares = jnp.sum(jnp.sum(system * system, axis=0, keepdims=True), axis=1, keepdims=True)
    frob = jnp.sqrt(squares)
    iterate = system / frob
    inverse = 1.5 * identity - 0.5 * iterate
    iterate = product(inverse, iterate)
    for sweep in range(1, ITERS):
        newton = 1.5 * identity - 0.5 * product(inverse, iterate)
        if sweep < ITERS - 1:
            both = product(newton, jnp.concatenate([iterate, inverse], axis=1))
            iterate, inverse = both[:, :K], both[:, K:]
        else:
            inverse = product(newton, inverse)
    shift = product(product(jnp.broadcast_to(pull, (16, K)), inverse), inverse)[0:1] / frob
    out[...] = (jnp.sqrt((K - 1.0) / frob) * inverse.T + shift).astype(BF16)


def transposed_weights(parts):
    return pl.pallas_call(
        weights_kernel,
        out_shape=jax.ShapeDtypeStruct((K, K), BF16),
        in_specs=in_vmem(1),
        out_specs=in_vmem(1)[0],
        compiler_params=params(),
        cost_estimate=cost(4e9),
    )(parts)


def perturb_kernel(state, mean, perturb):
    for pair in range(mean.shape[0]):
        for i in range(2):
            span = slice(i * K, (i + 1) * K)
            values = state[2 * pair + i].astype(F32)
            average = jnp.mean(values, axis=0, keepdims=True)
            mean[pair : pair + 1, span] = average
            perturb[pair, :, span] = (values - average).astype(BF16)


def perturbations(state):
    pairs = state.shape[0] // 2
    return pl.pallas_call(
        perturb_kernel,
        out_shape=[
            jax.ShapeDtypeStruct((pairs, 2 * K), F32),
            jax.ShapeDtypeStruct((pairs, K, 2 * K), BF16),
        ],
        in_specs=in_vmem(1),
        out_specs=in_vmem(2),
        compiler_params=params(),
        cost_estimate=cost(SHORT),
    )(state)


def column_coefs():
    lane = lax.broadcasted_iota(jnp.int32, (1, 2 * K), 1) % K
    position = (lane.astype(F32) + 0.5) / K
    return lane, jnp.maximum(0.5 - position, 0.0), jnp.maximum(position - 0.5, 0.0)


def own_kernel(own, mean, perturb, out):
    _, left_coef, right_coef = column_coefs()
    own_coef = 1.0 - left_coef - right_coef
    for pair in range(mean.shape[0]):
        sums = jnp.dot(own[...], perturb[pair], preferred_element_type=F32)
        out[pair] = mean[pair : pair + 1] + own_coef * sums


def own_part(own, mean, perturb):
    return pl.pallas_call(
        own_kernel,
        out_shape=jax.ShapeDtypeStruct(perturb.shape, F32),
        in_specs=in_vmem(3),
        out_specs=in_vmem(1)[0],
        compiler_params=params(),
        cost_estimate=cost(2e9),
    )(own, mean, perturb)


def side_kernel(left, right, part, perturb, out, held, sems):
    lane, left_coef, right_coef = column_coefs()
    coef = left_coef + right_coef
    weights = jnp.concatenate([left[...], right[...]], axis=0)
    chunks = sems.shape[0]
    pairs = perturb.shape[0] // chunks
    copies = []
    for chunk in range(chunks):
        for pair in range(chunk * pairs, (chunk + 1) * pairs):
            sums = jnp.dot(weights, perturb[pair], preferred_element_type=F32)
            side = jnp.where(lane < K // 2, sums[:K], sums[K:])
            total = (part[pair] + coef * side).astype(BF16)
            for i in range(2):
                held[2 * pair + i] = total[:, i * K : (i + 1) * K]
        rows = pl.ds(2 * chunk * pairs, 2 * pairs)
        copies.append(pltpu.make_async_copy(held.at[rows], out.at[rows], sems.at[chunk]))
        copies[-1].start()
    for copy in copies:
        copy.wait()


def add_sides(left, right, part, perturb):
    shape = (2 * perturb.shape[0], K, K)
    return pl.pallas_call(
        side_kernel,
        out_shape=jax.ShapeDtypeStruct(shape, BF16),
        in_specs=in_vmem(4),
        out_specs=pl.BlockSpec(memory_space=pltpu.HBM),
        scratch_shapes=[pltpu.VMEM(shape, BF16), pltpu.SemaphoreType.DMA((6,))],
        compiler_params=params(),
        cost_estimate=cost(2e9),
    )(left, right, part, perturb)


def on_device(departures, innovation, obs_weight, send_rows, send_counts, state):
    n_grid = lax.axis_size("grid")
    low_half, high_half, near = make_messages(
        departures, innovation, obs_weight, send_rows[0].T
    )
    left = hop(low_half, 0, 1, 0)
    right = hop(high_half, 0, -1, 0)
    other = hop(near, 0, 0, 1)

    whole = lambda which: ((0, which, 0), (1, which, HALF))
    found = pick_rows(
        ((whole(0), (0, 0, 8), None), (whole(1), (1, 0, 12), None)), SHORT, near, other
    )
    mean, perturb = perturbations(state)
    low_half, high_half, found, mean, perturb = lax.optimization_barrier(
        (low_half, high_half, found, mean, perturb)
    )
    left_more = hop(high_half, 0, 1, 0)
    right_more = hop(low_half, 0, -1, 0)
    left, right, found, mean, perturb = lax.optimization_barrier(
        (left, right, found, mean, perturb)
    )
    far_low, far_high = hop(left, 0, 1, 0), hop(right, 0, -1, 0)

    def firsts(core):
        row = 8 + 4 * core
        return (((0, 0, 0),), (0, 0, row), None), (((1, 1, 0),), (1, 0, row), None)

    def seconds(core):
        row = 8 + 4 * core
        return (((1, 2, 0),), (0, 0, row), 4), (((0, 3, 0),), (1, 0, row), 5)

    same = pick_rows(firsts(0), SHORT, left, right)
    left, right, same = lax.optimization_barrier((left, right, same))
    left_other, right_other = hop(left, 0, 0, 1), hop(right, 0, 0, 1)
    same = pick_rows(seconds(0), LONG, left, right, left_more, right_more, *same)
    left_more, right_more, same = lax.optimization_barrier((left_more, right_more, same))
    left_more_other, right_more_other = hop(left_more, 0, 0, 1), hop(right_more, 0, 0, 1)
    cross = pick_rows(firsts(1), LONG, left_other, right_other)
    cross = pick_rows(
        seconds(1), SHORT, left_other, right_other, left_more_other, right_more_other, *cross
    )
    far_low, far_high, cross = lax.optimization_barrier((far_low, far_high, cross))
    far_low_other, far_high_other = hop(far_low, 0, 0, 1), hop(far_high, 0, 0, 1)
    far = pick_rows(((((0, 0, 0), (1, 1, 0)), (0, 0, 4), None),), SHORT, far_low, far_high)[0]
    last = (far_low_other, far_high_other, far, *found, same[0], cross[0], same[1], cross[1])

    across = last_grams((2,), BF16, *last)[0]
    from_across = hop(across, 2, 0, 0)
    up, down = last_grams((1, 3), BF16, *last)
    from_up, from_down = hop(up, 1, 0, 0), hop(down, -1, 0, 0)
    own = last_grams((0,), F32, *last)[0]
    parts = sum_parts(own, from_across, from_up, from_down)
    parts = lax.all_to_all(parts, "obs", 0, 0, tiled=True)

    own = transposed_weights(parts)
    low = lax.ppermute(own, "grid", [(j, (j + 1) % n_grid) for j in range(n_grid)])
    high = lax.ppermute(own, "grid", [(j, (j - 1) % n_grid) for j in range(n_grid)])
    part = own_part(own, mean, perturb)
    return add_sides(low, high, part, perturb)


def solution(mesh):
    in_specs = (
        P(("obs", "grid"), None),
        P(("obs", "grid")),
        P(("obs", "grid")),
        P(("obs", "grid"), None, None),
        P(("obs", "grid"), None),
        P("obs", None, "grid"),
    )
    out_specs = P("obs", None, "grid")
    return jax.shard_map(
        on_device, mesh=mesh, in_specs=in_specs, out_specs=out_specs, check_vma=False
    )
```

```python
import functools

import jax
import jax.numpy as jnp
from jax import lax
from jax.experimental import pallas as pl
from jax.experimental.pallas import tpu as pltpu
from jax.sharding import PartitionSpec as P

ITERS = 6
Y, X, CORES = 4, 4, 2
F32, BF16 = jnp.float32, jnp.bfloat16
K = 128
LOW = 512
BLOCKS = 4
HALF = 2 * K + 16
PACK = 80
VMEM = 20 * 1024 * 1024


def params():
    return pltpu.CompilerParams(vmem_limit_bytes=VMEM)


LONG, SHORT = 6e10, 1e6


def cost(flops):
    return pl.CostEstimate(flops=int(flops), bytes_accessed=100_000, transcendentals=0)


def in_vmem(count):
    return [pl.BlockSpec(memory_space=pltpu.VMEM)] * count


def hop(value, dy, dx, dc):
    pairs = []
    for place in range(Y * X * CORES):
        y, x, c = place // (X * CORES), place // CORES % X, place % CORES
        pairs.append((place, ((y + dy) % Y * X + (x + dx) % X) * CORES + (c ^ dc)))
    return lax.ppermute(value, "grid", pairs)


def dims(m, n):
    return (((m,), (n,)), ((), ()))


def send_picks(turned, cx, swapped):
    lines = []
    for y in range(Y):
        rows = turned[pl.ds(y * X * CORES + cx, 8, stride=Y * X * CORES), :]
        pair = [rows[0:4], rows[4:8]]
        pairs = jnp.concatenate(pair[::-1] if swapped else pair, axis=1)
        fours = jnp.concatenate([pairs[0:2], pairs[2:4]], axis=1)
        lines.append(jnp.concatenate([fours[0:1], fours[1:2]], axis=1))
    picks = jnp.concatenate(lines, axis=0)
    power = jnp.maximum(lax.shift_right_arithmetic(picks, 7), 0)
    code = lax.shift_left(128 + jnp.bitwise_and(picks, 127), power)
    return jnp.where(picks >= 0, code, 0).astype(F32)


def read_picks(rows):
    left = rows.astype(F32)
    high = jnp.zeros_like(left)
    for step in (8, 4, 2, 1):
        large = left >= 128.0 * 2**step
        left = jnp.where(large, left * 0.5**step, left)
        high = jnp.where(large, high + step, high)
    return jnp.where(left > 0.0, left - 128.0 + 128.0 * high, -1.0).astype(jnp.int32)


def message_kernel(departures, innovation, obs_weight, send_rows, *refs):
    outs, (rows, innov, weight, picks, turned) = refs[:3], refs[3:8]
    built, (in_sems, out_sems) = refs[8:11], refs[11:]
    small = ((send_rows, picks), (obs_weight, weight), (innovation, innov))
    small = [pltpu.make_async_copy(*pair, in_sems.at[i]) for i, pair in enumerate(small)]
    large = []
    for block in range(BLOCKS):
        span = pl.ds(block * LOW, LOW)
        large.append(
            pltpu.make_async_copy(departures.at[span], rows.at[span], in_sems.at[3 + block])
        )
    for copy in small + large:
        copy.start()
    small[0].wait()
    grid = lax.axis_index("grid")
    x, c = lax.rem(lax.div(grid, CORES), X), lax.rem(grid, CORES)
    turned[...] = picks[...].T
    groups = []
    for dx in range(X):
        for dc in range(CORES):
            cx = lax.rem(x + dx, X) * CORES + lax.rem(c + dc, CORES)
            groups.append(send_picks(turned, cx, dc == 1))
    small[1].wait()
    small[2].wait()
    root = jnp.sqrt(weight[...].reshape(1, BLOCKS * LOW))
    scaled = innov[...].reshape(1, BLOCKS * LOW) * root
    blank = jnp.zeros((2, LOW), F32)
    both, out_both = built[2], outs[2]
    copies = []
    for half in range(2):
        one, out_one = built[half], outs[half]
        at = half * HALF
        innovs = []
        for block in range(2):
            start = (2 * half + block) * LOW
            span = slice(start, start + LOW)
            large[2 * half + block].wait()
            part = (rows[span, :].astype(F32).T * root[:, span]).astype(BF16)
            one[block * K : (block + 1) * K, :] = part
            both[at + block * K : at + (block + 1) * K, :] = part
            innovs.append(scaled[:, span])
        top = innovs + [blank, groups[4 + half]]
        next_one = groups[2:4] if half == 0 else groups[6:8]
        one[2 * K :, :] = jnp.concatenate(top + next_one, axis=0).astype(BF16)
        both[at + 2 * K : at + HALF, :] = jnp.concatenate(top + groups[0:2], axis=0).astype(BF16)
        copies.append(pltpu.make_async_copy(one, out_one, out_sems.at[half]))
        span = pl.ds(at, HALF)
        copies.append(
            pltpu.make_async_copy(both.at[span], out_both.at[span], out_sems.at[2 + half])
        )
        for copy in copies[-2:]:
            copy.start()
    for copy in copies:
        copy.wait()


def make_messages(*args):
    shapes = [(HALF, LOW), (HALF, LOW), (2 * HALF, LOW)]
    hbm = pl.BlockSpec(memory_space=pltpu.HBM)
    return pl.pallas_call(
        message_kernel,
        out_shape=[jax.ShapeDtypeStruct(shape, BF16) for shape in shapes],
        in_specs=[hbm] * 4,
        out_specs=[hbm] * 3,
        scratch_shapes=[pltpu.VMEM(arg.shape, arg.dtype) for arg in args]
        + [pltpu.VMEM(args[3].shape[::-1], jnp.int32)]
        + [pltpu.VMEM(shape, BF16) for shape in shapes]
        + [pltpu.SemaphoreType.DMA((3 + BLOCKS,)), pltpu.SemaphoreType.DMA((4,))],
        compiler_params=pltpu.CompilerParams(vmem_limit_bytes=60 * 1024 * 1024),
        cost_estimate=cost(2e9),
    )(*args)


def pick(parts, picks):
    high = lax.shift_right_arithmetic(picks, 9)
    first = parts[0][0]
    live = picks >= 0 if len(parts) == 2 else lax.shift_right_arithmetic(high, 1) == first
    low = jnp.where(live, jnp.bitwise_and(picks, LOW - 1), -1)
    place = lax.broadcasted_iota(jnp.int32, (LOW, 256), 0).astype(jnp.int16)
    low = jnp.broadcast_to(low, (LOW, 256)).astype(jnp.int16)
    one_hot = jnp.where(place == low, jnp.ones((), BF16), jnp.zeros((), BF16))
    blocks, innovs = [], []
    for _, rows in parts:
        found = jnp.dot(rows, one_hot, preferred_element_type=F32)
        blocks += [found[:K], found[K : 2 * K]]
        innovs += [found[2 * K : 2 * K + 1], found[2 * K + 1 : 2 * K + 2]]
    members, innov = blocks[0], innovs[0]
    for block in range(1, len(blocks)):
        here = high == 2 * first + block
        members = jnp.where(here, blocks[block], members)
        innov = jnp.where(here, innovs[block], innov)
    return jnp.concatenate([members, jnp.broadcast_to(innov, (16, 256))], axis=0).astype(BF16)


def tail_picks(ref, at, row):
    return read_picks(ref[at + 2 * K : at + HALF, :].astype(F32)[row : row + 4])


def pick_kernel(sources, count, *refs):
    outs = refs[count:]
    picks = [tail_picks(refs[which], at, row) for _, (which, at, row), _ in sources]
    for step in range(2 * Y):
        y, span = step // 2, slice(step % 2 * 256, step % 2 * 256 + 256)
        for out, (parts, _, before), values in zip(outs, sources, picks):
            tables = [(half, refs[which][at : at + HALF, :]) for half, which, at in parts]
            found = pick(tables, values[y : y + 1, span])
            out[step] = found if before is None else found + refs[before][step]


def pick_rows(sources, flops, *args):
    return pl.pallas_call(
        functools.partial(pick_kernel, sources, len(args)),
        out_shape=[jax.ShapeDtypeStruct((2 * Y, 144, 256), BF16)] * len(sources),
        in_specs=in_vmem(len(args)),
        out_specs=in_vmem(len(sources)),
        compiler_params=params(),
        cost_estimate=cost(flops),
    )(*args)


def join(first, second):
    low = lax.broadcasted_iota(jnp.int32, first.shape, 1) < K // 2
    return jnp.where(low, first, second), jnp.where(low, second, first)


def pack(total):
    row = lax.broadcasted_iota(jnp.int32, (64, K), 0)
    lane = lax.broadcasted_iota(jnp.int32, (64, K), 1)
    lower = total[64:K]
    upper = jnp.where(lane < row, pltpu.roll(lower, 64, 1), total[0:64])
    diagonal = jnp.sum(jnp.where(lane == row + 64, lower, 0.0), axis=0, keepdims=True)
    return upper, diagonal, total[K : K + 1]


def unpack(packed):
    row = lax.broadcasted_iota(jnp.int32, (64, K), 0)
    lane = lax.broadcasted_iota(jnp.int32, (64, K), 1)
    upper = packed[0:64]
    above = jnp.where(lane > row, upper, 0.0)
    below = pltpu.roll(jnp.where(lane < row, upper, 0.0), 64, 1)
    off = jnp.concatenate([above, below], axis=0)
    low = jnp.where(lane == row + 64, packed[64:65], 0.0)
    diagonal = jnp.concatenate([jnp.where(lane == row, upper, 0.0), low], axis=0)
    return off + off.T + diagonal, packed[65:66]


def last_kernel(shifts, low, high, same, *rest):
    found, outs, picks = rest[:6], rest[6:-1], rest[-1]
    place = lax.div(lax.axis_index("grid"), X * CORES)
    picks[...] = tail_picks(high, 0, 4)
    table = ((0, low[...]), (1, high[...]))
    for out, shift in zip(outs, shifts):
        y = lax.rem(place + shift, Y)
        tail_row = lax.broadcasted_iota(jnp.int32, (16, K), 0)
        tail = jnp.zeros((16, K), F32)
        for i in range(2):
            span = slice(i * 256, i * 256 + 256)
            last = pick(table, picks[pl.ds(y, 1), :][:, span])
            shards = [ref[2 * y + i] for ref in (*found, same)] + [last]
            for half in range(2):
                span = slice(half * K, half * K + K)
                pairs = [
                    join(shards[n][:, span], shards[n + 1][:, span])
                    for n in range(0, len(shards), 2)
                ]
                for side in range(2):
                    rows = jnp.concatenate([pair[side] for pair in pairs], axis=1)
                    total = lax.dot_general(rows, rows[:K], dims(1, 1), preferred_element_type=F32)
                    patch = i + 2 * half + 4 * side
                    upper, diagonal, pull = pack(total)
                    out[patch * 64 : patch * 64 + 64, :] = upper.astype(out.dtype)
                    tail = jnp.where(tail_row == 2 * patch, diagonal, tail)
                    tail = jnp.where(tail_row == 2 * patch + 1, pull, tail)
        out[8 * 64 :, :] = tail.astype(out.dtype)


def last_grams(shifts, dtype, *args):
    return pl.pallas_call(
        functools.partial(last_kernel, shifts),
        out_shape=[jax.ShapeDtypeStruct((8 * 64 + 16, K), dtype)] * len(shifts),
        in_specs=in_vmem(len(args)),
        out_specs=in_vmem(len(shifts)),
        scratch_shapes=[pltpu.VMEM((Y, LOW), jnp.int32)],
        compiler_params=params(),
        cost_estimate=cost(1e9 * len(shifts)),
    )(*args)


def sum_kernel(own, a, b, c, out):
    def total(span):
        return own[span, :] + (a[span, :].astype(F32) + b[span, :].astype(F32) + c[span, :].astype(F32))

    tails = total(slice(8 * 64, 8 * 64 + 16))
    first = lax.broadcasted_iota(jnp.int32, (16, K), 0) == 0
    for patch in range(8):
        out[patch, 0:64, :] = total(slice(patch * 64, patch * 64 + 64)).astype(BF16)
        tail = jnp.where(first, tails[2 * patch : 2 * patch + 1], tails[2 * patch + 1 : 2 * patch + 2])
        out[patch, 64:PACK, :] = tail.astype(BF16)


def sum_parts(*args):
    return pl.pallas_call(
        sum_kernel,
        out_shape=jax.ShapeDtypeStruct((8, PACK, K), BF16),
        in_specs=in_vmem(4),
        out_specs=in_vmem(1)[0],
        compiler_params=params(),
        cost_estimate=cost(5e8),
    )(*args)


def split(value):
    high = value.astype(BF16)
    return high, (value - high.astype(F32)).astype(BF16)


def product(left, right):
    lh, ll = split(left)
    rh, rl = split(right)
    return jnp.dot(
        jnp.concatenate([lh, lh, ll], axis=1),
        jnp.concatenate([rh, rl, rh], axis=0),
        preferred_element_type=F32,
    )


def weights_kernel(parts, out):
    gram, pull = unpack(jnp.sum(parts[...].astype(F32), axis=0))
    row = lax.broadcasted_iota(jnp.int32, (K, K), 0)
    col = lax.broadcasted_iota(jnp.int32, (K, K), 1)
    identity = (row == col).astype(F32)
    system = gram + (K - 1.0) * identity
    squares = jnp.sum(jnp.sum(system * system, axis=0, keepdims=True), axis=1, keepdims=True)
    frob = jnp.sqrt(squares)
    iterate = system / frob
    inverse = 1.5 * identity - 0.5 * iterate
    iterate = product(inverse, iterate)
    for sweep in range(1, ITERS):
        newton = 1.5 * identity - 0.5 * product(inverse, iterate)
        if sweep < ITERS - 1:
            both = product(newton, jnp.concatenate([iterate, inverse], axis=1))
            iterate, inverse = both[:, :K], both[:, K:]
        else:
            shift = product(product(jnp.broadcast_to(pull, (16, K)), inverse), inverse)
            shift = product(product(shift, newton), newton)[0:1] / frob
            inverse = product(newton, inverse)
    out[...] = (jnp.sqrt((K - 1.0) / frob) * inverse.T + shift).astype(BF16)


def transposed_weights(parts):
    return pl.pallas_call(
        weights_kernel,
        out_shape=jax.ShapeDtypeStruct((K, K), BF16),
        in_specs=in_vmem(1),
        out_specs=in_vmem(1)[0],
        compiler_params=params(),
        cost_estimate=cost(4e9),
    )(parts)


def perturb_kernel(state, mean, perturb):
    for pair in range(mean.shape[0]):
        for i in range(2):
            span = slice(i * K, (i + 1) * K)
            values = state[2 * pair + i].astype(F32)
            average = jnp.mean(values, axis=0, keepdims=True)
            mean[pair : pair + 1, span] = average
            perturb[pair, :, span] = (values - average).astype(BF16)


def perturbations(state):
    pairs = state.shape[0] // 2
    return pl.pallas_call(
        perturb_kernel,
        out_shape=[
            jax.ShapeDtypeStruct((pairs, 2 * K), F32),
            jax.ShapeDtypeStruct((pairs, K, 2 * K), BF16),
        ],
        in_specs=in_vmem(1),
        out_specs=in_vmem(2),
        compiler_params=params(),
        cost_estimate=cost(LONG),
    )(state)


def column_coefs():
    lane = lax.broadcasted_iota(jnp.int32, (1, 2 * K), 1) % K
    position = (lane.astype(F32) + 0.5) / K
    return lane, jnp.maximum(0.5 - position, 0.0), jnp.maximum(position - 0.5, 0.0)


def own_kernel(own, mean, perturb, out):
    _, left_coef, right_coef = column_coefs()
    own_coef = 1.0 - left_coef - right_coef
    for pair in range(mean.shape[0]):
        sums = jnp.dot(own[...], perturb[pair], preferred_element_type=F32)
        out[pair] = mean[pair : pair + 1] + own_coef * sums


def own_part(own, mean, perturb):
    return pl.pallas_call(
        own_kernel,
        out_shape=jax.ShapeDtypeStruct(perturb.shape, F32),
        in_specs=in_vmem(3),
        out_specs=in_vmem(1)[0],
        compiler_params=params(),
        cost_estimate=cost(2e9),
    )(own, mean, perturb)


def side_kernel(left, right, part, perturb, out, held, sems):
    lane, left_coef, right_coef = column_coefs()
    coef = left_coef + right_coef
    weights = jnp.concatenate([left[...], right[...]], axis=0)
    chunks = sems.shape[0]
    pairs = perturb.shape[0] // chunks
    copies = []
    for chunk in range(chunks):
        for pair in range(chunk * pairs, (chunk + 1) * pairs):
            sums = jnp.dot(weights, perturb[pair], preferred_element_type=F32)
            side = jnp.where(lane < K // 2, sums[:K], sums[K:])
            total = (part[pair] + coef * side).astype(BF16)
            for i in range(2):
                held[2 * pair + i] = total[:, i * K : (i + 1) * K]
        rows = pl.ds(2 * chunk * pairs, 2 * pairs)
        copies.append(pltpu.make_async_copy(held.at[rows], out.at[rows], sems.at[chunk]))
        copies[-1].start()
    for copy in copies:
        copy.wait()


def add_sides(left, right, part, perturb):
    shape = (2 * perturb.shape[0], K, K)
    return pl.pallas_call(
        side_kernel,
        out_shape=jax.ShapeDtypeStruct(shape, BF16),
        in_specs=in_vmem(4),
        out_specs=pl.BlockSpec(memory_space=pltpu.HBM),
        scratch_shapes=[pltpu.VMEM(shape, BF16), pltpu.SemaphoreType.DMA((6,))],
        compiler_params=params(),
        cost_estimate=cost(2e9),
    )(left, right, part, perturb)


def on_device(departures, innovation, obs_weight, send_rows, send_counts, state):
    n_grid = lax.axis_size("grid")
    low_half, high_half, near = make_messages(
        departures, innovation, obs_weight, send_rows[0].T
    )
    left = hop(low_half, 0, 1, 0)
    right = hop(high_half, 0, -1, 0)
    other = hop(near, 0, 0, 1)

    whole = lambda which: ((0, which, 0), (1, which, HALF))
    found = pick_rows(
        ((whole(0), (0, 0, 8), None), (whole(1), (1, 0, 12), None)), SHORT, near, other
    )
    mean, perturb = perturbations(state)
    low_half, high_half, found, mean, perturb = lax.optimization_barrier(
        (low_half, high_half, found, mean, perturb)
    )
    left_more = hop(high_half, 0, 1, 0)
    right_more = hop(low_half, 0, -1, 0)
    left, right, found, mean, perturb = lax.optimization_barrier(
        (left, right, found, mean, perturb)
    )
    far_low, far_high = hop(left, 0, 1, 0), hop(right, 0, -1, 0)

    def firsts(core):
        row = 8 + 4 * core
        return (((0, 0, 0),), (0, 0, row), None), (((1, 1, 0),), (1, 0, row), None)

    def seconds(core):
        row = 8 + 4 * core
        return (((1, 2, 0),), (0, 0, row), 4), (((0, 3, 0),), (1, 0, row), 5)

    same = pick_rows(firsts(0), SHORT, left, right)
    left, right, same = lax.optimization_barrier((left, right, same))
    left_other, right_other = hop(left, 0, 0, 1), hop(right, 0, 0, 1)
    same = pick_rows(seconds(0), LONG, left, right, left_more, right_more, *same)
    left_more, right_more, same = lax.optimization_barrier((left_more, right_more, same))
    left_more_other, right_more_other = hop(left_more, 0, 0, 1), hop(right_more, 0, 0, 1)
    cross = pick_rows(firsts(1), LONG, left_other, right_other)
    cross = pick_rows(
        seconds(1), SHORT, left_other, right_other, left_more_other, right_more_other, *cross
    )
    far_low, far_high, cross = lax.optimization_barrier((far_low, far_high, cross))
    far_low_other, far_high_other = hop(far_low, 0, 0, 1), hop(far_high, 0, 0, 1)
    far = pick_rows(((((0, 0, 0), (1, 1, 0)), (0, 0, 4), None),), SHORT, far_low, far_high)[0]
    last = (far_low_other, far_high_other, far, *found, same[0], cross[0], same[1], cross[1])

    across = last_grams((2,), BF16, *last)[0]
    from_across = hop(across, 2, 0, 0)
    up, down = last_grams((1, 3), BF16, *last)
    from_up, from_down = hop(up, 1, 0, 0), hop(down, -1, 0, 0)
    own = last_grams((0,), F32, *last)[0]
    parts = sum_parts(own, from_across, from_up, from_down)
    parts = lax.all_to_all(parts, "obs", 0, 0, tiled=True)

    own = transposed_weights(parts)
    low = lax.ppermute(own, "grid", [(j, (j + 1) % n_grid) for j in range(n_grid)])
    high = lax.ppermute(own, "grid", [(j, (j - 1) % n_grid) for j in range(n_grid)])
    part = own_part(own, mean, perturb)
    return add_sides(low, high, part, perturb)


def solution(mesh):
    in_specs = (
        P(("obs", "grid"), None),
        P(("obs", "grid")),
        P(("obs", "grid")),
        P(("obs", "grid"), None, None),
        P(("obs", "grid"), None),
        P("obs", None, "grid"),
    )
    out_specs = P("obs", None, "grid")
    return jax.shard_map(
        on_device, mesh=mesh, in_specs=in_specs, out_specs=out_specs, check_vma=False
    )
```

```python
import functools

import jax
import jax.numpy as jnp
from jax import lax
from jax.experimental import pallas as pl
from jax.experimental.pallas import tpu as pltpu
from jax.sharding import PartitionSpec as P

ITERS = 6
Y, X, CORES = 4, 4, 2
F32, BF16 = jnp.float32, jnp.bfloat16
K = 128
LOW = 512
BLOCKS = 4
HALF = 2 * K + 16
PACK = 80
VMEM = 20 * 1024 * 1024


def params():
    return pltpu.CompilerParams(vmem_limit_bytes=VMEM)


LONG, SHORT = 6e10, 1e6


def cost(flops):
    return pl.CostEstimate(flops=int(flops), bytes_accessed=100_000, transcendentals=0)


def in_vmem(count):
    return [pl.BlockSpec(memory_space=pltpu.VMEM)] * count


def hop(value, dy, dx, dc):
    pairs = []
    for place in range(Y * X * CORES):
        y, x, c = place // (X * CORES), place // CORES % X, place % CORES
        pairs.append((place, ((y + dy) % Y * X + (x + dx) % X) * CORES + (c ^ dc)))
    return lax.ppermute(value, "grid", pairs)


def dims(m, n):
    return (((m,), (n,)), ((), ()))


def send_picks(turned, cx, swapped):
    lines = []
    for y in range(Y):
        rows = turned[pl.ds(y * X * CORES + cx, 8, stride=Y * X * CORES), :]
        pair = [rows[0:4], rows[4:8]]
        pairs = jnp.concatenate(pair[::-1] if swapped else pair, axis=1)
        fours = jnp.concatenate([pairs[0:2], pairs[2:4]], axis=1)
        lines.append(jnp.concatenate([fours[0:1], fours[1:2]], axis=1))
    picks = jnp.concatenate(lines, axis=0)
    power = jnp.maximum(lax.shift_right_arithmetic(picks, 7), 0)
    code = lax.shift_left(128 + jnp.bitwise_and(picks, 127), power)
    return jnp.where(picks >= 0, code, 0).astype(F32)


def read_picks(rows):
    left = rows.astype(F32)
    high = jnp.zeros_like(left)
    for step in (8, 4, 2, 1):
        large = left >= 128.0 * 2**step
        left = jnp.where(large, left * 0.5**step, left)
        high = jnp.where(large, high + step, high)
    return jnp.where(left > 0.0, left - 128.0 + 128.0 * high, -1.0).astype(jnp.int32)


def message_kernel(departures, innovation, obs_weight, send_rows, *refs):
    outs, (rows, innov, weight, picks, turned) = refs[:3], refs[3:8]
    built, in_sems = outs, refs[8]
    small = ((send_rows, picks), (obs_weight, weight), (innovation, innov))
    small = [pltpu.make_async_copy(*pair, in_sems.at[i]) for i, pair in enumerate(small)]
    large = []
    for block in range(BLOCKS):
        span = pl.ds(block * LOW, LOW)
        large.append(
            pltpu.make_async_copy(departures.at[span], rows.at[span], in_sems.at[3 + block])
        )
    for copy in small + large:
        copy.start()
    small[0].wait()
    grid = lax.axis_index("grid")
    x, c = lax.rem(lax.div(grid, CORES), X), lax.rem(grid, CORES)
    turned[...] = picks[...].T
    groups = []
    for dx in range(X):
        for dc in range(CORES):
            cx = lax.rem(x + dx, X) * CORES + lax.rem(c + dc, CORES)
            groups.append(send_picks(turned, cx, dc == 1))
    small[1].wait()
    small[2].wait()
    root = jnp.sqrt(weight[...].reshape(1, BLOCKS * LOW))
    scaled = innov[...].reshape(1, BLOCKS * LOW) * root
    blank = jnp.zeros((2, LOW), F32)
    both = built[2]
    for half in range(2):
        one = built[half]
        at = half * HALF
        innovs = []
        for block in range(2):
            start = (2 * half + block) * LOW
            span = slice(start, start + LOW)
            large[2 * half + block].wait()
            part = (rows[span, :].astype(F32).T * root[:, span]).astype(BF16)
            one[block * K : (block + 1) * K, :] = part
            both[at + block * K : at + (block + 1) * K, :] = part
            innovs.append(scaled[:, span])
        top = innovs + [blank, groups[4 + half]]
        next_one = groups[2:4] if half == 0 else groups[6:8]
        one[2 * K :, :] = jnp.concatenate(top + next_one, axis=0).astype(BF16)
        both[at + 2 * K : at + HALF, :] = jnp.concatenate(top + groups[0:2], axis=0).astype(BF16)


def make_messages(*args):
    shapes = [(HALF, LOW), (HALF, LOW), (2 * HALF, LOW)]
    hbm = pl.BlockSpec(memory_space=pltpu.HBM)
    return pl.pallas_call(
        message_kernel,
        out_shape=[jax.ShapeDtypeStruct(shape, BF16) for shape in shapes],
        in_specs=[hbm] * 4,
        out_specs=in_vmem(3),
        scratch_shapes=[pltpu.VMEM(arg.shape, arg.dtype) for arg in args]
        + [pltpu.VMEM(args[3].shape[::-1], jnp.int32)]
        + [pltpu.SemaphoreType.DMA((3 + BLOCKS,))],
        compiler_params=pltpu.CompilerParams(vmem_limit_bytes=VMEM),
        cost_estimate=cost(2e9),
    )(*[pltpu.with_memory_space_constraint(arg, pltpu.HBM) for arg in args])


def pick(parts, picks):
    high = lax.shift_right_arithmetic(picks, 9)
    first = parts[0][0]
    live = picks >= 0 if len(parts) == 2 else lax.shift_right_arithmetic(high, 1) == first
    low = jnp.where(live, jnp.bitwise_and(picks, LOW - 1), -1)
    place = lax.broadcasted_iota(jnp.int32, (LOW, 256), 0).astype(jnp.int16)
    low = jnp.broadcast_to(low, (LOW, 256)).astype(jnp.int16)
    one_hot = jnp.where(place == low, jnp.ones((), BF16), jnp.zeros((), BF16))
    blocks, innovs = [], []
    for _, rows in parts:
        found = jnp.dot(rows, one_hot, preferred_element_type=F32)
        blocks += [found[:K], found[K : 2 * K]]
        innovs += [found[2 * K : 2 * K + 1], found[2 * K + 1 : 2 * K + 2]]
    members, innov = blocks[0], innovs[0]
    for block in range(1, len(blocks)):
        here = high == 2 * first + block
        members = jnp.where(here, blocks[block], members)
        innov = jnp.where(here, innovs[block], innov)
    return jnp.concatenate([members, jnp.broadcast_to(innov, (16, 256))], axis=0).astype(BF16)


def tail_picks(ref, at, row):
    return read_picks(ref[at + 2 * K : at + HALF, :].astype(F32)[row : row + 4])


def pick_kernel(sources, count, *refs):
    outs = refs[count:]
    picks = [tail_picks(refs[which], at, row) for _, (which, at, row), _ in sources]
    for step in range(2 * Y):
        y, span = step // 2, slice(step % 2 * 256, step % 2 * 256 + 256)
        for out, (parts, _, before), values in zip(outs, sources, picks):
            tables = [(half, refs[which][at : at + HALF, :]) for half, which, at in parts]
            found = pick(tables, values[y : y + 1, span])
            out[step] = found if before is None else found + refs[before][step]


def pick_rows(sources, flops, *args):
    return pl.pallas_call(
        functools.partial(pick_kernel, sources, len(args)),
        out_shape=[jax.ShapeDtypeStruct((2 * Y, 144, 256), BF16)] * len(sources),
        in_specs=in_vmem(len(args)),
        out_specs=in_vmem(len(sources)),
        compiler_params=params(),
        cost_estimate=cost(flops),
    )(*args)


def join(first, second):
    low = lax.broadcasted_iota(jnp.int32, first.shape, 1) < K // 2
    return jnp.where(low, first, second), jnp.where(low, second, first)


def pack(total):
    row = lax.broadcasted_iota(jnp.int32, (64, K), 0)
    lane = lax.broadcasted_iota(jnp.int32, (64, K), 1)
    lower = total[64:K]
    upper = jnp.where(lane < row, pltpu.roll(lower, 64, 1), total[0:64])
    diagonal = jnp.sum(jnp.where(lane == row + 64, lower, 0.0), axis=0, keepdims=True)
    return upper, diagonal, total[K : K + 1]


def unpack(packed):
    row = lax.broadcasted_iota(jnp.int32, (64, K), 0)
    lane = lax.broadcasted_iota(jnp.int32, (64, K), 1)
    upper = packed[0:64]
    above = jnp.where(lane > row, upper, 0.0)
    below = pltpu.roll(jnp.where(lane < row, upper, 0.0), 64, 1)
    off = jnp.concatenate([above, below], axis=0)
    low = jnp.where(lane == row + 64, packed[64:65], 0.0)
    diagonal = jnp.concatenate([jnp.where(lane == row, upper, 0.0), low], axis=0)
    return off + off.T + diagonal, packed[65:66]


def last_kernel(shifts, low, high, same, *rest):
    found, outs, picks = rest[:6], rest[6:-1], rest[-1]
    place = lax.div(lax.axis_index("grid"), X * CORES)
    picks[...] = tail_picks(high, 0, 4)
    table = ((0, low[...]), (1, high[...]))
    for out, shift in zip(outs, shifts):
        y = lax.rem(place + shift, Y)
        tail_row = lax.broadcasted_iota(jnp.int32, (16, K), 0)
        tail = jnp.zeros((16, K), F32)
        for i in range(2):
            span = slice(i * 256, i * 256 + 256)
            last = pick(table, picks[pl.ds(y, 1), :][:, span])
            shards = [ref[2 * y + i] for ref in (*found, same)] + [last]
            for half in range(2):
                span = slice(half * K, half * K + K)
                pairs = [
                    join(shards[n][:, span], shards[n + 1][:, span])
                    for n in range(0, len(shards), 2)
                ]
                for side in range(2):
                    rows = jnp.concatenate([pair[side] for pair in pairs], axis=1)
                    total = lax.dot_general(rows, rows[:K], dims(1, 1), preferred_element_type=F32)
                    patch = i + 2 * half + 4 * side
                    upper, diagonal, pull = pack(total)
                    out[patch * 64 : patch * 64 + 64, :] = upper.astype(out.dtype)
                    tail = jnp.where(tail_row == 2 * patch, diagonal, tail)
                    tail = jnp.where(tail_row == 2 * patch + 1, pull, tail)
        out[8 * 64 :, :] = tail.astype(out.dtype)


def last_grams(shifts, dtype, *args):
    return pl.pallas_call(
        functools.partial(last_kernel, shifts),
        out_shape=[jax.ShapeDtypeStruct((8 * 64 + 16, K), dtype)] * len(shifts),
        in_specs=in_vmem(len(args)),
        out_specs=in_vmem(len(shifts)),
        scratch_shapes=[pltpu.VMEM((Y, LOW), jnp.int32)],
        compiler_params=params(),
        cost_estimate=cost(1e9 * len(shifts)),
    )(*args)


def sum_kernel(own, a, b, c, out):
    def total(span):
        return own[span, :] + (a[span, :].astype(F32) + b[span, :].astype(F32) + c[span, :].astype(F32))

    tails = total(slice(8 * 64, 8 * 64 + 16))
    first = lax.broadcasted_iota(jnp.int32, (16, K), 0) == 0
    for patch in range(8):
        out[patch, 0:64, :] = total(slice(patch * 64, patch * 64 + 64)).astype(BF16)
        tail = jnp.where(first, tails[2 * patch : 2 * patch + 1], tails[2 * patch + 1 : 2 * patch + 2])
        out[patch, 64:PACK, :] = tail.astype(BF16)


def sum_parts(*args):
    return pl.pallas_call(
        sum_kernel,
        out_shape=jax.ShapeDtypeStruct((8, PACK, K), BF16),
        in_specs=in_vmem(4),
        out_specs=in_vmem(1)[0],
        compiler_params=params(),
        cost_estimate=cost(5e8),
    )(*args)


def split(value):
    high = value.astype(BF16)
    return high, (value - high.astype(F32)).astype(BF16)


def product(left, right):
    lh, ll = split(left)
    rh, rl = split(right)
    return jnp.dot(
        jnp.concatenate([lh, lh, ll], axis=1),
        jnp.concatenate([rh, rl, rh], axis=0),
        preferred_element_type=F32,
    )


def weights_kernel(parts, out):
    gram, pull = unpack(jnp.sum(parts[...].astype(F32), axis=0))
    row = lax.broadcasted_iota(jnp.int32, (K, K), 0)
    col = lax.broadcasted_iota(jnp.int32, (K, K), 1)
    identity = (row == col).astype(F32)
    system = gram + (K - 1.0) * identity
    squares = jnp.sum(jnp.sum(system * system, axis=0, keepdims=True), axis=1, keepdims=True)
    frob = jnp.sqrt(squares)
    iterate = system / frob
    inverse = 1.5 * identity - 0.5 * iterate
    iterate = product(inverse, iterate)
    for sweep in range(1, ITERS):
        newton = 1.5 * identity - 0.5 * product(inverse, iterate)
        if sweep < ITERS - 1:
            both = product(newton, jnp.concatenate([iterate, inverse], axis=1))
            iterate, inverse = both[:, :K], both[:, K:]
        else:
            inverse = product(newton, inverse)
    shift = product(product(jnp.broadcast_to(pull, (16, K)), inverse), inverse)[0:1] / frob
    out[...] = (jnp.sqrt((K - 1.0) / frob) * inverse.T + shift).astype(BF16)


def transposed_weights(parts):
    return pl.pallas_call(
        weights_kernel,
        out_shape=jax.ShapeDtypeStruct((K, K), BF16),
        in_specs=in_vmem(1),
        out_specs=in_vmem(1)[0],
        compiler_params=params(),
        cost_estimate=cost(4e9),
    )(parts)


def perturb_kernel(state, mean, perturb):
    for pair in range(mean.shape[0]):
        for i in range(2):
            span = slice(i * K, (i + 1) * K)
            values = state[2 * pair + i].astype(F32)
            average = jnp.mean(values, axis=0, keepdims=True)
            mean[pair : pair + 1, span] = average
            perturb[pair, :, span] = (values - average).astype(BF16)


def perturbations(state):
    pairs = state.shape[0] // 2
    return pl.pallas_call(
        perturb_kernel,
        out_shape=[
            jax.ShapeDtypeStruct((pairs, 2 * K), F32),
            jax.ShapeDtypeStruct((pairs, K, 2 * K), BF16),
        ],
        in_specs=in_vmem(1),
        out_specs=in_vmem(2),
        compiler_params=params(),
        cost_estimate=cost(LONG),
    )(state)


def column_coefs():
    lane = lax.broadcasted_iota(jnp.int32, (1, 2 * K), 1) % K
    position = (lane.astype(F32) + 0.5) / K
    return lane, jnp.maximum(0.5 - position, 0.0), jnp.maximum(position - 0.5, 0.0)


def own_kernel(own, mean, perturb, out):
    _, left_coef, right_coef = column_coefs()
    own_coef = 1.0 - left_coef - right_coef
    for pair in range(mean.shape[0]):
        sums = jnp.dot(own[...], perturb[pair], preferred_element_type=F32)
        out[pair] = mean[pair : pair + 1] + own_coef * sums


def own_part(own, mean, perturb):
    return pl.pallas_call(
        own_kernel,
        out_shape=jax.ShapeDtypeStruct(perturb.shape, F32),
        in_specs=in_vmem(3),
        out_specs=in_vmem(1)[0],
        compiler_params=params(),
        cost_estimate=cost(2e9),
    )(own, mean, perturb)


def side_kernel(left, right, part, perturb, out, held, sems):
    lane, left_coef, right_coef = column_coefs()
    coef = left_coef + right_coef
    weights = jnp.concatenate([left[...], right[...]], axis=0)
    chunks = sems.shape[0]
    pairs = perturb.shape[0] // chunks
    copies = []
    for chunk in range(chunks):
        for pair in range(chunk * pairs, (chunk + 1) * pairs):
            sums = jnp.dot(weights, perturb[pair], preferred_element_type=F32)
            side = jnp.where(lane < K // 2, sums[:K], sums[K:])
            total = (part[pair] + coef * side).astype(BF16)
            for i in range(2):
                held[2 * pair + i] = total[:, i * K : (i + 1) * K]
        rows = pl.ds(2 * chunk * pairs, 2 * pairs)
        copies.append(pltpu.make_async_copy(held.at[rows], out.at[rows], sems.at[chunk]))
        copies[-1].start()
    for copy in copies:
        copy.wait()


def add_sides(left, right, part, perturb):
    shape = (2 * perturb.shape[0], K, K)
    return pl.pallas_call(
        side_kernel,
        out_shape=jax.ShapeDtypeStruct(shape, BF16),
        in_specs=in_vmem(4),
        out_specs=pl.BlockSpec(memory_space=pltpu.HBM),
        scratch_shapes=[pltpu.VMEM(shape, BF16), pltpu.SemaphoreType.DMA((6,))],
        compiler_params=params(),
        cost_estimate=cost(2e9),
    )(left, right, part, perturb)


def on_device(departures, innovation, obs_weight, send_rows, send_counts, state):
    n_grid = lax.axis_size("grid")
    low_half, high_half, near = make_messages(
        departures, innovation, obs_weight, send_rows[0].T
    )
    left = hop(low_half, 0, 1, 0)
    right = hop(high_half, 0, -1, 0)
    other = hop(near, 0, 0, 1)

    whole = lambda which: ((0, which, 0), (1, which, HALF))
    found = pick_rows(
        ((whole(0), (0, 0, 8), None), (whole(1), (1, 0, 12), None)), SHORT, near, other
    )
    mean, perturb = perturbations(state)
    low_half, high_half, mean, perturb = lax.optimization_barrier(
        (low_half, high_half, mean, perturb)
    )
    left_more = hop(high_half, 0, 1, 0)
    right_more = hop(low_half, 0, -1, 0)
    left, right, found, mean, perturb = lax.optimization_barrier(
        (left, right, found, mean, perturb)
    )
    far_low, far_high = hop(left, 0, 1, 0), hop(right, 0, -1, 0)

    def firsts(core):
        row = 8 + 4 * core
        return (((0, 0, 0),), (0, 0, row), None), (((1, 1, 0),), (1, 0, row), None)

    def seconds(core):
        row = 8 + 4 * core
        return (((1, 2, 0),), (0, 0, row), 4), (((0, 3, 0),), (1, 0, row), 5)

    same = pick_rows(firsts(0), SHORT, left, right)
    left, right, same = lax.optimization_barrier((left, right, same))
    left_other, right_other = hop(left, 0, 0, 1), hop(right, 0, 0, 1)
    same = pick_rows(seconds(0), LONG, left, right, left_more, right_more, *same)
    left_more, right_more, same = lax.optimization_barrier((left_more, right_more, same))
    left_more_other, right_more_other = hop(left_more, 0, 0, 1), hop(right_more, 0, 0, 1)
    cross = pick_rows(firsts(1), LONG, left_other, right_other)
    cross = pick_rows(
        seconds(1), SHORT, left_other, right_other, left_more_other, right_more_other, *cross
    )
    far_low, far_high, cross = lax.optimization_barrier((far_low, far_high, cross))
    far_low_other, far_high_other = hop(far_low, 0, 0, 1), hop(far_high, 0, 0, 1)
    far = pick_rows(((((0, 0, 0), (1, 1, 0)), (0, 0, 4), None),), SHORT, far_low, far_high)[0]
    last = (far_low_other, far_high_other, far, *found, same[0], cross[0], same[1], cross[1])

    across = last_grams((2,), BF16, *last)[0]
    from_across = hop(across, 2, 0, 0)
    up, down = last_grams((1, 3), BF16, *last)
    from_up, from_down = hop(up, 1, 0, 0), hop(down, -1, 0, 0)
    own = last_grams((0,), F32, *last)[0]
    parts = sum_parts(own, from_across, from_up, from_down)
    parts = lax.all_to_all(parts, "obs", 0, 0, tiled=True)

    own = transposed_weights(parts)
    low = lax.ppermute(own, "grid", [(j, (j + 1) % n_grid) for j in range(n_grid)])
    high = lax.ppermute(own, "grid", [(j, (j - 1) % n_grid) for j in range(n_grid)])
    part = own_part(own, mean, perturb)
    return add_sides(low, high, part, perturb)


def solution(mesh):
    in_specs = (
        P(("obs", "grid"), None),
        P(("obs", "grid")),
        P(("obs", "grid")),
        P(("obs", "grid"), None, None),
        P(("obs", "grid"), None),
        P("obs", None, "grid"),
    )
    out_specs = P("obs", None, "grid")
    return jax.shard_map(
        on_device, mesh=mesh, in_specs=in_specs, out_specs=out_specs, check_vma=False
    )
```

```python
import functools

import jax
import jax.numpy as jnp
from jax import lax
from jax.experimental import pallas as pl
from jax.experimental.pallas import tpu as pltpu
from jax.sharding import PartitionSpec as P

ITERS = 6
Y, X, CORES = 4, 4, 2
F32, BF16 = jnp.float32, jnp.bfloat16
K = 128
LOW = 512
BLOCKS = 4
HALF = 2 * K + 16
PACK = 80
VMEM = 20 * 1024 * 1024


def params():
    return pltpu.CompilerParams(vmem_limit_bytes=VMEM)


LONG, SHORT = 6e10, 1e6


def cost(flops):
    return pl.CostEstimate(flops=int(flops), bytes_accessed=100_000, transcendentals=0)


def in_vmem(count):
    return [pl.BlockSpec(memory_space=pltpu.VMEM)] * count


def hop(value, dy, dx, dc):
    pairs = []
    for place in range(Y * X * CORES):
        y, x, c = place // (X * CORES), place // CORES % X, place % CORES
        pairs.append((place, ((y + dy) % Y * X + (x + dx) % X) * CORES + (c ^ dc)))
    return lax.ppermute(value, "grid", pairs)


def dims(m, n):
    return (((m,), (n,)), ((), ()))


def send_picks(turned, cx, swapped):
    lines = []
    for y in range(Y):
        rows = turned[pl.ds(y * X * CORES + cx, 8, stride=Y * X * CORES), :]
        pair = [rows[0:4], rows[4:8]]
        pairs = jnp.concatenate(pair[::-1] if swapped else pair, axis=1)
        fours = jnp.concatenate([pairs[0:2], pairs[2:4]], axis=1)
        lines.append(jnp.concatenate([fours[0:1], fours[1:2]], axis=1))
    picks = jnp.concatenate(lines, axis=0)
    power = jnp.maximum(lax.shift_right_arithmetic(picks, 7), 0)
    code = lax.shift_left(128 + jnp.bitwise_and(picks, 127), power)
    return jnp.where(picks >= 0, code, 0).astype(F32)


def read_picks(rows):
    left = rows.astype(F32)
    high = jnp.zeros_like(left)
    for step in (8, 4, 2, 1):
        large = left >= 128.0 * 2**step
        left = jnp.where(large, left * 0.5**step, left)
        high = jnp.where(large, high + step, high)
    return jnp.where(left > 0.0, left - 128.0 + 128.0 * high, -1.0).astype(jnp.int32)


def message_kernel(departures, innovation, obs_weight, send_rows, *refs):
    outs, (rows, innov, weight, picks, turned) = refs[:3], refs[3:8]
    built, in_sems = outs, refs[8]
    small = ((send_rows, picks), (obs_weight, weight), (innovation, innov))
    small = [pltpu.make_async_copy(*pair, in_sems.at[i]) for i, pair in enumerate(small)]
    large = []
    for block in range(BLOCKS):
        span = pl.ds(block * LOW, LOW)
        large.append(
            pltpu.make_async_copy(departures.at[span], rows.at[span], in_sems.at[3 + block])
        )
    for copy in small + large:
        copy.start()
    small[0].wait()
    grid = lax.axis_index("grid")
    x, c = lax.rem(lax.div(grid, CORES), X), lax.rem(grid, CORES)
    turned[...] = picks[...].T
    groups = []
    for dx in range(X):
        for dc in range(CORES):
            cx = lax.rem(x + dx, X) * CORES + lax.rem(c + dc, CORES)
            groups.append(send_picks(turned, cx, dc == 1))
    small[1].wait()
    small[2].wait()
    root = jnp.sqrt(weight[...].reshape(1, BLOCKS * LOW))
    scaled = innov[...].reshape(1, BLOCKS * LOW) * root
    blank = jnp.zeros((2, LOW), F32)
    both = built[2]
    for half in range(2):
        one = built[half]
        at = half * HALF
        innovs = []
        for block in range(2):
            start = (2 * half + block) * LOW
            span = slice(start, start + LOW)
            large[2 * half + block].wait()
            part = (rows[span, :].astype(F32).T * root[:, span]).astype(BF16)
            one[block * K : (block + 1) * K, :] = part
            both[at + block * K : at + (block + 1) * K, :] = part
            innovs.append(scaled[:, span])
        top = innovs + [blank, groups[4 + half]]
        next_one = groups[2:4] if half == 0 else groups[6:8]
        one[2 * K :, :] = jnp.concatenate(top + next_one, axis=0).astype(BF16)
        both[at + 2 * K : at + HALF, :] = jnp.concatenate(top + groups[0:2], axis=0).astype(BF16)


def make_messages(*args):
    shapes = [(HALF, LOW), (HALF, LOW), (2 * HALF, LOW)]
    hbm = pl.BlockSpec(memory_space=pltpu.HBM)
    return pl.pallas_call(
        message_kernel,
        out_shape=[jax.ShapeDtypeStruct(shape, BF16) for shape in shapes],
        in_specs=[hbm] * 4,
        out_specs=in_vmem(3),
        scratch_shapes=[pltpu.VMEM(arg.shape, arg.dtype) for arg in args]
        + [pltpu.VMEM(args[3].shape[::-1], jnp.int32)]
        + [pltpu.SemaphoreType.DMA((3 + BLOCKS,))],
        compiler_params=pltpu.CompilerParams(vmem_limit_bytes=VMEM),
        cost_estimate=cost(2e9),
    )(*[pltpu.with_memory_space_constraint(arg, pltpu.HBM) for arg in args])


def pick(parts, picks):
    high = lax.shift_right_arithmetic(picks, 9)
    first = parts[0][0]
    live = picks >= 0 if len(parts) == 2 else lax.shift_right_arithmetic(high, 1) == first
    low = jnp.where(live, jnp.bitwise_and(picks, LOW - 1), -1)
    place = lax.broadcasted_iota(jnp.int32, (LOW, 256), 0).astype(jnp.int16)
    low = jnp.broadcast_to(low, (LOW, 256)).astype(jnp.int16)
    one_hot = jnp.where(place == low, jnp.ones((), BF16), jnp.zeros((), BF16))
    blocks, innovs = [], []
    for _, rows in parts:
        found = jnp.dot(rows, one_hot, preferred_element_type=F32)
        blocks += [found[:K], found[K : 2 * K]]
        innovs += [found[2 * K : 2 * K + 1], found[2 * K + 1 : 2 * K + 2]]
    members, innov = blocks[0], innovs[0]
    for block in range(1, len(blocks)):
        here = high == 2 * first + block
        members = jnp.where(here, blocks[block], members)
        innov = jnp.where(here, innovs[block], innov)
    return jnp.concatenate([members, jnp.broadcast_to(innov, (16, 256))], axis=0).astype(BF16)


def tail_picks(ref, at, row):
    return read_picks(ref[at + 2 * K : at + HALF, :].astype(F32)[row : row + 4])


def pick_kernel(sources, count, *refs):
    outs = refs[count:]
    picks = [tail_picks(refs[which], at, row) for _, (which, at, row), _ in sources]
    for step in range(2 * Y):
        y, span = step // 2, slice(step % 2 * 256, step % 2 * 256 + 256)
        for out, (parts, _, before), values in zip(outs, sources, picks):
            tables = [(half, refs[which][at : at + HALF, :]) for half, which, at in parts]
            found = pick(tables, values[y : y + 1, span])
            out[step] = found if before is None else found + refs[before][step]


def pick_rows(sources, flops, *args):
    return pl.pallas_call(
        functools.partial(pick_kernel, sources, len(args)),
        out_shape=[jax.ShapeDtypeStruct((2 * Y, 144, 256), BF16)] * len(sources),
        in_specs=in_vmem(len(args)),
        out_specs=in_vmem(len(sources)),
        compiler_params=params(),
        cost_estimate=cost(flops),
    )(*args)


def join(first, second):
    low = lax.broadcasted_iota(jnp.int32, first.shape, 1) < K // 2
    return jnp.where(low, first, second), jnp.where(low, second, first)


def pack(total):
    row = lax.broadcasted_iota(jnp.int32, (64, K), 0)
    lane = lax.broadcasted_iota(jnp.int32, (64, K), 1)
    lower = total[64:K]
    upper = jnp.where(lane < row, pltpu.roll(lower, 64, 1), total[0:64])
    diagonal = jnp.sum(jnp.where(lane == row + 64, lower, 0.0), axis=0, keepdims=True)
    return upper, diagonal, total[K : K + 1]


def unpack(packed):
    row = lax.broadcasted_iota(jnp.int32, (64, K), 0)
    lane = lax.broadcasted_iota(jnp.int32, (64, K), 1)
    upper = packed[0:64]
    above = jnp.where(lane > row, upper, 0.0)
    below = pltpu.roll(jnp.where(lane < row, upper, 0.0), 64, 1)
    off = jnp.concatenate([above, below], axis=0)
    low = jnp.where(lane == row + 64, packed[64:65], 0.0)
    diagonal = jnp.concatenate([jnp.where(lane == row, upper, 0.0), low], axis=0)
    return off + off.T + diagonal, packed[65:66]


def last_kernel(shifts, low, high, same, *rest):
    found, outs, picks = rest[:6], rest[6:-1], rest[-1]
    place = lax.div(lax.axis_index("grid"), X * CORES)
    picks[...] = tail_picks(high, 0, 4)
    table = ((0, low[...]), (1, high[...]))
    for out, shift in zip(outs, shifts):
        y = lax.rem(place + shift, Y)
        tail_row = lax.broadcasted_iota(jnp.int32, (16, K), 0)
        tail = jnp.zeros((16, K), F32)
        for i in range(2):
            span = slice(i * 256, i * 256 + 256)
            last = pick(table, picks[pl.ds(y, 1), :][:, span])
            shards = [ref[2 * y + i] for ref in (*found, same)] + [last]
            for half in range(2):
                span = slice(half * K, half * K + K)
                pairs = [
                    join(shards[n][:, span], shards[n + 1][:, span])
                    for n in range(0, len(shards), 2)
                ]
                for side in range(2):
                    rows = jnp.concatenate([pair[side] for pair in pairs], axis=1)
                    total = lax.dot_general(rows, rows[:K], dims(1, 1), preferred_element_type=F32)
                    patch = i + 2 * half + 4 * side
                    upper, diagonal, pull = pack(total)
                    out[patch * 64 : patch * 64 + 64, :] = upper.astype(out.dtype)
                    tail = jnp.where(tail_row == 2 * patch, diagonal, tail)
                    tail = jnp.where(tail_row == 2 * patch + 1, pull, tail)
        out[8 * 64 :, :] = tail.astype(out.dtype)


def last_grams(shifts, dtype, *args):
    return pl.pallas_call(
        functools.partial(last_kernel, shifts),
        out_shape=[jax.ShapeDtypeStruct((8 * 64 + 16, K), dtype)] * len(shifts),
        in_specs=in_vmem(len(args)),
        out_specs=in_vmem(len(shifts)),
        scratch_shapes=[pltpu.VMEM((Y, LOW), jnp.int32)],
        compiler_params=params(),
        cost_estimate=cost(1e9 * len(shifts)),
    )(*args)


def sum_kernel(own, a, b, c, out):
    def total(span):
        return own[span, :] + (a[span, :].astype(F32) + b[span, :].astype(F32) + c[span, :].astype(F32))

    tails = total(slice(8 * 64, 8 * 64 + 16))
    first = lax.broadcasted_iota(jnp.int32, (16, K), 0) == 0
    for patch in range(8):
        out[patch, 0:64, :] = total(slice(patch * 64, patch * 64 + 64)).astype(BF16)
        tail = jnp.where(first, tails[2 * patch : 2 * patch + 1], tails[2 * patch + 1 : 2 * patch + 2])
        out[patch, 64:PACK, :] = tail.astype(BF16)


def sum_parts(*args):
    return pl.pallas_call(
        sum_kernel,
        out_shape=jax.ShapeDtypeStruct((8, PACK, K), BF16),
        in_specs=in_vmem(4),
        out_specs=in_vmem(1)[0],
        compiler_params=params(),
        cost_estimate=cost(5e8),
    )(*args)


def split(value):
    high = value.astype(BF16)
    return high, (value - high.astype(F32)).astype(BF16)


def product(left, right):
    lh, ll = split(left)
    rh, rl = split(right)
    return jnp.dot(
        jnp.concatenate([lh, lh, ll], axis=1),
        jnp.concatenate([rh, rl, rh], axis=0),
        preferred_element_type=F32,
    )


def weights_kernel(parts, out):
    gram, pull = unpack(jnp.sum(parts[...].astype(F32), axis=0))
    row = lax.broadcasted_iota(jnp.int32, (K, K), 0)
    col = lax.broadcasted_iota(jnp.int32, (K, K), 1)
    identity = (row == col).astype(F32)
    system = gram + (K - 1.0) * identity
    squares = jnp.sum(jnp.sum(system * system, axis=0, keepdims=True), axis=1, keepdims=True)
    frob = jnp.sqrt(squares)
    iterate = system / frob
    inverse = 1.5 * identity - 0.5 * iterate
    iterate = product(inverse, iterate)
    for sweep in range(1, ITERS):
        newton = 1.5 * identity - 0.5 * product(inverse, iterate)
        if sweep < ITERS - 1:
            both = product(newton, jnp.concatenate([iterate, inverse], axis=1))
            iterate, inverse = both[:, :K], both[:, K:]
        else:
            inverse = product(newton, inverse)
    shift = product(product(jnp.broadcast_to(pull, (16, K)), inverse), inverse)[0:1] / frob
    out[...] = (jnp.sqrt((K - 1.0) / frob) * inverse.T + shift).astype(BF16)


def transposed_weights(parts):
    return pl.pallas_call(
        weights_kernel,
        out_shape=jax.ShapeDtypeStruct((K, K), BF16),
        in_specs=in_vmem(1),
        out_specs=in_vmem(1)[0],
        compiler_params=params(),
        cost_estimate=cost(4e9),
    )(parts)


def column_coefs():
    position = lax.broadcasted_iota(jnp.int32, (1, 2 * K), 1) % K
    position = (position.astype(F32) + 0.5) / K
    return jnp.maximum(0.5 - position, 0.0), jnp.maximum(position - 0.5, 0.0)


def perturb_kernel(state, mean, perturb, sides):
    for pair in range(mean.shape[0]):
        for i in range(2):
            span = slice(i * K, (i + 1) * K)
            values = state[2 * pair + i].astype(F32)
            average = jnp.mean(values, axis=0, keepdims=True)
            mean[pair : pair + 1, span] = average
            rounded = (values - average).astype(BF16)
            perturb[pair, :, span] = rounded
            for side, coef in enumerate(column_coefs()):
                scaled = coef[:, span] * rounded.astype(F32)
                sides[pair, side * K : (side + 1) * K, span] = scaled.astype(BF16)


def perturbations(state):
    pairs = state.shape[0] // 2
    return pl.pallas_call(
        perturb_kernel,
        out_shape=[
            jax.ShapeDtypeStruct((pairs, 2 * K), F32),
            jax.ShapeDtypeStruct((pairs, K, 2 * K), BF16),
            jax.ShapeDtypeStruct((pairs, 2 * K, 2 * K), BF16),
        ],
        in_specs=in_vmem(1),
        out_specs=in_vmem(3),
        compiler_params=params(),
        cost_estimate=cost(LONG),
    )(state)


def own_kernel(own, mean, perturb, out):
    left_coef, right_coef = column_coefs()
    own_coef = 1.0 - left_coef - right_coef
    for pair in range(mean.shape[0]):
        sums = jnp.dot(own[...], perturb[pair], preferred_element_type=F32)
        out[pair] = mean[pair : pair + 1] + own_coef * sums


def own_part(own, mean, perturb):
    return pl.pallas_call(
        own_kernel,
        out_shape=jax.ShapeDtypeStruct(perturb.shape, F32),
        in_specs=in_vmem(3),
        out_specs=in_vmem(1)[0],
        compiler_params=params(),
        cost_estimate=cost(2e9),
    )(own, mean, perturb)


def side_kernel(left, right, part, sides, out, held, sems):
    weights = jnp.concatenate([left[...], right[...]], axis=1)
    chunks = sems.shape[0]
    pairs = sides.shape[0] // chunks
    copies = []
    for chunk in range(chunks):
        for pair in range(chunk * pairs, (chunk + 1) * pairs):
            total = part[pair] + jnp.dot(weights, sides[pair], preferred_element_type=F32)
            total = total.astype(BF16)
            for i in range(2):
                held[2 * pair + i] = total[:, i * K : (i + 1) * K]
        rows = pl.ds(2 * chunk * pairs, 2 * pairs)
        copies.append(pltpu.make_async_copy(held.at[rows], out.at[rows], sems.at[chunk]))
        copies[-1].start()
    for copy in copies:
        copy.wait()


def add_sides(left, right, part, sides):
    shape = (2 * sides.shape[0], K, K)
    return pl.pallas_call(
        side_kernel,
        out_shape=jax.ShapeDtypeStruct(shape, BF16),
        in_specs=in_vmem(4),
        out_specs=pl.BlockSpec(memory_space=pltpu.HBM),
        scratch_shapes=[pltpu.VMEM(shape, BF16), pltpu.SemaphoreType.DMA((8,))],
        compiler_params=params(),
        cost_estimate=cost(2e9),
    )(left, right, part, sides)


def on_device(departures, innovation, obs_weight, send_rows, send_counts, state):
    n_grid = lax.axis_size("grid")
    low_half, high_half, near = make_messages(
        departures, innovation, obs_weight, send_rows[0].T
    )
    left = hop(low_half, 0, 1, 0)
    right = hop(high_half, 0, -1, 0)
    other = hop(near, 0, 0, 1)

    whole = lambda which: ((0, which, 0), (1, which, HALF))
    found = pick_rows(
        ((whole(0), (0, 0, 8), None), (whole(1), (1, 0, 12), None)), SHORT, near, other
    )
    mean, perturb, sides = perturbations(state)
    low_half, high_half, mean, perturb, sides = lax.optimization_barrier(
        (low_half, high_half, mean, perturb, sides)
    )
    left_more = hop(high_half, 0, 1, 0)
    right_more = hop(low_half, 0, -1, 0)
    left, right, found, mean, perturb = lax.optimization_barrier(
        (left, right, found, mean, perturb)
    )
    far_low, far_high = hop(left, 0, 1, 0), hop(right, 0, -1, 0)

    def firsts(core):
        row = 8 + 4 * core
        return (((0, 0, 0),), (0, 0, row), None), (((1, 1, 0),), (1, 0, row), None)

    def seconds(core):
        row = 8 + 4 * core
        return (((1, 2, 0),), (0, 0, row), 4), (((0, 3, 0),), (1, 0, row), 5)

    same = pick_rows(firsts(0), SHORT, left, right)
    left, right, same = lax.optimization_barrier((left, right, same))
    left_other, right_other = hop(left, 0, 0, 1), hop(right, 0, 0, 1)
    same = pick_rows(seconds(0), LONG, left, right, left_more, right_more, *same)
    left_more, right_more, same = lax.optimization_barrier((left_more, right_more, same))
    left_more_other, right_more_other = hop(left_more, 0, 0, 1), hop(right_more, 0, 0, 1)
    cross = pick_rows(firsts(1), LONG, left_other, right_other)
    cross = pick_rows(
        seconds(1), SHORT, left_other, right_other, left_more_other, right_more_other, *cross
    )
    far_low, far_high, cross = lax.optimization_barrier((far_low, far_high, cross))
    far_low_other, far_high_other = hop(far_low, 0, 0, 1), hop(far_high, 0, 0, 1)
    far = pick_rows(((((0, 0, 0), (1, 1, 0)), (0, 0, 4), None),), SHORT, far_low, far_high)[0]
    last = (far_low_other, far_high_other, far, *found, same[0], cross[0], same[1], cross[1])

    across = last_grams((2,), BF16, *last)[0]
    from_across = hop(across, 2, 0, 0)
    from_up = hop(last_grams((1,), BF16, *last)[0], 1, 0, 0)
    from_down = hop(last_grams((3,), BF16, *last)[0], -1, 0, 0)
    own = last_grams((0,), F32, *last)[0]
    parts = sum_parts(own, from_across, from_up, from_down)
    parts = lax.all_to_all(parts, "obs", 0, 0, tiled=True)

    own = transposed_weights(parts)
    low = lax.ppermute(own, "grid", [(j, (j + 1) % n_grid) for j in range(n_grid)])
    high = lax.ppermute(own, "grid", [(j, (j - 1) % n_grid) for j in range(n_grid)])
    part = own_part(own, mean, perturb)
    return add_sides(low, high, part, sides)


def solution(mesh):
    in_specs = (
        P(("obs", "grid"), None),
        P(("obs", "grid")),
        P(("obs", "grid")),
        P(("obs", "grid"), None, None),
        P(("obs", "grid"), None),
        P("obs", None, "grid"),
    )
    out_specs = P("obs", None, "grid")
    return jax.shard_map(
        on_device, mesh=mesh, in_specs=in_specs, out_specs=out_specs, check_vma=False
    )
```

```python
import functools

import jax
import jax.numpy as jnp
from jax import lax
from jax.experimental import pallas as pl
from jax.experimental.pallas import tpu as pltpu
from jax.sharding import PartitionSpec as P

ITERS = 6
Y, X, CORES = 4, 4, 2
F32, BF16 = jnp.float32, jnp.bfloat16
K = 128
LOW = 512
BLOCKS = 4
HALF = 2 * K + 16
PACK = 80
VMEM = 20 * 1024 * 1024


def params():
    return pltpu.CompilerParams(vmem_limit_bytes=VMEM)


LONG, SHORT = 6e10, 1e6


def cost(flops):
    return pl.CostEstimate(flops=int(flops), bytes_accessed=100_000, transcendentals=0)


def in_vmem(count):
    return [pl.BlockSpec(memory_space=pltpu.VMEM)] * count


def hop(value, dy, dx, dc):
    pairs = []
    for place in range(Y * X * CORES):
        y, x, c = place // (X * CORES), place // CORES % X, place % CORES
        pairs.append((place, ((y ^ dy) * X + (x ^ dx)) * CORES + (c ^ dc)))
    return lax.ppermute(value, "grid", pairs)


def dims(m, n):
    return (((m,), (n,)), ((), ()))


def send_picks(turned, cx, swapped):
    lines = []
    for y in range(Y):
        rows = turned[pl.ds(y * X * CORES + cx, 8, stride=Y * X * CORES), :]
        pair = [rows[0:4], rows[4:8]]
        pairs = jnp.concatenate(pair[::-1] if swapped else pair, axis=1)
        fours = jnp.concatenate([pairs[0:2], pairs[2:4]], axis=1)
        lines.append(jnp.concatenate([fours[0:1], fours[1:2]], axis=1))
    picks = jnp.concatenate(lines, axis=0)
    power = jnp.maximum(lax.shift_right_arithmetic(picks, 7), 0)
    code = lax.shift_left(128 + jnp.bitwise_and(picks, 127), power)
    return jnp.where(picks >= 0, code, 0).astype(F32)


def read_picks(rows):
    left = rows.astype(F32)
    high = jnp.zeros_like(left)
    for step in (8, 4, 2, 1):
        large = left >= 128.0 * 2**step
        left = jnp.where(large, left * 0.5**step, left)
        high = jnp.where(large, high + step, high)
    return jnp.where(left > 0.0, left - 128.0 + 128.0 * high, -1.0).astype(jnp.int32)


def message_kernel(departures, innovation, obs_weight, send_rows, *refs):
    outs, (rows, innov, weight, picks, turned) = refs[:3], refs[3:8]
    built, in_sems = outs, refs[8]
    small = ((send_rows, picks), (obs_weight, weight), (innovation, innov))
    small = [pltpu.make_async_copy(*pair, in_sems.at[i]) for i, pair in enumerate(small)]
    large = []
    for block in range(BLOCKS):
        span = pl.ds(block * LOW, LOW)
        large.append(
            pltpu.make_async_copy(departures.at[span], rows.at[span], in_sems.at[3 + block])
        )
    for copy in small + large:
        copy.start()
    small[0].wait()
    grid = lax.axis_index("grid")
    x, c = lax.rem(lax.div(grid, CORES), X), lax.rem(grid, CORES)
    turned[...] = picks[...].T
    groups = []
    for dx in range(X):
        for dc in range(CORES):
            cx = jnp.bitwise_xor(x, dx) * CORES + jnp.bitwise_xor(c, dc)
            groups.append(send_picks(turned, cx, dc == 1))
    small[1].wait()
    small[2].wait()
    root = jnp.sqrt(weight[...].reshape(1, BLOCKS * LOW))
    scaled = innov[...].reshape(1, BLOCKS * LOW) * root
    blank = jnp.zeros((2, LOW), F32)
    both = built[2]
    for half in range(2):
        one = built[half]
        at = half * HALF
        innovs = []
        for block in range(2):
            start = (2 * half + block) * LOW
            span = slice(start, start + LOW)
            large[2 * half + block].wait()
            part = (rows[span, :].astype(F32).T * root[:, span]).astype(BF16)
            one[block * K : (block + 1) * K, :] = part
            both[at + block * K : at + (block + 1) * K, :] = part
            innovs.append(scaled[:, span])
        top = innovs + [blank, groups[4 + half]]
        next_one = groups[2:4] if half == 0 else groups[6:8]
        one[2 * K :, :] = jnp.concatenate(top + next_one, axis=0).astype(BF16)
        both[at + 2 * K : at + HALF, :] = jnp.concatenate(top + groups[0:2], axis=0).astype(BF16)


def make_messages(*args):
    shapes = [(HALF, LOW), (HALF, LOW), (2 * HALF, LOW)]
    hbm = pl.BlockSpec(memory_space=pltpu.HBM)
    return pl.pallas_call(
        message_kernel,
        out_shape=[jax.ShapeDtypeStruct(shape, BF16) for shape in shapes],
        in_specs=[hbm] * 4,
        out_specs=in_vmem(3),
        scratch_shapes=[pltpu.VMEM(arg.shape, arg.dtype) for arg in args]
        + [pltpu.VMEM(args[3].shape[::-1], jnp.int32)]
        + [pltpu.SemaphoreType.DMA((3 + BLOCKS,))],
        compiler_params=pltpu.CompilerParams(vmem_limit_bytes=VMEM),
        cost_estimate=cost(2e9),
    )(*[pltpu.with_memory_space_constraint(arg, pltpu.HBM) for arg in args])


def pick(parts, picks):
    high = lax.shift_right_arithmetic(picks, 9)
    first = parts[0][0]
    live = picks >= 0 if len(parts) == 2 else lax.shift_right_arithmetic(high, 1) == first
    low = jnp.where(live, jnp.bitwise_and(picks, LOW - 1), -1)
    place = lax.broadcasted_iota(jnp.int32, (LOW, 256), 0).astype(jnp.int16)
    low = jnp.broadcast_to(low, (LOW, 256)).astype(jnp.int16)
    one_hot = jnp.where(place == low, jnp.ones((), BF16), jnp.zeros((), BF16))
    blocks, innovs = [], []
    for _, rows in parts:
        found = jnp.dot(rows, one_hot, preferred_element_type=F32)
        blocks += [found[:K], found[K : 2 * K]]
        innovs += [found[2 * K : 2 * K + 1], found[2 * K + 1 : 2 * K + 2]]
    members, innov = blocks[0], innovs[0]
    for block in range(1, len(blocks)):
        here = high == 2 * first + block
        members = jnp.where(here, blocks[block], members)
        innov = jnp.where(here, innovs[block], innov)
    return jnp.concatenate([members, jnp.broadcast_to(innov, (16, 256))], axis=0).astype(BF16)


def tail_picks(ref, at, row):
    return read_picks(ref[at + 2 * K : at + HALF, :].astype(F32)[row : row + 4])


def pick_kernel(sources, count, *refs):
    outs = refs[count:]
    picks = [tail_picks(refs[which], at, row) for _, (which, at, row), _ in sources]
    for step in range(2 * Y):
        y, span = step // 2, slice(step % 2 * 256, step % 2 * 256 + 256)
        for out, (parts, _, before), values in zip(outs, sources, picks):
            tables = [(half, refs[which][at : at + HALF, :]) for half, which, at in parts]
            found = pick(tables, values[y : y + 1, span])
            out[step] = found if before is None else found + refs[before][step]


def pick_rows(sources, flops, *args):
    return pl.pallas_call(
        functools.partial(pick_kernel, sources, len(args)),
        out_shape=[jax.ShapeDtypeStruct((2 * Y, 144, 256), BF16)] * len(sources),
        in_specs=in_vmem(len(args)),
        out_specs=in_vmem(len(sources)),
        compiler_params=params(),
        cost_estimate=cost(flops),
    )(*args)


def join(first, second):
    low = lax.broadcasted_iota(jnp.int32, first.shape, 1) < K // 2
    return jnp.where(low, first, second), jnp.where(low, second, first)


def pack(total):
    row = lax.broadcasted_iota(jnp.int32, (64, K), 0)
    lane = lax.broadcasted_iota(jnp.int32, (64, K), 1)
    lower = total[64:K]
    upper = jnp.where(lane < row, pltpu.roll(lower, 64, 1), total[0:64])
    diagonal = jnp.sum(jnp.where(lane == row + 64, lower, 0.0), axis=0, keepdims=True)
    return upper, diagonal, total[K : K + 1]


def unpack(packed):
    row = lax.broadcasted_iota(jnp.int32, (64, K), 0)
    lane = lax.broadcasted_iota(jnp.int32, (64, K), 1)
    upper = packed[0:64]
    above = jnp.where(lane > row, upper, 0.0)
    below = pltpu.roll(jnp.where(lane < row, upper, 0.0), 64, 1)
    off = jnp.concatenate([above, below], axis=0)
    low = jnp.where(lane == row + 64, packed[64:65], 0.0)
    diagonal = jnp.concatenate([jnp.where(lane == row, upper, 0.0), low], axis=0)
    return off + off.T + diagonal, packed[65:66]


def last_kernel(shifts, low, high, same, *rest):
    found, outs, picks = rest[:6], rest[6:-1], rest[-1]
    place = lax.div(lax.axis_index("grid"), X * CORES)
    picks[...] = tail_picks(high, 0, 4)
    table = ((0, low[...]), (1, high[...]))
    for out, shift in zip(outs, shifts):
        y = jnp.bitwise_xor(place, shift)
        tail_row = lax.broadcasted_iota(jnp.int32, (16, K), 0)
        tail = jnp.zeros((16, K), F32)
        for i in range(2):
            span = slice(i * 256, i * 256 + 256)
            last = pick(table, picks[pl.ds(y, 1), :][:, span])
            shards = [ref[2 * y + i] for ref in (*found, same)] + [last]
            for half in range(2):
                span = slice(half * K, half * K + K)
                pairs = [
                    join(shards[n][:, span], shards[n + 1][:, span])
                    for n in range(0, len(shards), 2)
                ]
                for side in range(2):
                    rows = jnp.concatenate([pair[side] for pair in pairs], axis=1)
                    total = lax.dot_general(rows, rows[:K], dims(1, 1), preferred_element_type=F32)
                    patch = i + 2 * half + 4 * side
                    upper, diagonal, pull = pack(total)
                    out[patch * 64 : patch * 64 + 64, :] = upper.astype(out.dtype)
                    tail = jnp.where(tail_row == 2 * patch, diagonal, tail)
                    tail = jnp.where(tail_row == 2 * patch + 1, pull, tail)
        out[8 * 64 :, :] = tail.astype(out.dtype)


def last_grams(shifts, dtype, *args):
    return pl.pallas_call(
        functools.partial(last_kernel, shifts),
        out_shape=[jax.ShapeDtypeStruct((8 * 64 + 16, K), dtype)] * len(shifts),
        in_specs=in_vmem(len(args)),
        out_specs=in_vmem(len(shifts)),
        scratch_shapes=[pltpu.VMEM((Y, LOW), jnp.int32)],
        compiler_params=params(),
        cost_estimate=cost(1e9 * len(shifts)),
    )(*args)


def sum_kernel(own, a, b, c, out):
    def total(span):
        return own[span, :] + (a[span, :].astype(F32) + b[span, :].astype(F32) + c[span, :].astype(F32))

    tails = total(slice(8 * 64, 8 * 64 + 16))
    first = lax.broadcasted_iota(jnp.int32, (16, K), 0) == 0
    for patch in range(8):
        out[patch, 0:64, :] = total(slice(patch * 64, patch * 64 + 64)).astype(BF16)
        tail = jnp.where(first, tails[2 * patch : 2 * patch + 1], tails[2 * patch + 1 : 2 * patch + 2])
        out[patch, 64:PACK, :] = tail.astype(BF16)


def sum_parts(*args):
    return pl.pallas_call(
        sum_kernel,
        out_shape=jax.ShapeDtypeStruct((8, PACK, K), BF16),
        in_specs=in_vmem(4),
        out_specs=in_vmem(1)[0],
        compiler_params=params(),
        cost_estimate=cost(5e8),
    )(*args)


def split(value):
    high = value.astype(BF16)
    return high, (value - high.astype(F32)).astype(BF16)


def product(left, right):
    lh, ll = split(left)
    rh, rl = split(right)
    return jnp.dot(
        jnp.concatenate([lh, lh, ll], axis=1),
        jnp.concatenate([rh, rl, rh], axis=0),
        preferred_element_type=F32,
    )


def weights_kernel(parts, out):
    gram, pull = unpack(jnp.sum(parts[...].astype(F32), axis=0))
    row = lax.broadcasted_iota(jnp.int32, (K, K), 0)
    col = lax.broadcasted_iota(jnp.int32, (K, K), 1)
    identity = (row == col).astype(F32)
    system = gram + (K - 1.0) * identity
    squares = jnp.sum(jnp.sum(system * system, axis=0, keepdims=True), axis=1, keepdims=True)
    frob = jnp.sqrt(squares)
    iterate = system / frob
    inverse = 1.5 * identity - 0.5 * iterate
    iterate = product(inverse, iterate)
    for sweep in range(1, ITERS):
        newton = 1.5 * identity - 0.5 * product(inverse, iterate)
        if sweep < ITERS - 1:
            both = product(newton, jnp.concatenate([iterate, inverse], axis=1))
            iterate, inverse = both[:, :K], both[:, K:]
        else:
            inverse = product(newton, inverse)
    shift = product(product(jnp.broadcast_to(pull, (16, K)), inverse), inverse)[0:1] / frob
    out[...] = (jnp.sqrt((K - 1.0) / frob) * inverse.T + shift).astype(BF16)


def transposed_weights(parts):
    return pl.pallas_call(
        weights_kernel,
        out_shape=jax.ShapeDtypeStruct((K, K), BF16),
        in_specs=in_vmem(1),
        out_specs=in_vmem(1)[0],
        compiler_params=params(),
        cost_estimate=cost(4e9),
    )(parts)


def column_coefs():
    position = lax.broadcasted_iota(jnp.int32, (1, 2 * K), 1) % K
    position = (position.astype(F32) + 0.5) / K
    return jnp.maximum(0.5 - position, 0.0), jnp.maximum(position - 0.5, 0.0)


def perturb_kernel(state, mean, perturb, sides):
    for pair in range(mean.shape[0]):
        for i in range(2):
            span = slice(i * K, (i + 1) * K)
            values = state[2 * pair + i].astype(F32)
            average = jnp.mean(values, axis=0, keepdims=True)
            mean[pair : pair + 1, span] = average
            rounded = (values - average).astype(BF16)
            perturb[pair, :, span] = rounded
            for side, coef in enumerate(column_coefs()):
                scaled = coef[:, span] * rounded.astype(F32)
                sides[pair, side * K : (side + 1) * K, span] = scaled.astype(BF16)


def perturbations(state):
    pairs = state.shape[0] // 2
    return pl.pallas_call(
        perturb_kernel,
        out_shape=[
            jax.ShapeDtypeStruct((pairs, 2 * K), F32),
            jax.ShapeDtypeStruct((pairs, K, 2 * K), BF16),
            jax.ShapeDtypeStruct((pairs, 2 * K, 2 * K), BF16),
        ],
        in_specs=in_vmem(1),
        out_specs=in_vmem(3),
        compiler_params=params(),
        cost_estimate=cost(LONG),
    )(state)


def own_kernel(own, mean, perturb, out):
    left_coef, right_coef = column_coefs()
    own_coef = 1.0 - left_coef - right_coef
    for pair in range(mean.shape[0]):
        sums = jnp.dot(own[...], perturb[pair], preferred_element_type=F32)
        out[pair] = mean[pair : pair + 1] + own_coef * sums


def own_part(own, mean, perturb):
    return pl.pallas_call(
        own_kernel,
        out_shape=jax.ShapeDtypeStruct(perturb.shape, F32),
        in_specs=in_vmem(3),
        out_specs=in_vmem(1)[0],
        compiler_params=params(),
        cost_estimate=cost(2e9),
    )(own, mean, perturb)


def side_kernel(beyond, beside, part, sides, out, held, sems):
    first_core = lax.rem(lax.axis_index("grid"), CORES) == 0
    left = jnp.where(first_core, beyond[...], beside[...])
    right = jnp.where(first_core, beside[...], beyond[...])
    weights = jnp.concatenate([left, right], axis=1)
    chunks = sems.shape[0]
    pairs = sides.shape[0] // chunks
    copies = []
    for chunk in range(chunks):
        for pair in range(chunk * pairs, (chunk + 1) * pairs):
            total = part[pair] + jnp.dot(weights, sides[pair], preferred_element_type=F32)
            total = total.astype(BF16)
            for i in range(2):
                held[2 * pair + i] = total[:, i * K : (i + 1) * K]
        rows = pl.ds(2 * chunk * pairs, 2 * pairs)
        copies.append(pltpu.make_async_copy(held.at[rows], out.at[rows], sems.at[chunk]))
        copies[-1].start()
    for copy in copies:
        copy.wait()


def add_sides(beyond, beside, part, sides):
    shape = (2 * sides.shape[0], K, K)
    return pl.pallas_call(
        side_kernel,
        out_shape=jax.ShapeDtypeStruct(shape, BF16),
        in_specs=in_vmem(4),
        out_specs=pl.BlockSpec(memory_space=pltpu.HBM),
        scratch_shapes=[pltpu.VMEM(shape, BF16), pltpu.SemaphoreType.DMA((8,))],
        compiler_params=params(),
        cost_estimate=cost(2e9),
    )(beyond, beside, part, sides)


def on_device(departures, innovation, obs_weight, send_rows, send_counts, state):
    n_grid = lax.axis_size("grid")
    low_half, high_half, near = make_messages(
        departures, innovation, obs_weight, send_rows[0].T
    )
    left = hop(low_half, 0, 1, 0)
    right = hop(high_half, 0, 3, 0)
    other = hop(near, 0, 0, 1)

    whole = lambda which: ((0, which, 0), (1, which, HALF))
    found = pick_rows(
        ((whole(0), (0, 0, 8), None), (whole(1), (1, 0, 12), None)), SHORT, near, other
    )
    mean, perturb, sides = perturbations(state)
    low_half, high_half, mean, perturb, sides = lax.optimization_barrier(
        (low_half, high_half, mean, perturb, sides)
    )
    left_more = hop(high_half, 0, 1, 0)
    right_more = hop(low_half, 0, 3, 0)
    left, right, found, mean, perturb = lax.optimization_barrier(
        (left, right, found, mean, perturb)
    )
    far_low, far_high = hop(left, 0, 3, 0), hop(right, 0, 1, 0)

    def firsts(core):
        row = 8 + 4 * core
        return (((0, 0, 0),), (0, 0, row), None), (((1, 1, 0),), (1, 0, row), None)

    def seconds(core):
        row = 8 + 4 * core
        return (((1, 2, 0),), (0, 0, row), 4), (((0, 3, 0),), (1, 0, row), 5)

    same = pick_rows(firsts(0), SHORT, left, right)
    left, right, same = lax.optimization_barrier((left, right, same))
    left_other, right_other = hop(left, 0, 0, 1), hop(right, 0, 0, 1)
    same = pick_rows(seconds(0), LONG, left, right, left_more, right_more, *same)
    left_more, right_more, same = lax.optimization_barrier((left_more, right_more, same))
    left_more_other, right_more_other = hop(left_more, 0, 0, 1), hop(right_more, 0, 0, 1)
    cross = pick_rows(firsts(1), LONG, left_other, right_other)
    cross = pick_rows(
        seconds(1), SHORT, left_other, right_other, left_more_other, right_more_other, *cross
    )
    far_low, far_high, cross = lax.optimization_barrier((far_low, far_high, cross))
    far_low_other, far_high_other = hop(far_low, 0, 0, 1), hop(far_high, 0, 0, 1)
    far = pick_rows(((((0, 0, 0), (1, 1, 0)), (0, 0, 4), None),), SHORT, far_low, far_high)[0]
    last = (far_low_other, far_high_other, far, *found, same[0], cross[0], same[1], cross[1])

    across = last_grams((2,), BF16, *last)[0]
    from_across = hop(across, 2, 0, 0)
    from_up = hop(last_grams((1,), BF16, *last)[0], 1, 0, 0)
    from_down = hop(last_grams((3,), BF16, *last)[0], 3, 0, 0)
    own = last_grams((0,), F32, *last)[0]
    parts = sum_parts(own, from_across, from_up, from_down)
    parts = lax.all_to_all(parts, "obs", 0, 0, tiled=True)

    own = transposed_weights(parts)
    beyond = lax.ppermute(own, "grid", [(j, (j + 2 * (j % 2) - 1) % n_grid) for j in range(n_grid)])
    beside = hop(own, 0, 0, 1)
    part = own_part(own, mean, perturb)
    return add_sides(beyond, beside, part, sides)


def solution(mesh):
    in_specs = (
        P(("obs", "grid"), None),
        P(("obs", "grid")),
        P(("obs", "grid")),
        P(("obs", "grid"), None, None),
        P(("obs", "grid"), None),
        P("obs", None, "grid"),
    )
    out_specs = P("obs", None, "grid")
    return jax.shard_map(
        on_device, mesh=mesh, in_specs=in_specs, out_specs=out_specs, check_vma=False
    )
```

```python
import functools

import jax
import jax.numpy as jnp
from jax import lax
from jax.experimental import pallas as pl
from jax.experimental.pallas import tpu as pltpu
from jax.sharding import PartitionSpec as P

ITERS = 6
Y, X, CORES = 4, 4, 2
F32, BF16 = jnp.float32, jnp.bfloat16
K = 128
LOW = 512
BLOCKS = 4
HALF = 2 * K + 16
PACK = 80
VMEM = 20 * 1024 * 1024


def params():
    return pltpu.CompilerParams(vmem_limit_bytes=VMEM)


LONG, SHORT = 6e10, 1e6


def cost(flops):
    return pl.CostEstimate(flops=int(flops), bytes_accessed=100_000, transcendentals=0)


def in_vmem(count):
    return [pl.BlockSpec(memory_space=pltpu.VMEM)] * count


def hop(value, dy, dx, dc):
    pairs = []
    for place in range(Y * X * CORES):
        y, x, c = place // (X * CORES), place // CORES % X, place % CORES
        pairs.append((place, ((y + dy) % Y * X + (x + dx) % X) * CORES + (c ^ dc)))
    return lax.ppermute(value, "grid", pairs)


def dims(m, n):
    return (((m,), (n,)), ((), ()))


def send_picks(turned, cx, swapped):
    lines = []
    for y in range(Y):
        rows = turned[pl.ds(y * X * CORES + cx, 8, stride=Y * X * CORES), :]
        pair = [rows[0:4], rows[4:8]]
        pairs = jnp.concatenate(pair[::-1] if swapped else pair, axis=1)
        fours = jnp.concatenate([pairs[0:2], pairs[2:4]], axis=1)
        lines.append(jnp.concatenate([fours[0:1], fours[1:2]], axis=1))
    picks = jnp.concatenate(lines, axis=0)
    power = jnp.maximum(lax.shift_right_arithmetic(picks, 7), 0)
    code = lax.shift_left(128 + jnp.bitwise_and(picks, 127), power)
    return jnp.where(picks >= 0, code, 0).astype(F32)


def read_picks(rows):
    left = rows.astype(F32)
    high = jnp.zeros_like(left)
    for step in (8, 4, 2, 1):
        large = left >= 128.0 * 2**step
        left = jnp.where(large, left * 0.5**step, left)
        high = jnp.where(large, high + step, high)
    return jnp.where(left > 0.0, left - 128.0 + 128.0 * high, -1.0).astype(jnp.int32)


def message_kernel(departures, innovation, obs_weight, send_rows, *refs):
    outs, (rows, innov, weight, picks, turned) = refs[:3], refs[3:8]
    built, in_sems = outs, refs[8]
    small = ((send_rows, picks), (obs_weight, weight), (innovation, innov))
    small = [pltpu.make_async_copy(*pair, in_sems.at[i]) for i, pair in enumerate(small)]
    large = []
    for block in range(BLOCKS):
        span = pl.ds(block * LOW, LOW)
        large.append(
            pltpu.make_async_copy(departures.at[span], rows.at[span], in_sems.at[3 + block])
        )
    for copy in small + large:
        copy.start()
    small[0].wait()
    grid = lax.axis_index("grid")
    x, c = lax.rem(lax.div(grid, CORES), X), lax.rem(grid, CORES)
    turned[...] = picks[...].T
    groups = []
    for dx in range(X):
        for dc in range(CORES):
            cx = lax.rem(x + dx, X) * CORES + lax.rem(c + dc, CORES)
            groups.append(send_picks(turned, cx, dc == 1))
    small[1].wait()
    small[2].wait()
    root = jnp.sqrt(weight[...].reshape(1, BLOCKS * LOW))
    scaled = innov[...].reshape(1, BLOCKS * LOW) * root
    blank = jnp.zeros((2, LOW), F32)
    both = built[2]
    for half in range(2):
        one = built[half]
        at = half * HALF
        innovs = []
        for block in range(2):
            start = (2 * half + block) * LOW
            span = slice(start, start + LOW)
            large[2 * half + block].wait()
            part = (rows[span, :].astype(F32).T * root[:, span]).astype(BF16)
            one[block * K : (block + 1) * K, :] = part
            both[at + block * K : at + (block + 1) * K, :] = part
            innovs.append(scaled[:, span])
        top = innovs + [blank, groups[4 + half]]
        next_one = groups[2:4] if half == 0 else groups[6:8]
        one[2 * K :, :] = jnp.concatenate(top + next_one, axis=0).astype(BF16)
        both[at + 2 * K : at + HALF, :] = jnp.concatenate(top + groups[0:2], axis=0).astype(BF16)


def make_messages(*args):
    shapes = [(HALF, LOW), (HALF, LOW), (2 * HALF, LOW)]
    hbm = pl.BlockSpec(memory_space=pltpu.HBM)
    return pl.pallas_call(
        message_kernel,
        out_shape=[jax.ShapeDtypeStruct(shape, BF16) for shape in shapes],
        in_specs=[hbm] * 4,
        out_specs=in_vmem(3),
        scratch_shapes=[pltpu.VMEM(arg.shape, arg.dtype) for arg in args]
        + [pltpu.VMEM(args[3].shape[::-1], jnp.int32)]
        + [pltpu.SemaphoreType.DMA((3 + BLOCKS,))],
        compiler_params=pltpu.CompilerParams(vmem_limit_bytes=VMEM),
        cost_estimate=cost(2e9),
    )(*[pltpu.with_memory_space_constraint(arg, pltpu.HBM) for arg in args])


def pick(parts, picks):
    high = lax.shift_right_arithmetic(picks, 9)
    first = parts[0][0]
    live = picks >= 0 if len(parts) == 2 else lax.shift_right_arithmetic(high, 1) == first
    low = jnp.where(live, jnp.bitwise_and(picks, LOW - 1), -1)
    place = lax.broadcasted_iota(jnp.int32, (LOW, 256), 0).astype(jnp.int16)
    low = jnp.broadcast_to(low, (LOW, 256)).astype(jnp.int16)
    one_hot = jnp.where(place == low, jnp.ones((), BF16), jnp.zeros((), BF16))
    blocks, innovs = [], []
    for _, rows in parts:
        found = jnp.dot(rows, one_hot, preferred_element_type=F32)
        blocks += [found[:K], found[K : 2 * K]]
        innovs += [found[2 * K : 2 * K + 1], found[2 * K + 1 : 2 * K + 2]]
    members, innov = blocks[0], innovs[0]
    for block in range(1, len(blocks)):
        here = high == 2 * first + block
        members = jnp.where(here, blocks[block], members)
        innov = jnp.where(here, innovs[block], innov)
    return jnp.concatenate([members, jnp.broadcast_to(innov, (16, 256))], axis=0).astype(BF16)


def tail_picks(ref, at, row):
    return read_picks(ref[at + 2 * K : at + HALF, :].astype(F32)[row : row + 4])


def pick_kernel(sources, count, *refs):
    outs = refs[count:]
    picks = [tail_picks(refs[which], at, row) for _, (which, at, row), _ in sources]
    for step in range(2 * Y):
        y, span = step // 2, slice(step % 2 * 256, step % 2 * 256 + 256)
        for out, (parts, _, before), values in zip(outs, sources, picks):
            tables = [(half, refs[which][at : at + HALF, :]) for half, which, at in parts]
            found = pick(tables, values[y : y + 1, span])
            out[step] = found if before is None else found + refs[before][step]


def pick_rows(sources, flops, *args):
    return pl.pallas_call(
        functools.partial(pick_kernel, sources, len(args)),
        out_shape=[jax.ShapeDtypeStruct((2 * Y, 144, 256), BF16)] * len(sources),
        in_specs=in_vmem(len(args)),
        out_specs=in_vmem(len(sources)),
        compiler_params=params(),
        cost_estimate=cost(flops),
    )(*args)


def join(first, second):
    low = lax.broadcasted_iota(jnp.int32, first.shape, 1) < K // 2
    return jnp.where(low, first, second), jnp.where(low, second, first)


def pack(total):
    row = lax.broadcasted_iota(jnp.int32, (64, K), 0)
    lane = lax.broadcasted_iota(jnp.int32, (64, K), 1)
    lower = total[64:K]
    upper = jnp.where(lane < row, pltpu.roll(lower, 64, 1), total[0:64])
    diagonal = jnp.sum(jnp.where(lane == row + 64, lower, 0.0), axis=0, keepdims=True)
    return upper, diagonal, total[K : K + 1]


def unpack(packed):
    row = lax.broadcasted_iota(jnp.int32, (64, K), 0)
    lane = lax.broadcasted_iota(jnp.int32, (64, K), 1)
    upper = packed[0:64]
    above = jnp.where(lane > row, upper, 0.0)
    below = pltpu.roll(jnp.where(lane < row, upper, 0.0), 64, 1)
    off = jnp.concatenate([above, below], axis=0)
    low = jnp.where(lane == row + 64, packed[64:65], 0.0)
    diagonal = jnp.concatenate([jnp.where(lane == row, upper, 0.0), low], axis=0)
    return off + off.T + diagonal, packed[65:66]


def last_kernel(shifts, low, high, same, *rest):
    found, outs, picks = rest[:6], rest[6:-1], rest[-1]
    place = lax.div(lax.axis_index("grid"), X * CORES)
    picks[...] = tail_picks(high, 0, 4)
    table = ((0, low[...]), (1, high[...]))
    for out, shift in zip(outs, shifts):
        y = lax.rem(place + shift, Y)
        tail_row = lax.broadcasted_iota(jnp.int32, (16, K), 0)
        tail = jnp.zeros((16, K), F32)
        for i in range(2):
            span = slice(i * 256, i * 256 + 256)
            last = pick(table, picks[pl.ds(y, 1), :][:, span])
            shards = [ref[2 * y + i] for ref in (*found, same)] + [last]
            for half in range(2):
                span = slice(half * K, half * K + K)
                pairs = [
                    join(shards[n][:, span], shards[n + 1][:, span])
                    for n in range(0, len(shards), 2)
                ]
                for side in range(2):
                    rows = jnp.concatenate([pair[side] for pair in pairs], axis=1)
                    total = lax.dot_general(rows, rows[:K], dims(1, 1), preferred_element_type=F32)
                    patch = i + 2 * half + 4 * side
                    upper, diagonal, pull = pack(total)
                    out[patch * 64 : patch * 64 + 64, :] = upper.astype(out.dtype)
                    tail = jnp.where(tail_row == 2 * patch, diagonal, tail)
                    tail = jnp.where(tail_row == 2 * patch + 1, pull, tail)
        out[8 * 64 :, :] = tail.astype(out.dtype)


def last_grams(shifts, dtype, *args):
    return pl.pallas_call(
        functools.partial(last_kernel, shifts),
        out_shape=[jax.ShapeDtypeStruct((8 * 64 + 16, K), dtype)] * len(shifts),
        in_specs=in_vmem(len(args)),
        out_specs=in_vmem(len(shifts)),
        scratch_shapes=[pltpu.VMEM((Y, LOW), jnp.int32)],
        compiler_params=params(),
        cost_estimate=cost(1e9 * len(shifts)),
    )(*args)


def sum_kernel(own, a, b, c, out):
    def total(span):
        return own[span, :] + (a[span, :].astype(F32) + b[span, :].astype(F32) + c[span, :].astype(F32))

    tails = total(slice(8 * 64, 8 * 64 + 16))
    first = lax.broadcasted_iota(jnp.int32, (16, K), 0) == 0
    for patch in range(8):
        out[patch, 0:64, :] = total(slice(patch * 64, patch * 64 + 64)).astype(BF16)
        tail = jnp.where(first, tails[2 * patch : 2 * patch + 1], tails[2 * patch + 1 : 2 * patch + 2])
        out[patch, 64:PACK, :] = tail.astype(BF16)


def sum_parts(*args):
    return pl.pallas_call(
        sum_kernel,
        out_shape=jax.ShapeDtypeStruct((8, PACK, K), BF16),
        in_specs=in_vmem(4),
        out_specs=in_vmem(1)[0],
        compiler_params=params(),
        cost_estimate=cost(5e8),
    )(*args)


def split(value):
    high = value.astype(BF16)
    return high, (value - high.astype(F32)).astype(BF16)


def product(left, right):
    lh, ll = split(left)
    rh, rl = split(right)
    return jnp.dot(
        jnp.concatenate([lh, lh, ll], axis=1),
        jnp.concatenate([rh, rl, rh], axis=0),
        preferred_element_type=F32,
    )


def weights_kernel(parts, out):
    gram, pull = unpack(jnp.sum(parts[...].astype(F32), axis=0))
    row = lax.broadcasted_iota(jnp.int32, (K, K), 0)
    col = lax.broadcasted_iota(jnp.int32, (K, K), 1)
    identity = (row == col).astype(F32)
    system = gram + (K - 1.0) * identity
    squares = jnp.sum(jnp.sum(system * system, axis=0, keepdims=True), axis=1, keepdims=True)
    frob = jnp.sqrt(squares)
    iterate = system / frob
    inverse = 1.5 * identity - 0.5 * iterate
    iterate = product(inverse, iterate)
    for sweep in range(1, ITERS):
        newton = 1.5 * identity - 0.5 * product(inverse, iterate)
        if sweep < ITERS - 1:
            both = product(newton, jnp.concatenate([iterate, inverse], axis=1))
            iterate, inverse = both[:, :K], both[:, K:]
        else:
            inverse = product(newton, inverse)
    shift = product(product(jnp.broadcast_to(pull, (16, K)), inverse), inverse)[0:1] / frob
    out[...] = (jnp.sqrt((K - 1.0) / frob) * inverse.T + shift).astype(BF16)


def transposed_weights(parts):
    return pl.pallas_call(
        weights_kernel,
        out_shape=jax.ShapeDtypeStruct((K, K), BF16),
        in_specs=in_vmem(1),
        out_specs=in_vmem(1)[0],
        compiler_params=params(),
        cost_estimate=cost(4e9),
    )(parts)


def column_coefs():
    position = lax.broadcasted_iota(jnp.int32, (1, 2 * K), 1) % K
    position = (position.astype(F32) + 0.5) / K
    return jnp.maximum(0.5 - position, 0.0), jnp.maximum(position - 0.5, 0.0)


def perturb_kernel(state, mean, perturb, sides):
    for pair in range(mean.shape[0]):
        for i in range(2):
            span = slice(i * K, (i + 1) * K)
            values = state[2 * pair + i].astype(F32)
            average = jnp.mean(values, axis=0, keepdims=True)
            mean[pair : pair + 1, span] = average
            rounded = (values - average).astype(BF16)
            perturb[pair, :, span] = rounded
            for side, coef in enumerate(column_coefs()):
                scaled = coef[:, span] * rounded.astype(F32)
                sides[pair, side * K : (side + 1) * K, span] = scaled.astype(BF16)


def perturbations(state):
    pairs = state.shape[0] // 2
    return pl.pallas_call(
        perturb_kernel,
        out_shape=[
            jax.ShapeDtypeStruct((pairs, 2 * K), F32),
            jax.ShapeDtypeStruct((pairs, K, 2 * K), BF16),
            jax.ShapeDtypeStruct((pairs, 2 * K, 2 * K), BF16),
        ],
        in_specs=in_vmem(1),
        out_specs=in_vmem(3),
        compiler_params=params(),
        cost_estimate=cost(LONG),
    )(state)


def own_kernel(own, mean, perturb, out):
    left_coef, right_coef = column_coefs()
    own_coef = 1.0 - left_coef - right_coef
    for pair in range(mean.shape[0]):
        sums = jnp.dot(own[...], perturb[pair], preferred_element_type=F32)
        out[pair] = mean[pair : pair + 1] + own_coef * sums


def own_part(own, mean, perturb):
    return pl.pallas_call(
        own_kernel,
        out_shape=jax.ShapeDtypeStruct(perturb.shape, F32),
        in_specs=in_vmem(3),
        out_specs=in_vmem(1)[0],
        compiler_params=params(),
        cost_estimate=cost(2e9),
    )(own, mean, perturb)


def side_kernel(beyond, beside, part, sides, out, held, sems):
    first_core = lax.rem(lax.axis_index("grid"), CORES) == 0
    left = jnp.where(first_core, beyond[...], beside[...])
    right = jnp.where(first_core, beside[...], beyond[...])
    weights = jnp.concatenate([left, right], axis=1)
    chunks = sems.shape[0]
    pairs = sides.shape[0] // chunks
    copies = []
    for chunk in range(chunks):
        for pair in range(chunk * pairs, (chunk + 1) * pairs):
            total = part[pair] + jnp.dot(weights, sides[pair], preferred_element_type=F32)
            total = total.astype(BF16)
            for i in range(2):
                held[2 * pair + i] = total[:, i * K : (i + 1) * K]
        rows = pl.ds(2 * chunk * pairs, 2 * pairs)
        copies.append(pltpu.make_async_copy(held.at[rows], out.at[rows], sems.at[chunk]))
        copies[-1].start()
    for copy in copies:
        copy.wait()


def add_sides(beyond, beside, part, sides):
    shape = (2 * sides.shape[0], K, K)
    return pl.pallas_call(
        side_kernel,
        out_shape=jax.ShapeDtypeStruct(shape, BF16),
        in_specs=in_vmem(4),
        out_specs=pl.BlockSpec(memory_space=pltpu.HBM),
        scratch_shapes=[pltpu.VMEM(shape, BF16), pltpu.SemaphoreType.DMA((8,))],
        compiler_params=params(),
        cost_estimate=cost(2e9),
    )(beyond, beside, part, sides)


def on_device(departures, innovation, obs_weight, send_rows, send_counts, state):
    n_grid = lax.axis_size("grid")
    low_half, high_half, near = make_messages(
        departures, innovation, obs_weight, send_rows[0].T
    )
    left = hop(low_half, 0, 1, 0)
    right = hop(high_half, 0, -1, 0)
    other = hop(near, 0, 0, 1)

    whole = lambda which: ((0, which, 0), (1, which, HALF))
    found = pick_rows(
        ((whole(0), (0, 0, 8), None), (whole(1), (1, 0, 12), None)), SHORT, near, other
    )
    mean, perturb, sides = perturbations(state)
    low_half, high_half, mean, perturb, sides = lax.optimization_barrier(
        (low_half, high_half, mean, perturb, sides)
    )
    left_more = hop(high_half, 0, 1, 0)
    right_more = hop(low_half, 0, -1, 0)
    left, right, found, mean, perturb = lax.optimization_barrier(
        (left, right, found, mean, perturb)
    )
    far_low, far_high = hop(left, 0, 1, 0), hop(right, 0, -1, 0)

    def firsts(core):
        row = 8 + 4 * core
        return (((0, 0, 0),), (0, 0, row), None), (((1, 1, 0),), (1, 0, row), None)

    def seconds(core):
        row = 8 + 4 * core
        return (((1, 2, 0),), (0, 0, row), 4), (((0, 3, 0),), (1, 0, row), 5)

    same = pick_rows(firsts(0), SHORT, left, right)
    left, right, same = lax.optimization_barrier((left, right, same))
    left_other, right_other = hop(left, 0, 0, 1), hop(right, 0, 0, 1)
    same = pick_rows(seconds(0), LONG, left, right, left_more, right_more, *same)
    left_more, right_more, same = lax.optimization_barrier((left_more, right_more, same))
    left_more_other, right_more_other = hop(left_more, 0, 0, 1), hop(right_more, 0, 0, 1)
    cross = pick_rows(firsts(1), LONG, left_other, right_other)
    cross = pick_rows(
        seconds(1), SHORT, left_other, right_other, left_more_other, right_more_other, *cross
    )
    far_low, far_high, cross = lax.optimization_barrier((far_low, far_high, cross))
    far_low_other, far_high_other = hop(far_low, 0, 0, 1), hop(far_high, 0, 0, 1)
    far = pick_rows(((((0, 0, 0), (1, 1, 0)), (0, 0, 4), None),), SHORT, far_low, far_high)[0]
    last = (far_low_other, far_high_other, far, *found, same[0], cross[0], same[1], cross[1])

    across = last_grams((2,), BF16, *last)[0]
    from_across = hop(across, 2, 0, 0)
    from_up = hop(last_grams((1,), BF16, *last)[0], 1, 0, 0)
    from_down = hop(last_grams((3,), BF16, *last)[0], -1, 0, 0)
    own = last_grams((0,), F32, *last)[0]
    parts = sum_parts(own, from_across, from_up, from_down)
    parts = lax.all_to_all(parts, "obs", 0, 0, tiled=True)

    own = transposed_weights(parts)
    beyond = lax.ppermute(own, "grid", [(j, (j + 2 * (j % 2) - 1) % n_grid) for j in range(n_grid)])
    part = own_part(own, mean, perturb)
    own, part = lax.optimization_barrier((own, part))
    beside = hop(own, 0, 0, 1)
    return add_sides(beyond, beside, part, sides)


def solution(mesh):
    in_specs = (
        P(("obs", "grid"), None),
        P(("obs", "grid")),
        P(("obs", "grid")),
        P(("obs", "grid"), None, None),
        P(("obs", "grid"), None),
        P("obs", None, "grid"),
    )
    out_specs = P("obs", None, "grid")
    return jax.shard_map(
        on_device, mesh=mesh, in_specs=in_specs, out_specs=out_specs, check_vma=False
    )
```

```python
import functools

import jax
import jax.numpy as jnp
from jax import lax
from jax.experimental import pallas as pl
from jax.experimental.pallas import tpu as pltpu
from jax.sharding import PartitionSpec as P

ITERS = 6
Y, X, CORES = 4, 4, 2
F32, BF16 = jnp.float32, jnp.bfloat16
K = 128
LOW = 512
BLOCKS = 4
HALF = 2 * K + 16
PACK = 80
VMEM = 20 * 1024 * 1024


def params():
    return pltpu.CompilerParams(vmem_limit_bytes=VMEM)


LONG, SHORT = 6e10, 1e6


def cost(flops):
    return pl.CostEstimate(flops=int(flops), bytes_accessed=100_000, transcendentals=0)


def in_vmem(count):
    return [pl.BlockSpec(memory_space=pltpu.VMEM)] * count


def hop(value, dy, dx, dc):
    pairs = []
    for place in range(Y * X * CORES):
        y, x, c = place // (X * CORES), place // CORES % X, place % CORES
        pairs.append((place, ((y + dy) % Y * X + (x + dx) % X) * CORES + (c ^ dc)))
    return lax.ppermute(value, "grid", pairs)


def dims(m, n):
    return (((m,), (n,)), ((), ()))


def send_picks(turned, cx, swapped):
    lines = []
    for y in range(Y):
        rows = turned[pl.ds(y * X * CORES + cx, 8, stride=Y * X * CORES), :]
        pair = [rows[0:4], rows[4:8]]
        pairs = jnp.concatenate(pair[::-1] if swapped else pair, axis=1)
        fours = jnp.concatenate([pairs[0:2], pairs[2:4]], axis=1)
        lines.append(jnp.concatenate([fours[0:1], fours[1:2]], axis=1))
    picks = jnp.concatenate(lines, axis=0)
    power = jnp.maximum(lax.shift_right_arithmetic(picks, 7), 0)
    code = lax.shift_left(128 + jnp.bitwise_and(picks, 127), power)
    return jnp.where(picks >= 0, code, 0).astype(F32)


def read_picks(rows):
    left = rows.astype(F32)
    high = jnp.zeros_like(left)
    for step in (8, 4, 2, 1):
        large = left >= 128.0 * 2**step
        left = jnp.where(large, left * 0.5**step, left)
        high = jnp.where(large, high + step, high)
    return jnp.where(left > 0.0, left - 128.0 + 128.0 * high, -1.0).astype(jnp.int32)


def message_kernel(departures, innovation, obs_weight, send_rows, *refs):
    outs, (rows, innov, weight, picks, turned) = refs[:3], refs[3:8]
    built, in_sems = outs, refs[8]
    small = ((send_rows, picks), (obs_weight, weight), (innovation, innov))
    small = [pltpu.make_async_copy(*pair, in_sems.at[i]) for i, pair in enumerate(small)]
    large = []
    for block in range(BLOCKS):
        span = pl.ds(block * LOW, LOW)
        large.append(
            pltpu.make_async_copy(departures.at[span], rows.at[span], in_sems.at[3 + block])
        )
    for copy in small + large:
        copy.start()
    small[0].wait()
    grid = lax.axis_index("grid")
    x, c = lax.rem(lax.div(grid, CORES), X), lax.rem(grid, CORES)
    turned[...] = picks[...].T
    groups = []
    for dx in range(X):
        for dc in range(CORES):
            cx = lax.rem(x + dx, X) * CORES + lax.rem(c + dc, CORES)
            groups.append(send_picks(turned, cx, dc == 1))
    small[1].wait()
    small[2].wait()
    root = jnp.sqrt(weight[...].reshape(1, BLOCKS * LOW))
    scaled = innov[...].reshape(1, BLOCKS * LOW) * root
    blank = jnp.zeros((2, LOW), F32)
    both = built[2]
    for half in range(2):
        one = built[half]
        at = half * HALF
        innovs = []
        for block in range(2):
            start = (2 * half + block) * LOW
            span = slice(start, start + LOW)
            large[2 * half + block].wait()
            part = (rows[span, :].astype(F32).T * root[:, span]).astype(BF16)
            one[block * K : (block + 1) * K, :] = part
            both[at + block * K : at + (block + 1) * K, :] = part
            innovs.append(scaled[:, span])
        top = innovs + [blank, groups[4 + half]]
        next_one = groups[2:4] if half == 0 else groups[6:8]
        one[2 * K :, :] = jnp.concatenate(top + next_one, axis=0).astype(BF16)
        both[at + 2 * K : at + HALF, :] = jnp.concatenate(top + groups[0:2], axis=0).astype(BF16)


def make_messages(*args):
    shapes = [(HALF, LOW), (HALF, LOW), (2 * HALF, LOW)]
    hbm = pl.BlockSpec(memory_space=pltpu.HBM)
    return pl.pallas_call(
        message_kernel,
        out_shape=[jax.ShapeDtypeStruct(shape, BF16) for shape in shapes],
        in_specs=[hbm] * 4,
        out_specs=in_vmem(3),
        scratch_shapes=[pltpu.VMEM(arg.shape, arg.dtype) for arg in args]
        + [pltpu.VMEM(args[3].shape[::-1], jnp.int32)]
        + [pltpu.SemaphoreType.DMA((3 + BLOCKS,))],
        compiler_params=pltpu.CompilerParams(vmem_limit_bytes=VMEM),
        cost_estimate=cost(2e9),
    )(*[pltpu.with_memory_space_constraint(arg, pltpu.HBM) for arg in args])


def pick(parts, picks):
    high = lax.shift_right_arithmetic(picks, 9)
    first = parts[0][0]
    live = picks >= 0 if len(parts) == 2 else lax.shift_right_arithmetic(high, 1) == first
    low = jnp.where(live, jnp.bitwise_and(picks, LOW - 1), -1)
    place = lax.broadcasted_iota(jnp.int32, (LOW, 256), 0).astype(jnp.int16)
    low = jnp.broadcast_to(low, (LOW, 256)).astype(jnp.int16)
    one_hot = jnp.where(place == low, jnp.ones((), BF16), jnp.zeros((), BF16))
    blocks, innovs = [], []
    for _, rows in parts:
        found = jnp.dot(rows, one_hot, preferred_element_type=F32)
        blocks += [found[:K], found[K : 2 * K]]
        innovs += [found[2 * K : 2 * K + 1], found[2 * K + 1 : 2 * K + 2]]
    members, innov = blocks[0], innovs[0]
    for block in range(1, len(blocks)):
        here = high == 2 * first + block
        members = jnp.where(here, blocks[block], members)
        innov = jnp.where(here, innovs[block], innov)
    return jnp.concatenate([members, jnp.broadcast_to(innov, (16, 256))], axis=0).astype(BF16)


def tail_picks(ref, at, row):
    return read_picks(ref[at + 2 * K : at + HALF, :].astype(F32)[row : row + 4])


def pick_kernel(sources, count, *refs):
    outs = refs[count:]
    picks = [tail_picks(refs[which], at, row) for _, (which, at, row), _ in sources]
    for step in range(2 * Y):
        y, span = step // 2, slice(step % 2 * 256, step % 2 * 256 + 256)
        for out, (parts, _, before), values in zip(outs, sources, picks):
            tables = [(half, refs[which][at : at + HALF, :]) for half, which, at in parts]
            found = pick(tables, values[y : y + 1, span])
            out[step] = found if before is None else found + refs[before][step]


def pick_rows(sources, flops, *args):
    return pl.pallas_call(
        functools.partial(pick_kernel, sources, len(args)),
        out_shape=[jax.ShapeDtypeStruct((2 * Y, 144, 256), BF16)] * len(sources),
        in_specs=in_vmem(len(args)),
        out_specs=in_vmem(len(sources)),
        compiler_params=params(),
        cost_estimate=cost(flops),
    )(*args)


def join(first, second):
    low = lax.broadcasted_iota(jnp.int32, first.shape, 1) < K // 2
    return jnp.where(low, first, second), jnp.where(low, second, first)


def pack(total):
    row = lax.broadcasted_iota(jnp.int32, (64, K), 0)
    lane = lax.broadcasted_iota(jnp.int32, (64, K), 1)
    lower = total[64:K]
    upper = jnp.where(lane < row, pltpu.roll(lower, 64, 1), total[0:64])
    diagonal = jnp.sum(jnp.where(lane == row + 64, lower, 0.0), axis=0, keepdims=True)
    return upper, diagonal, total[K : K + 1]


def unpack(packed):
    row = lax.broadcasted_iota(jnp.int32, (64, K), 0)
    lane = lax.broadcasted_iota(jnp.int32, (64, K), 1)
    upper = packed[0:64]
    above = jnp.where(lane > row, upper, 0.0)
    below = pltpu.roll(jnp.where(lane < row, upper, 0.0), 64, 1)
    off = jnp.concatenate([above, below], axis=0)
    low = jnp.where(lane == row + 64, packed[64:65], 0.0)
    diagonal = jnp.concatenate([jnp.where(lane == row, upper, 0.0), low], axis=0)
    return off + off.T + diagonal, packed[65:66]


def last_kernel(shifts, low, high, same, *rest):
    found, outs, picks = rest[:6], rest[6:-1], rest[-1]
    place = lax.div(lax.axis_index("grid"), X * CORES)
    picks[...] = tail_picks(high, 0, 4)
    table = ((0, low[...]), (1, high[...]))
    for out, shift in zip(outs, shifts):
        y = lax.rem(place + shift, Y)
        tail_row = lax.broadcasted_iota(jnp.int32, (16, K), 0)
        tail = jnp.zeros((16, K), F32)
        for i in range(2):
            span = slice(i * 256, i * 256 + 256)
            last = pick(table, picks[pl.ds(y, 1), :][:, span])
            shards = [ref[2 * y + i] for ref in (*found, same)] + [last]
            for half in range(2):
                span = slice(half * K, half * K + K)
                pairs = [
                    join(shards[n][:, span], shards[n + 1][:, span])
                    for n in range(0, len(shards), 2)
                ]
                for side in range(2):
                    rows = jnp.concatenate([pair[side] for pair in pairs], axis=1)
                    total = lax.dot_general(rows, rows[:K], dims(1, 1), preferred_element_type=F32)
                    patch = i + 2 * half + 4 * side
                    upper, diagonal, pull = pack(total)
                    out[patch * 64 : patch * 64 + 64, :] = upper.astype(out.dtype)
                    tail = jnp.where(tail_row == 2 * patch, diagonal, tail)
                    tail = jnp.where(tail_row == 2 * patch + 1, pull, tail)
        out[8 * 64 :, :] = tail.astype(out.dtype)


def last_grams(shifts, dtype, *args):
    return pl.pallas_call(
        functools.partial(last_kernel, shifts),
        out_shape=[jax.ShapeDtypeStruct((8 * 64 + 16, K), dtype)] * len(shifts),
        in_specs=in_vmem(len(args)),
        out_specs=in_vmem(len(shifts)),
        scratch_shapes=[pltpu.VMEM((Y, LOW), jnp.int32)],
        compiler_params=params(),
        cost_estimate=cost(1e9 * len(shifts)),
    )(*args)


def sum_kernel(own, a, b, c, out):
    def total(span):
        return own[span, :] + (a[span, :].astype(F32) + b[span, :].astype(F32) + c[span, :].astype(F32))

    tails = total(slice(8 * 64, 8 * 64 + 16))
    first = lax.broadcasted_iota(jnp.int32, (16, K), 0) == 0
    for patch in range(8):
        out[patch, 0:64, :] = total(slice(patch * 64, patch * 64 + 64)).astype(BF16)
        tail = jnp.where(first, tails[2 * patch : 2 * patch + 1], tails[2 * patch + 1 : 2 * patch + 2])
        out[patch, 64:PACK, :] = tail.astype(BF16)


def sum_parts(*args):
    return pl.pallas_call(
        sum_kernel,
        out_shape=jax.ShapeDtypeStruct((8, PACK, K), BF16),
        in_specs=in_vmem(4),
        out_specs=in_vmem(1)[0],
        compiler_params=params(),
        cost_estimate=cost(5e8),
    )(*args)


def split(value):
    high = value.astype(BF16)
    return high, (value - high.astype(F32)).astype(BF16)


def product(left, right):
    lh, ll = split(left)
    rh, rl = split(right)
    return jnp.dot(
        jnp.concatenate([lh, lh, ll], axis=1),
        jnp.concatenate([rh, rl, rh], axis=0),
        preferred_element_type=F32,
    )


def weights_kernel(parts, out):
    gram, pull = unpack(jnp.sum(parts[...].astype(F32), axis=0))
    row = lax.broadcasted_iota(jnp.int32, (K, K), 0)
    col = lax.broadcasted_iota(jnp.int32, (K, K), 1)
    identity = (row == col).astype(F32)
    system = gram + (K - 1.0) * identity
    squares = jnp.sum(jnp.sum(system * system, axis=0, keepdims=True), axis=1, keepdims=True)
    frob = jnp.sqrt(squares)
    iterate = system / frob
    inverse = 1.5 * identity - 0.5 * iterate
    iterate = product(inverse, iterate)
    for sweep in range(1, ITERS):
        newton = 1.5 * identity - 0.5 * product(inverse, iterate)
        if sweep < ITERS - 1:
            both = product(newton, jnp.concatenate([iterate, inverse], axis=1))
            iterate, inverse = both[:, :K], both[:, K:]
        else:
            inverse = product(newton, inverse)
    shift = product(product(jnp.broadcast_to(pull, (16, K)), inverse), inverse)[0:1] / frob
    out[...] = (jnp.sqrt((K - 1.0) / frob) * inverse.T + shift).astype(BF16)


def transposed_weights(parts):
    return pl.pallas_call(
        weights_kernel,
        out_shape=jax.ShapeDtypeStruct((K, K), BF16),
        in_specs=in_vmem(1),
        out_specs=in_vmem(1)[0],
        compiler_params=params(),
        cost_estimate=cost(4e9),
    )(parts)


def column_coefs():
    position = lax.broadcasted_iota(jnp.int32, (1, 2 * K), 1) % K
    position = (position.astype(F32) + 0.5) / K
    return jnp.maximum(0.5 - position, 0.0), jnp.maximum(position - 0.5, 0.0)


def perturb_kernel(state, mean, perturb, sides):
    for pair in range(mean.shape[0]):
        for i in range(2):
            span = slice(i * K, (i + 1) * K)
            values = state[2 * pair + i].astype(F32)
            average = jnp.mean(values, axis=0, keepdims=True)
            mean[pair : pair + 1, span] = average
            rounded = (values - average).astype(BF16)
            perturb[pair, :, span] = rounded
            for side, coef in enumerate(column_coefs()):
                scaled = coef[:, span] * rounded.astype(F32)
                sides[pair, side * K : (side + 1) * K, span] = scaled.astype(BF16)


def perturbations(state):
    pairs = state.shape[0] // 2
    return pl.pallas_call(
        perturb_kernel,
        out_shape=[
            jax.ShapeDtypeStruct((pairs, 2 * K), F32),
            jax.ShapeDtypeStruct((pairs, K, 2 * K), BF16),
            jax.ShapeDtypeStruct((pairs, 2 * K, 2 * K), BF16),
        ],
        in_specs=in_vmem(1),
        out_specs=in_vmem(3),
        compiler_params=params(),
        cost_estimate=cost(LONG),
    )(state)


def own_kernel(own, mean, perturb, out):
    left_coef, right_coef = column_coefs()
    own_coef = 1.0 - left_coef - right_coef
    for pair in range(mean.shape[0]):
        sums = jnp.dot(own[...], perturb[pair], preferred_element_type=F32)
        out[pair] = mean[pair : pair + 1] + own_coef * sums


def own_part(own, mean, perturb):
    return pl.pallas_call(
        own_kernel,
        out_shape=jax.ShapeDtypeStruct(perturb.shape, F32),
        in_specs=in_vmem(3),
        out_specs=in_vmem(1)[0],
        compiler_params=params(),
        cost_estimate=cost(2e9),
    )(own, mean, perturb)


def side_kernel(beyond, beside, part, sides, out, held, sems):
    first_core = lax.rem(lax.axis_index("grid"), CORES) == 0
    left = jnp.where(first_core, beyond[...], beside[...])
    right = jnp.where(first_core, beside[...], beyond[...])
    weights = jnp.concatenate([left, right], axis=1)
    chunks = sems.shape[0]
    pairs = sides.shape[0] // chunks
    copies = []
    for chunk in range(chunks):
        for pair in range(chunk * pairs, (chunk + 1) * pairs):
            total = part[pair] + jnp.dot(weights, sides[pair], preferred_element_type=F32)
            total = total.astype(BF16)
            for i in range(2):
                held[2 * pair + i] = total[:, i * K : (i + 1) * K]
        rows = pl.ds(2 * chunk * pairs, 2 * pairs)
        copies.append(pltpu.make_async_copy(held.at[rows], out.at[rows], sems.at[chunk]))
        copies[-1].start()
    for copy in copies:
        copy.wait()


def add_sides(beyond, beside, part, sides):
    shape = (2 * sides.shape[0], K, K)
    return pl.pallas_call(
        side_kernel,
        out_shape=jax.ShapeDtypeStruct(shape, BF16),
        in_specs=in_vmem(4),
        out_specs=pl.BlockSpec(memory_space=pltpu.HBM),
        scratch_shapes=[pltpu.VMEM(shape, BF16), pltpu.SemaphoreType.DMA((12,))],
        compiler_params=params(),
        cost_estimate=cost(2e9),
    )(beyond, beside, part, sides)


def on_device(departures, innovation, obs_weight, send_rows, send_counts, state):
    n_grid = lax.axis_size("grid")
    low_half, high_half, near = make_messages(
        departures, innovation, obs_weight, send_rows[0].T
    )
    left = hop(low_half, 0, 1, 0)
    right = hop(high_half, 0, -1, 0)
    other = hop(near, 0, 0, 1)

    whole = lambda which: ((0, which, 0), (1, which, HALF))
    found = pick_rows(
        ((whole(0), (0, 0, 8), None), (whole(1), (1, 0, 12), None)), SHORT, near, other
    )
    mean, perturb, sides = perturbations(state)
    low_half, high_half, mean, perturb, sides = lax.optimization_barrier(
        (low_half, high_half, mean, perturb, sides)
    )
    left_more = hop(high_half, 0, 1, 0)
    right_more = hop(low_half, 0, -1, 0)
    left, found, mean, perturb = lax.optimization_barrier((left, found, mean, perturb))
    far_low = hop(left, 0, 1, 0)
    left, right, found = lax.optimization_barrier((left, right, found))
    far_high = hop(right, 0, -1, 0)

    def firsts(core):
        row = 8 + 4 * core
        return (((0, 0, 0),), (0, 0, row), None), (((1, 1, 0),), (1, 0, row), None)

    def seconds(core):
        row = 8 + 4 * core
        return (((1, 2, 0),), (0, 0, row), 4), (((0, 3, 0),), (1, 0, row), 5)

    same = pick_rows(firsts(0), SHORT, left, right)
    left, right, same = lax.optimization_barrier((left, right, same))
    left_other, right_other = hop(left, 0, 0, 1), hop(right, 0, 0, 1)
    same = pick_rows(seconds(0), LONG, left, right, left_more, right_more, *same)
    left_more, right_more, same = lax.optimization_barrier((left_more, right_more, same))
    left_more_other, right_more_other = hop(left_more, 0, 0, 1), hop(right_more, 0, 0, 1)
    cross = pick_rows(firsts(1), LONG, left_other, right_other)
    cross = pick_rows(
        seconds(1), SHORT, left_other, right_other, left_more_other, right_more_other, *cross
    )
    far_low, far_high, cross = lax.optimization_barrier((far_low, far_high, cross))
    far_low_other, far_high_other = hop(far_low, 0, 0, 1), hop(far_high, 0, 0, 1)
    far = pick_rows(((((0, 0, 0), (1, 1, 0)), (0, 0, 4), None),), SHORT, far_low, far_high)[0]
    last = (far_low_other, far_high_other, far, *found, same[0], cross[0], same[1], cross[1])

    across = last_grams((2,), BF16, *last)[0]
    from_across = hop(across, 2, 0, 0)
    from_up = hop(last_grams((1,), BF16, *last)[0], 1, 0, 0)
    from_down = hop(last_grams((3,), BF16, *last)[0], -1, 0, 0)
    own = last_grams((0,), F32, *last)[0]
    parts = sum_parts(own, from_across, from_up, from_down)
    parts = lax.all_to_all(parts, "obs", 0, 0, tiled=True)

    own = transposed_weights(parts)
    beyond = lax.ppermute(own, "grid", [(j, (j + 2 * (j % 2) - 1) % n_grid) for j in range(n_grid)])
    part = own_part(own, mean, perturb)
    own, part = lax.optimization_barrier((own, part))
    beside = hop(own, 0, 0, 1)
    return add_sides(beyond, beside, part, sides)


def solution(mesh):
    in_specs = (
        P(("obs", "grid"), None),
        P(("obs", "grid")),
        P(("obs", "grid")),
        P(("obs", "grid"), None, None),
        P(("obs", "grid"), None),
        P("obs", None, "grid"),
    )
    out_specs = P("obs", None, "grid")
    return jax.shard_map(
        on_device, mesh=mesh, in_specs=in_specs, out_specs=out_specs, check_vma=False
    )
```

```python
import functools

import jax
import jax.numpy as jnp
from jax import lax
from jax.experimental import pallas as pl
from jax.experimental.pallas import tpu as pltpu
from jax.sharding import PartitionSpec as P

ITERS = 6
Y, X, CORES = 4, 4, 2
F32, BF16 = jnp.float32, jnp.bfloat16
K = 128
LOW = 512
BLOCKS = 4
HALF = 2 * K + 16
PACK = 80
VMEM = 20 * 1024 * 1024


def params():
    return pltpu.CompilerParams(vmem_limit_bytes=VMEM)


LONG, SHORT = 6e10, 1e6
AWAY = (1, 2, 3)


def cost(flops):
    return pl.CostEstimate(flops=int(flops), bytes_accessed=100_000, transcendentals=0)


def in_vmem(count):
    return [pl.BlockSpec(memory_space=pltpu.VMEM)] * count


def hop(value, dy, dx, dc):
    pairs = []
    for place in range(Y * X * CORES):
        y, x, c = place // (X * CORES), place // CORES % X, place % CORES
        pairs.append((place, ((y + dy) % Y * X + (x + dx) % X) * CORES + (c ^ dc)))
    return lax.ppermute(value, "grid", pairs)


def dims(m, n):
    return (((m,), (n,)), ((), ()))


def send_picks(turned, cx, swapped):
    lines = []
    for y in range(Y):
        rows = turned[pl.ds(y * X * CORES + cx, 8, stride=Y * X * CORES), :]
        pair = [rows[0:4], rows[4:8]]
        pairs = jnp.concatenate(pair[::-1] if swapped else pair, axis=1)
        fours = jnp.concatenate([pairs[0:2], pairs[2:4]], axis=1)
        lines.append(jnp.concatenate([fours[0:1], fours[1:2]], axis=1))
    picks = jnp.concatenate(lines, axis=0)
    power = jnp.maximum(lax.shift_right_arithmetic(picks, 7), 0)
    code = lax.shift_left(128 + jnp.bitwise_and(picks, 127), power)
    return jnp.where(picks >= 0, code, 0).astype(F32)


def read_picks(rows):
    left = rows.astype(F32)
    high = jnp.zeros_like(left)
    for step in (8, 4, 2, 1):
        large = left >= 128.0 * 2**step
        left = jnp.where(large, left * 0.5**step, left)
        high = jnp.where(large, high + step, high)
    return jnp.where(left > 0.0, left - 128.0 + 128.0 * high, -1.0).astype(jnp.int32)


def message_kernel(departures, innovation, obs_weight, send_rows, *refs):
    outs, (rows, innov, weight, picks, turned) = refs[:3], refs[3:8]
    built, in_sems = outs, refs[8]
    small = ((send_rows, picks), (obs_weight, weight), (innovation, innov))
    small = [pltpu.make_async_copy(*pair, in_sems.at[i]) for i, pair in enumerate(small)]
    large = []
    for block in range(BLOCKS):
        span = pl.ds(block * LOW, LOW)
        large.append(
            pltpu.make_async_copy(departures.at[span], rows.at[span], in_sems.at[3 + block])
        )
    for copy in small + large:
        copy.start()
    small[0].wait()
    grid = lax.axis_index("grid")
    x, c = lax.rem(lax.div(grid, CORES), X), lax.rem(grid, CORES)
    turned[...] = picks[...].T
    groups = []
    for dx in range(X):
        for dc in range(CORES):
            cx = lax.rem(x + dx, X) * CORES + lax.rem(c + dc, CORES)
            groups.append(send_picks(turned, cx, dc == 1))
    small[1].wait()
    small[2].wait()
    root = jnp.sqrt(weight[...].reshape(1, BLOCKS * LOW))
    scaled = innov[...].reshape(1, BLOCKS * LOW) * root
    blank = jnp.zeros((2, LOW), F32)
    both = built[2]
    for half in range(2):
        one = built[half]
        at = half * HALF
        innovs = []
        for block in range(2):
            start = (2 * half + block) * LOW
            span = slice(start, start + LOW)
            large[2 * half + block].wait()
            part = (rows[span, :].astype(F32).T * root[:, span]).astype(BF16)
            one[block * K : (block + 1) * K, :] = part
            both[at + block * K : at + (block + 1) * K, :] = part
            innovs.append(scaled[:, span])
        top = innovs + [blank, groups[4 + half]]
        next_one = groups[2:4] if half == 0 else groups[6:8]
        one[2 * K :, :] = jnp.concatenate(top + next_one, axis=0).astype(BF16)
        both[at + 2 * K : at + HALF, :] = jnp.concatenate(top + groups[0:2], axis=0).astype(BF16)


def make_messages(*args):
    shapes = [(HALF, LOW), (HALF, LOW), (2 * HALF, LOW)]
    hbm = pl.BlockSpec(memory_space=pltpu.HBM)
    return pl.pallas_call(
        message_kernel,
        out_shape=[jax.ShapeDtypeStruct(shape, BF16) for shape in shapes],
        in_specs=[hbm] * 4,
        out_specs=in_vmem(3),
        scratch_shapes=[pltpu.VMEM(arg.shape, arg.dtype) for arg in args]
        + [pltpu.VMEM(args[3].shape[::-1], jnp.int32)]
        + [pltpu.SemaphoreType.DMA((3 + BLOCKS,))],
        compiler_params=pltpu.CompilerParams(vmem_limit_bytes=VMEM),
        cost_estimate=cost(2e9),
    )(*[pltpu.with_memory_space_constraint(arg, pltpu.HBM) for arg in args])


def pick(parts, picks):
    high = lax.shift_right_arithmetic(picks, 9)
    first = parts[0][0]
    live = picks >= 0 if len(parts) == 2 else lax.shift_right_arithmetic(high, 1) == first
    low = jnp.where(live, jnp.bitwise_and(picks, LOW - 1), -1)
    place = lax.broadcasted_iota(jnp.int32, (LOW, 256), 0).astype(jnp.int16)
    low = jnp.broadcast_to(low, (LOW, 256)).astype(jnp.int16)
    one_hot = jnp.where(place == low, jnp.ones((), BF16), jnp.zeros((), BF16))
    blocks, innovs = [], []
    for _, rows in parts:
        found = jnp.dot(rows, one_hot, preferred_element_type=F32)
        blocks += [found[:K], found[K : 2 * K]]
        innovs += [found[2 * K : 2 * K + 1], found[2 * K + 1 : 2 * K + 2]]
    members, innov = blocks[0], innovs[0]
    for block in range(1, len(blocks)):
        here = high == 2 * first + block
        members = jnp.where(here, blocks[block], members)
        innov = jnp.where(here, innovs[block], innov)
    return jnp.concatenate([members, jnp.broadcast_to(innov, (16, 256))], axis=0).astype(BF16)


def tail_picks(ref, at, row):
    return read_picks(ref[at + 2 * K : at + HALF, :].astype(F32)[row : row + 4])


def pick_kernel(sources, shifts, count, *refs):
    outs, scratch = refs[count:-1], refs[-1]
    place = lax.div(lax.axis_index("grid"), X * CORES)
    for n, (_, (which, at, row), _) in enumerate(sources):
        scratch[n] = tail_picks(refs[which], at, row)
    for shift in shifts:
        y = lax.rem(place + shift, Y)
        for i in range(2):
            span = slice(i * 256, i * 256 + 256)
            for n, (out, (parts, _, before)) in enumerate(zip(outs, sources)):
                tables = [(half, refs[which][at : at + HALF, :]) for half, which, at in parts]
                found = pick(tables, scratch[n, pl.ds(y, 1), :][:, span])
                out[2 * y + i] = found if before is None else found + refs[before][2 * y + i]


def pick_rows(sources, shifts, flops, *args):
    return pl.pallas_call(
        functools.partial(pick_kernel, sources, shifts, len(args)),
        out_shape=[jax.ShapeDtypeStruct((2 * Y, 144, 256), BF16)] * len(sources),
        in_specs=in_vmem(len(args)),
        out_specs=in_vmem(len(sources)),
        scratch_shapes=[pltpu.VMEM((len(sources), Y, LOW), jnp.int32)],
        compiler_params=params(),
        cost_estimate=cost(flops),
    )(*args)


def join(first, second):
    low = lax.broadcasted_iota(jnp.int32, first.shape, 1) < K // 2
    return jnp.where(low, first, second), jnp.where(low, second, first)


def pack(total):
    row = lax.broadcasted_iota(jnp.int32, (64, K), 0)
    lane = lax.broadcasted_iota(jnp.int32, (64, K), 1)
    lower = total[64:K]
    upper = jnp.where(lane < row, pltpu.roll(lower, 64, 1), total[0:64])
    diagonal = jnp.sum(jnp.where(lane == row + 64, lower, 0.0), axis=0, keepdims=True)
    return upper, diagonal, total[K : K + 1]


def unpack(packed):
    row = lax.broadcasted_iota(jnp.int32, (64, K), 0)
    lane = lax.broadcasted_iota(jnp.int32, (64, K), 1)
    upper = packed[0:64]
    above = jnp.where(lane > row, upper, 0.0)
    below = pltpu.roll(jnp.where(lane < row, upper, 0.0), 64, 1)
    off = jnp.concatenate([above, below], axis=0)
    low = jnp.where(lane == row + 64, packed[64:65], 0.0)
    diagonal = jnp.concatenate([jnp.where(lane == row, upper, 0.0), low], axis=0)
    return off + off.T + diagonal, packed[65:66]


def write_grams(out, i, shards, tail):
    tail_row = lax.broadcasted_iota(jnp.int32, (16, K), 0)
    for half in range(2):
        span = slice(half * K, half * K + K)
        pairs = [
            join(shards[n][:, span], shards[n + 1][:, span]) for n in range(0, len(shards), 2)
        ]
        for side in range(2):
            rows = jnp.concatenate([pair[side] for pair in pairs], axis=1)
            total = lax.dot_general(rows, rows[:K], dims(1, 1), preferred_element_type=F32)
            patch = i + 2 * half + 4 * side
            upper, diagonal, pull = pack(total)
            out[patch * 64 : patch * 64 + 64, :] = upper.astype(out.dtype)
            tail = jnp.where(tail_row == 2 * patch, diagonal, tail)
            tail = jnp.where(tail_row == 2 * patch + 1, pull, tail)
    return tail


def last_kernel(shifts, low, high, same, *rest):
    found, outs, picks = rest[:6], rest[6:-1], rest[-1]
    place = lax.div(lax.axis_index("grid"), X * CORES)
    picks[...] = tail_picks(high, 0, 4)
    table = ((0, low[...]), (1, high[...]))
    for out, shift in zip(outs, shifts):
        y = lax.rem(place + shift, Y)
        tail = jnp.zeros((16, K), F32)
        for i in range(2):
            span = slice(i * 256, i * 256 + 256)
            last = pick(table, picks[pl.ds(y, 1), :][:, span])
            shards = [ref[2 * y + i] for ref in (*found, same)] + [last]
            tail = write_grams(out, i, shards, tail)
        out[8 * 64 :, :] = tail.astype(out.dtype)


def own_grams_kernel(sources, *refs):
    found, tables, (out, scratch) = refs[:2], refs[2:-2], refs[-2:]
    y = lax.div(lax.axis_index("grid"), X * CORES)
    for n, (_, _, which, row) in enumerate(sources):
        scratch[n] = tail_picks(tables[which], 0, row)
    tail = jnp.zeros((16, K), F32)
    for i in range(2):
        span = slice(i * 256, i * 256 + 256)
        shards = [ref[2 * y + i] for ref in found]
        for n, (low, high, _, _) in enumerate(sources):
            parts = ((0, tables[low][...]), (1, tables[high][...]))
            shards.append(pick(parts, scratch[n, pl.ds(y, 1), :][:, span]))
        tail = write_grams(out, i, shards, tail)
    out[8 * 64 :, :] = tail


def own_grams(sources, *args):
    return pl.pallas_call(
        functools.partial(own_grams_kernel, sources),
        out_shape=jax.ShapeDtypeStruct((8 * 64 + 16, K), F32),
        in_specs=in_vmem(len(args)),
        out_specs=in_vmem(1)[0],
        scratch_shapes=[pltpu.VMEM((len(sources), Y, LOW), jnp.int32)],
        compiler_params=params(),
        cost_estimate=cost(1e9),
    )(*args)


def last_grams(shifts, dtype, *args):
    return pl.pallas_call(
        functools.partial(last_kernel, shifts),
        out_shape=[jax.ShapeDtypeStruct((8 * 64 + 16, K), dtype)] * len(shifts),
        in_specs=in_vmem(len(args)),
        out_specs=in_vmem(len(shifts)),
        scratch_shapes=[pltpu.VMEM((Y, LOW), jnp.int32)],
        compiler_params=params(),
        cost_estimate=cost(1e9 * len(shifts)),
    )(*args)


def sum_kernel(own, a, b, c, out):
    def total(span):
        return own[span, :] + (a[span, :].astype(F32) + b[span, :].astype(F32) + c[span, :].astype(F32))

    tails = total(slice(8 * 64, 8 * 64 + 16))
    first = lax.broadcasted_iota(jnp.int32, (16, K), 0) == 0
    for patch in range(8):
        out[patch, 0:64, :] = total(slice(patch * 64, patch * 64 + 64)).astype(BF16)
        tail = jnp.where(first, tails[2 * patch : 2 * patch + 1], tails[2 * patch + 1 : 2 * patch + 2])
        out[patch, 64:PACK, :] = tail.astype(BF16)


def sum_parts(*args):
    return pl.pallas_call(
        sum_kernel,
        out_shape=jax.ShapeDtypeStruct((8, PACK, K), BF16),
        in_specs=in_vmem(4),
        out_specs=in_vmem(1)[0],
        compiler_params=params(),
        cost_estimate=cost(5e8),
    )(*args)


def split(value):
    high = value.astype(BF16)
    return high, (value - high.astype(F32)).astype(BF16)


def product(left, right):
    lh, ll = split(left)
    rh, rl = split(right)
    return jnp.dot(
        jnp.concatenate([lh, lh, ll], axis=1),
        jnp.concatenate([rh, rl, rh], axis=0),
        preferred_element_type=F32,
    )


def weights_kernel(parts, out):
    gram, pull = unpack(jnp.sum(parts[...].astype(F32), axis=0))
    row = lax.broadcasted_iota(jnp.int32, (K, K), 0)
    col = lax.broadcasted_iota(jnp.int32, (K, K), 1)
    identity = (row == col).astype(F32)
    system = gram + (K - 1.0) * identity
    squares = jnp.sum(jnp.sum(system * system, axis=0, keepdims=True), axis=1, keepdims=True)
    frob = jnp.sqrt(squares)
    iterate = system / frob
    inverse = 1.5 * identity - 0.5 * iterate
    iterate = product(inverse, iterate)
    for sweep in range(1, ITERS):
        newton = 1.5 * identity - 0.5 * product(inverse, iterate)
        if sweep < ITERS - 1:
            both = product(newton, jnp.concatenate([iterate, inverse], axis=1))
            iterate, inverse = both[:, :K], both[:, K:]
        else:
            inverse = product(newton, inverse)
    shift = product(product(jnp.broadcast_to(pull, (16, K)), inverse), inverse)[0:1] / frob
    out[...] = (jnp.sqrt((K - 1.0) / frob) * inverse.T + shift).astype(BF16)


def transposed_weights(parts):
    return pl.pallas_call(
        weights_kernel,
        out_shape=jax.ShapeDtypeStruct((K, K), BF16),
        in_specs=in_vmem(1),
        out_specs=in_vmem(1)[0],
        compiler_params=params(),
        cost_estimate=cost(4e9),
    )(parts)


def column_coefs():
    position = lax.broadcasted_iota(jnp.int32, (1, 2 * K), 1) % K
    position = (position.astype(F32) + 0.5) / K
    return jnp.maximum(0.5 - position, 0.0), jnp.maximum(position - 0.5, 0.0)


def perturb_kernel(state, mean, perturb, sides):
    for pair in range(mean.shape[0]):
        for i in range(2):
            span = slice(i * K, (i + 1) * K)
            values = state[2 * pair + i].astype(F32)
            average = jnp.mean(values, axis=0, keepdims=True)
            mean[pair : pair + 1, span] = average
            rounded = (values - average).astype(BF16)
            perturb[pair, :, span] = rounded
            for side, coef in enumerate(column_coefs()):
                scaled = coef[:, span] * rounded.astype(F32)
                sides[pair, side * K : (side + 1) * K, span] = scaled.astype(BF16)


def perturbations(state):
    pairs = state.shape[0] // 2
    return pl.pallas_call(
        perturb_kernel,
        out_shape=[
            jax.ShapeDtypeStruct((pairs, 2 * K), F32),
            jax.ShapeDtypeStruct((pairs, K, 2 * K), BF16),
            jax.ShapeDtypeStruct((pairs, 2 * K, 2 * K), BF16),
        ],
        in_specs=in_vmem(1),
        out_specs=in_vmem(3),
        compiler_params=params(),
        cost_estimate=cost(LONG),
    )(state)


def own_kernel(own, mean, perturb, out):
    left_coef, right_coef = column_coefs()
    own_coef = 1.0 - left_coef - right_coef
    for pair in range(mean.shape[0]):
        sums = jnp.dot(own[...], perturb[pair], preferred_element_type=F32)
        out[pair] = mean[pair : pair + 1] + own_coef * sums


def own_part(own, mean, perturb):
    return pl.pallas_call(
        own_kernel,
        out_shape=jax.ShapeDtypeStruct(perturb.shape, F32),
        in_specs=in_vmem(3),
        out_specs=in_vmem(1)[0],
        compiler_params=params(),
        cost_estimate=cost(2e9),
    )(own, mean, perturb)


def side_kernel(beyond, beside, part, sides, out, held, sems):
    first_core = lax.rem(lax.axis_index("grid"), CORES) == 0
    left = jnp.where(first_core, beyond[...], beside[...])
    right = jnp.where(first_core, beside[...], beyond[...])
    weights = jnp.concatenate([left, right], axis=1)
    chunks = sems.shape[0]
    pairs = sides.shape[0] // chunks
    copies = []
    for chunk in range(chunks):
        for pair in range(chunk * pairs, (chunk + 1) * pairs):
            total = part[pair] + jnp.dot(weights, sides[pair], preferred_element_type=F32)
            total = total.astype(BF16)
            for i in range(2):
                held[2 * pair + i] = total[:, i * K : (i + 1) * K]
        rows = pl.ds(2 * chunk * pairs, 2 * pairs)
        copies.append(pltpu.make_async_copy(held.at[rows], out.at[rows], sems.at[chunk]))
        copies[-1].start()
    for copy in copies:
        copy.wait()


def add_sides(beyond, beside, part, sides):
    shape = (2 * sides.shape[0], K, K)
    return pl.pallas_call(
        side_kernel,
        out_shape=jax.ShapeDtypeStruct(shape, BF16),
        in_specs=in_vmem(4),
        out_specs=pl.BlockSpec(memory_space=pltpu.HBM),
        scratch_shapes=[pltpu.VMEM(shape, BF16), pltpu.SemaphoreType.DMA((12,))],
        compiler_params=params(),
        cost_estimate=cost(2e9),
    )(beyond, beside, part, sides)


def on_device(departures, innovation, obs_weight, send_rows, send_counts, state):
    n_grid = lax.axis_size("grid")
    low_half, high_half, near = make_messages(
        departures, innovation, obs_weight, send_rows[0].T
    )
    left = hop(low_half, 0, 1, 0)
    right = hop(high_half, 0, -1, 0)
    other = hop(near, 0, 0, 1)

    whole = lambda which: ((0, which, 0), (1, which, HALF))
    found = pick_rows(
        ((whole(0), (0, 0, 8), None), (whole(1), (1, 0, 12), None)), (0, 1, 2, 3), SHORT, near, other
    )
    mean, perturb, sides = perturbations(state)
    low_half, high_half, mean, perturb, sides = lax.optimization_barrier(
        (low_half, high_half, mean, perturb, sides)
    )
    left_more = hop(high_half, 0, 1, 0)
    right_more = hop(low_half, 0, -1, 0)
    left, found, mean, perturb = lax.optimization_barrier((left, found, mean, perturb))
    far_low = hop(left, 0, 1, 0)
    left, right, found = lax.optimization_barrier((left, right, found))
    far_high = hop(right, 0, -1, 0)

    def firsts(core):
        row = 8 + 4 * core
        return (((0, 0, 0),), (0, 0, row), None), (((1, 1, 0),), (1, 0, row), None)

    def seconds(core):
        row = 8 + 4 * core
        return (((1, 2, 0),), (0, 0, row), 4), (((0, 3, 0),), (1, 0, row), 5)

    same = pick_rows(firsts(0), AWAY, SHORT, left, right)
    left, right, same = lax.optimization_barrier((left, right, same))
    left_other, right_other = hop(left, 0, 0, 1), hop(right, 0, 0, 1)
    same = pick_rows(seconds(0), AWAY, LONG, left, right, left_more, right_more, *same)
    left_more, right_more, same = lax.optimization_barrier((left_more, right_more, same))
    left_more_other, right_more_other = hop(left_more, 0, 0, 1), hop(right_more, 0, 0, 1)
    cross = pick_rows(firsts(1), AWAY, LONG, left_other, right_other)
    cross = pick_rows(
        seconds(1), AWAY, SHORT, left_other, right_other, left_more_other, right_more_other, *cross
    )
    far_low, far_high, cross = lax.optimization_barrier((far_low, far_high, cross))
    far_low_other, far_high_other = hop(far_low, 0, 0, 1), hop(far_high, 0, 0, 1)
    far = pick_rows(((((0, 0, 0), (1, 1, 0)), (0, 0, 4), None),), AWAY, SHORT, far_low, far_high)[0]
    last = (far_low_other, far_high_other, far, *found, same[0], cross[0], same[1], cross[1])

    across = last_grams((2,), BF16, *last)[0]
    from_across = hop(across, 2, 0, 0)
    from_up = hop(last_grams((1,), BF16, *last)[0], 1, 0, 0)
    from_down = hop(last_grams((3,), BF16, *last)[0], -1, 0, 0)
    sources = ((0, 2, 0, 8), (1, 3, 1, 12), (6, 4, 4, 8), (7, 5, 5, 12), (8, 9, 8, 4), (10, 11, 11, 4))
    own = own_grams(
        sources,
        *found,
        left,
        left_other,
        left_more,
        left_more_other,
        right,
        right_other,
        right_more,
        right_more_other,
        far_low,
        far_high,
        far_low_other,
        far_high_other,
    )
    parts = sum_parts(own, from_across, from_up, from_down)
    parts = lax.all_to_all(parts, "obs", 0, 0, tiled=True)

    own = transposed_weights(parts)
    beyond = lax.ppermute(own, "grid", [(j, (j + 2 * (j % 2) - 1) % n_grid) for j in range(n_grid)])
    part = own_part(own, mean, perturb)
    own, part = lax.optimization_barrier((own, part))
    beside = hop(own, 0, 0, 1)
    return add_sides(beyond, beside, part, sides)


def solution(mesh):
    in_specs = (
        P(("obs", "grid"), None),
        P(("obs", "grid")),
        P(("obs", "grid")),
        P(("obs", "grid"), None, None),
        P(("obs", "grid"), None),
        P("obs", None, "grid"),
    )
    out_specs = P("obs", None, "grid")
    return jax.shard_map(
        on_device, mesh=mesh, in_specs=in_specs, out_specs=out_specs, check_vma=False
    )
```

```python
import functools

import jax
import jax.numpy as jnp
from jax import lax
from jax.experimental import pallas as pl
from jax.experimental.pallas import tpu as pltpu
from jax.sharding import PartitionSpec as P

ITERS = 6
Y, X, CORES = 4, 4, 2
F32, BF16 = jnp.float32, jnp.bfloat16
K = 128
LOW = 512
BLOCKS = 4
HALF = 2 * K + 16
PACK = 80
VMEM = 20 * 1024 * 1024


def params():
    return pltpu.CompilerParams(vmem_limit_bytes=VMEM)


LONG, SHORT = 6e10, 1e6
AWAY = (1, 2, 3)


def cost(flops):
    return pl.CostEstimate(flops=int(flops), bytes_accessed=100_000, transcendentals=0)


def in_vmem(count):
    return [pl.BlockSpec(memory_space=pltpu.VMEM)] * count


def hop(value, dy, dx, dc):
    pairs = []
    for place in range(Y * X * CORES):
        y, x, c = place // (X * CORES), place // CORES % X, place % CORES
        pairs.append((place, ((y + dy) % Y * X + (x + dx) % X) * CORES + (c ^ dc)))
    return lax.ppermute(value, "grid", pairs)


def dims(m, n):
    return (((m,), (n,)), ((), ()))


def send_picks(turned, cx, swapped):
    lines = []
    for y in range(Y):
        rows = turned[pl.ds(y * X * CORES + cx, 8, stride=Y * X * CORES), :]
        pair = [rows[0:4], rows[4:8]]
        pairs = jnp.concatenate(pair[::-1] if swapped else pair, axis=1)
        fours = jnp.concatenate([pairs[0:2], pairs[2:4]], axis=1)
        lines.append(jnp.concatenate([fours[0:1], fours[1:2]], axis=1))
    picks = jnp.concatenate(lines, axis=0)
    power = jnp.maximum(lax.shift_right_arithmetic(picks, 7), 0)
    code = lax.shift_left(128 + jnp.bitwise_and(picks, 127), power)
    return jnp.where(picks >= 0, code, 0).astype(F32)


def read_picks(rows):
    left = rows.astype(F32)
    high = jnp.zeros_like(left)
    for step in (8, 4, 2, 1):
        large = left >= 128.0 * 2**step
        left = jnp.where(large, left * 0.5**step, left)
        high = jnp.where(large, high + step, high)
    return jnp.where(left > 0.0, left - 128.0 + 128.0 * high, -1.0).astype(jnp.int32)


def message_kernel(departures, innovation, obs_weight, send_rows, *refs):
    outs, (rows, innov, weight, picks, turned) = refs[:3], refs[3:8]
    built, in_sems = outs, refs[8]
    small = ((send_rows, picks), (obs_weight, weight), (innovation, innov))
    small = [pltpu.make_async_copy(*pair, in_sems.at[i]) for i, pair in enumerate(small)]
    large = []
    for block in range(BLOCKS):
        span = pl.ds(block * LOW, LOW)
        large.append(
            pltpu.make_async_copy(departures.at[span], rows.at[span], in_sems.at[3 + block])
        )
    for copy in small + large:
        copy.start()
    small[0].wait()
    grid = lax.axis_index("grid")
    x, c = lax.rem(lax.div(grid, CORES), X), lax.rem(grid, CORES)
    turned[...] = picks[...].T
    groups = []
    for dx in range(X):
        for dc in range(CORES):
            cx = lax.rem(x + dx, X) * CORES + lax.rem(c + dc, CORES)
            groups.append(send_picks(turned, cx, dc == 1))
    small[1].wait()
    small[2].wait()
    root = jnp.sqrt(weight[...].reshape(1, BLOCKS * LOW))
    scaled = innov[...].reshape(1, BLOCKS * LOW) * root
    blank = jnp.zeros((2, LOW), F32)
    both = built[2]
    for half in range(2):
        one = built[half]
        at = half * HALF
        innovs = []
        for block in range(2):
            start = (2 * half + block) * LOW
            span = slice(start, start + LOW)
            large[2 * half + block].wait()
            part = (rows[span, :].astype(F32).T * root[:, span]).astype(BF16)
            one[block * K : (block + 1) * K, :] = part
            both[at + block * K : at + (block + 1) * K, :] = part
            innovs.append(scaled[:, span])
        top = innovs + [blank, groups[4 + half]]
        next_one = groups[2:4] if half == 0 else groups[6:8]
        one[2 * K :, :] = jnp.concatenate(top + next_one, axis=0).astype(BF16)
        both[at + 2 * K : at + HALF, :] = jnp.concatenate(top + groups[0:2], axis=0).astype(BF16)


def make_messages(*args):
    shapes = [(HALF, LOW), (HALF, LOW), (2 * HALF, LOW)]
    hbm = pl.BlockSpec(memory_space=pltpu.HBM)
    return pl.pallas_call(
        message_kernel,
        out_shape=[jax.ShapeDtypeStruct(shape, BF16) for shape in shapes],
        in_specs=[hbm] * 4,
        out_specs=in_vmem(3),
        scratch_shapes=[pltpu.VMEM(arg.shape, arg.dtype) for arg in args]
        + [pltpu.VMEM(args[3].shape[::-1], jnp.int32)]
        + [pltpu.SemaphoreType.DMA((3 + BLOCKS,))],
        compiler_params=pltpu.CompilerParams(vmem_limit_bytes=VMEM),
        cost_estimate=cost(2e9),
    )(*[pltpu.with_memory_space_constraint(arg, pltpu.HBM) for arg in args])


def pick(parts, picks):
    high = lax.shift_right_arithmetic(picks, 9)
    first = parts[0][0]
    live = picks >= 0 if len(parts) == 2 else lax.shift_right_arithmetic(high, 1) == first
    low = jnp.where(live, jnp.bitwise_and(picks, LOW - 1), -1)
    place = lax.broadcasted_iota(jnp.int32, (LOW, 256), 0).astype(jnp.int16)
    low = jnp.broadcast_to(low, (LOW, 256)).astype(jnp.int16)
    one_hot = jnp.where(place == low, jnp.ones((), BF16), jnp.zeros((), BF16))
    blocks, innovs = [], []
    for _, rows in parts:
        found = jnp.dot(rows, one_hot, preferred_element_type=F32)
        blocks += [found[:K], found[K : 2 * K]]
        innovs += [found[2 * K : 2 * K + 1], found[2 * K + 1 : 2 * K + 2]]
    members, innov = blocks[0], innovs[0]
    for block in range(1, len(blocks)):
        here = high == 2 * first + block
        members = jnp.where(here, blocks[block], members)
        innov = jnp.where(here, innovs[block], innov)
    return jnp.concatenate([members, jnp.broadcast_to(innov, (16, 256))], axis=0).astype(BF16)


def tail_picks(ref, at, row):
    return read_picks(ref[at + 2 * K : at + HALF, :].astype(F32)[row : row + 4])


def pick_kernel(sources, shifts, count, *refs):
    outs, scratch = refs[count:-1], refs[-1]
    place = lax.div(lax.axis_index("grid"), X * CORES)
    for n, (_, (which, at, row), _) in enumerate(sources):
        scratch[n] = tail_picks(refs[which], at, row)
    for shift in shifts:
        y = lax.rem(place + shift, Y)
        for i in range(2):
            span = slice(i * 256, i * 256 + 256)
            for n, (out, (parts, _, before)) in enumerate(zip(outs, sources)):
                tables = [(half, refs[which][at : at + HALF, :]) for half, which, at in parts]
                found = pick(tables, scratch[n, pl.ds(y, 1), :][:, span])
                out[2 * y + i] = found if before is None else found + refs[before][2 * y + i]


def pick_rows(sources, shifts, flops, *args):
    return pl.pallas_call(
        functools.partial(pick_kernel, sources, shifts, len(args)),
        out_shape=[jax.ShapeDtypeStruct((2 * Y, 144, 256), BF16)] * len(sources),
        in_specs=in_vmem(len(args)),
        out_specs=in_vmem(len(sources)),
        scratch_shapes=[pltpu.VMEM((len(sources), Y, LOW), jnp.int32)],
        compiler_params=params(),
        cost_estimate=cost(flops),
    )(*args)


def join(first, second):
    low = lax.broadcasted_iota(jnp.int32, first.shape, 1) < K // 2
    return jnp.where(low, first, second), jnp.where(low, second, first)


def pack(total):
    row = lax.broadcasted_iota(jnp.int32, (64, K), 0)
    lane = lax.broadcasted_iota(jnp.int32, (64, K), 1)
    lower = total[64:K]
    upper = jnp.where(lane < row, pltpu.roll(lower, 64, 1), total[0:64])
    diagonal = jnp.sum(jnp.where(lane == row + 64, lower, 0.0), axis=0, keepdims=True)
    return upper, diagonal, total[K : K + 1]


def unpack(packed):
    row = lax.broadcasted_iota(jnp.int32, (64, K), 0)
    lane = lax.broadcasted_iota(jnp.int32, (64, K), 1)
    upper = packed[0:64]
    above = jnp.where(lane > row, upper, 0.0)
    below = pltpu.roll(jnp.where(lane < row, upper, 0.0), 64, 1)
    off = jnp.concatenate([above, below], axis=0)
    low = jnp.where(lane == row + 64, packed[64:65], 0.0)
    diagonal = jnp.concatenate([jnp.where(lane == row, upper, 0.0), low], axis=0)
    return off + off.T + diagonal, packed[65:66]


def write_grams(out, i, shards, tail):
    tail_row = lax.broadcasted_iota(jnp.int32, (16, K), 0)
    for half in range(2):
        span = slice(half * K, half * K + K)
        pairs = [
            join(shards[n][:, span], shards[n + 1][:, span]) for n in range(0, len(shards), 2)
        ]
        for side in range(2):
            rows = jnp.concatenate([pair[side] for pair in pairs], axis=1)
            total = lax.dot_general(rows, rows[:K], dims(1, 1), preferred_element_type=F32)
            patch = i + 2 * half + 4 * side
            upper, diagonal, pull = pack(total)
            out[patch * 64 : patch * 64 + 64, :] = upper.astype(out.dtype)
            tail = jnp.where(tail_row == 2 * patch, diagonal, tail)
            tail = jnp.where(tail_row == 2 * patch + 1, pull, tail)
    return tail


def last_kernel(shifts, low, high, same, *rest):
    found, outs, picks = rest[:6], rest[6:-1], rest[-1]
    place = lax.div(lax.axis_index("grid"), X * CORES)
    picks[...] = tail_picks(high, 0, 4)
    table = ((0, low[...]), (1, high[...]))
    for out, shift in zip(outs, shifts):
        y = lax.rem(place + shift, Y)
        tail = jnp.zeros((16, K), F32)
        for i in range(2):
            span = slice(i * 256, i * 256 + 256)
            last = pick(table, picks[pl.ds(y, 1), :][:, span])
            shards = [ref[2 * y + i] for ref in (*found, same)] + [last]
            tail = write_grams(out, i, shards, tail)
        out[8 * 64 :, :] = tail.astype(out.dtype)


def own_grams_kernel(sources, *refs):
    found, tables, (same, out, scratch) = refs[:2], refs[2:-3], refs[-3:]
    y = lax.div(lax.axis_index("grid"), X * CORES)
    for n, (_, _, which, row) in enumerate(sources):
        scratch[n] = tail_picks(tables[which], 0, row)
    tail = jnp.zeros((16, K), F32)
    for i in range(2):
        span = slice(i * 256, i * 256 + 256)
        shards = [ref[2 * y + i] for ref in found]
        for n, (low, high, _, _) in enumerate(sources):
            parts = ((0, tables[low][...]), (1, tables[high][...]))
            shards.append(pick(parts, scratch[n, pl.ds(y, 1), :][:, span]))
        shards.insert(-1, same[2 * y + i])
        tail = write_grams(out, i, shards, tail)
    out[8 * 64 :, :] = tail


def own_grams(sources, *args):
    return pl.pallas_call(
        functools.partial(own_grams_kernel, sources),
        out_shape=jax.ShapeDtypeStruct((8 * 64 + 16, K), F32),
        in_specs=in_vmem(len(args)),
        out_specs=in_vmem(1)[0],
        scratch_shapes=[pltpu.VMEM((len(sources), Y, LOW), jnp.int32)],
        compiler_params=params(),
        cost_estimate=cost(1e9),
    )(*args)


def last_grams(shifts, dtype, *args):
    return pl.pallas_call(
        functools.partial(last_kernel, shifts),
        out_shape=[jax.ShapeDtypeStruct((8 * 64 + 16, K), dtype)] * len(shifts),
        in_specs=in_vmem(len(args)),
        out_specs=in_vmem(len(shifts)),
        scratch_shapes=[pltpu.VMEM((Y, LOW), jnp.int32)],
        compiler_params=params(),
        cost_estimate=cost(1e9 * len(shifts)),
    )(*args)


def sum_kernel(own, a, b, c, out):
    def total(span):
        return own[span, :] + (a[span, :].astype(F32) + b[span, :].astype(F32) + c[span, :].astype(F32))

    tails = total(slice(8 * 64, 8 * 64 + 16))
    first = lax.broadcasted_iota(jnp.int32, (16, K), 0) == 0
    for patch in range(8):
        out[patch, 0:64, :] = total(slice(patch * 64, patch * 64 + 64)).astype(BF16)
        tail = jnp.where(first, tails[2 * patch : 2 * patch + 1], tails[2 * patch + 1 : 2 * patch + 2])
        out[patch, 64:PACK, :] = tail.astype(BF16)


def sum_parts(*args):
    return pl.pallas_call(
        sum_kernel,
        out_shape=jax.ShapeDtypeStruct((8, PACK, K), BF16),
        in_specs=in_vmem(4),
        out_specs=in_vmem(1)[0],
        compiler_params=params(),
        cost_estimate=cost(5e8),
    )(*args)


def split(value):
    high = value.astype(BF16)
    return high, (value - high.astype(F32)).astype(BF16)


def product(left, right):
    lh, ll = split(left)
    rh, rl = split(right)
    return jnp.dot(
        jnp.concatenate([lh, lh, ll], axis=1),
        jnp.concatenate([rh, rl, rh], axis=0),
        preferred_element_type=F32,
    )


def weights_kernel(parts, out):
    gram, pull = unpack(jnp.sum(parts[...].astype(F32), axis=0))
    row = lax.broadcasted_iota(jnp.int32, (K, K), 0)
    col = lax.broadcasted_iota(jnp.int32, (K, K), 1)
    identity = (row == col).astype(F32)
    system = gram + (K - 1.0) * identity
    squares = jnp.sum(jnp.sum(system * system, axis=0, keepdims=True), axis=1, keepdims=True)
    frob = jnp.sqrt(squares)
    iterate = system / frob
    inverse = 1.5 * identity - 0.5 * iterate
    iterate = product(inverse, iterate)
    for sweep in range(1, ITERS):
        newton = 1.5 * identity - 0.5 * product(inverse, iterate)
        if sweep < ITERS - 1:
            both = product(newton, jnp.concatenate([iterate, inverse], axis=1))
            iterate, inverse = both[:, :K], both[:, K:]
        else:
            inverse = product(newton, inverse)
    shift = product(product(jnp.broadcast_to(pull, (16, K)), inverse), inverse)[0:1] / frob
    out[...] = (jnp.sqrt((K - 1.0) / frob) * inverse.T + shift).astype(BF16)


def transposed_weights(parts):
    return pl.pallas_call(
        weights_kernel,
        out_shape=jax.ShapeDtypeStruct((K, K), BF16),
        in_specs=in_vmem(1),
        out_specs=in_vmem(1)[0],
        compiler_params=params(),
        cost_estimate=cost(4e9),
    )(parts)


def column_coefs():
    position = lax.broadcasted_iota(jnp.int32, (1, 2 * K), 1) % K
    position = (position.astype(F32) + 0.5) / K
    return jnp.maximum(0.5 - position, 0.0), jnp.maximum(position - 0.5, 0.0)


def perturb_kernel(state, mean, perturb, sides):
    for pair in range(mean.shape[0]):
        for i in range(2):
            span = slice(i * K, (i + 1) * K)
            values = state[2 * pair + i].astype(F32)
            average = jnp.mean(values, axis=0, keepdims=True)
            mean[pair : pair + 1, span] = average
            rounded = (values - average).astype(BF16)
            perturb[pair, :, span] = rounded
            for side, coef in enumerate(column_coefs()):
                scaled = coef[:, span] * rounded.astype(F32)
                sides[pair, side * K : (side + 1) * K, span] = scaled.astype(BF16)


def perturbations(state):
    pairs = state.shape[0] // 2
    return pl.pallas_call(
        perturb_kernel,
        out_shape=[
            jax.ShapeDtypeStruct((pairs, 2 * K), F32),
            jax.ShapeDtypeStruct((pairs, K, 2 * K), BF16),
            jax.ShapeDtypeStruct((pairs, 2 * K, 2 * K), BF16),
        ],
        in_specs=in_vmem(1),
        out_specs=in_vmem(3),
        compiler_params=params(),
        cost_estimate=cost(LONG),
    )(state)


def own_kernel(own, mean, perturb, out):
    left_coef, right_coef = column_coefs()
    own_coef = 1.0 - left_coef - right_coef
    for pair in range(mean.shape[0]):
        sums = jnp.dot(own[...], perturb[pair], preferred_element_type=F32)
        out[pair] = mean[pair : pair + 1] + own_coef * sums


def own_part(own, mean, perturb):
    return pl.pallas_call(
        own_kernel,
        out_shape=jax.ShapeDtypeStruct(perturb.shape, F32),
        in_specs=in_vmem(3),
        out_specs=in_vmem(1)[0],
        compiler_params=params(),
        cost_estimate=cost(2e9),
    )(own, mean, perturb)


def side_kernel(beyond, beside, part, sides, out, held, sems):
    first_core = lax.rem(lax.axis_index("grid"), CORES) == 0
    left = jnp.where(first_core, beyond[...], beside[...])
    right = jnp.where(first_core, beside[...], beyond[...])
    weights = jnp.concatenate([left, right], axis=1)
    chunks = sems.shape[0]
    pairs = sides.shape[0] // chunks
    copies = []
    for chunk in range(chunks):
        for pair in range(chunk * pairs, (chunk + 1) * pairs):
            total = part[pair] + jnp.dot(weights, sides[pair], preferred_element_type=F32)
            total = total.astype(BF16)
            for i in range(2):
                held[2 * pair + i] = total[:, i * K : (i + 1) * K]
        rows = pl.ds(2 * chunk * pairs, 2 * pairs)
        copies.append(pltpu.make_async_copy(held.at[rows], out.at[rows], sems.at[chunk]))
        copies[-1].start()
    for copy in copies:
        copy.wait()


def add_sides(beyond, beside, part, sides):
    shape = (2 * sides.shape[0], K, K)
    return pl.pallas_call(
        side_kernel,
        out_shape=jax.ShapeDtypeStruct(shape, BF16),
        in_specs=in_vmem(4),
        out_specs=pl.BlockSpec(memory_space=pltpu.HBM),
        scratch_shapes=[pltpu.VMEM(shape, BF16), pltpu.SemaphoreType.DMA((12,))],
        compiler_params=params(),
        cost_estimate=cost(2e9),
    )(beyond, beside, part, sides)


def on_device(departures, innovation, obs_weight, send_rows, send_counts, state):
    n_grid = lax.axis_size("grid")
    low_half, high_half, near = make_messages(
        departures, innovation, obs_weight, send_rows[0].T
    )
    left = hop(low_half, 0, 1, 0)
    right = hop(high_half, 0, -1, 0)
    other = hop(near, 0, 0, 1)

    whole = lambda which: ((0, which, 0), (1, which, HALF))
    found = pick_rows(
        ((whole(0), (0, 0, 8), None), (whole(1), (1, 0, 12), None)), (0, 1, 2, 3), SHORT, near, other
    )
    mean, perturb, sides = perturbations(state)
    low_half, high_half, mean, perturb, sides = lax.optimization_barrier(
        (low_half, high_half, mean, perturb, sides)
    )
    left_more = hop(high_half, 0, 1, 0)
    right_more = hop(low_half, 0, -1, 0)
    left, found, mean, perturb = lax.optimization_barrier((left, found, mean, perturb))
    far_low = hop(left, 0, 1, 0)
    left, right, found = lax.optimization_barrier((left, right, found))
    far_high = hop(right, 0, -1, 0)

    def firsts(core):
        row = 8 + 4 * core
        return (((0, 0, 0),), (0, 0, row), None), (((1, 1, 0),), (1, 0, row), None)

    def seconds(core):
        row = 8 + 4 * core
        return (((1, 2, 0),), (0, 0, row), 4), (((0, 3, 0),), (1, 0, row), 5)

    same = pick_rows(firsts(0), AWAY, SHORT, left, right)
    left, right, same = lax.optimization_barrier((left, right, same))
    left_other, right_other = hop(left, 0, 0, 1), hop(right, 0, 0, 1)
    same = pick_rows(seconds(0), AWAY, LONG, left, right, left_more, right_more, *same)
    left_more, right_more, same = lax.optimization_barrier((left_more, right_more, same))
    left_more_other, right_more_other = hop(left_more, 0, 0, 1), hop(right_more, 0, 0, 1)
    cross = pick_rows(firsts(1), AWAY, LONG, left_other, right_other)
    cross = pick_rows(
        seconds(1), AWAY, SHORT, left_other, right_other, left_more_other, right_more_other, *cross
    )
    far_low, far_high, cross = lax.optimization_barrier((far_low, far_high, cross))
    far_low_other, far_high_other = hop(far_low, 0, 0, 1), hop(far_high, 0, 0, 1)
    far = pick_rows(((((0, 0, 0), (1, 1, 0)), (0, 0, 4), None),), (0, 1, 2, 3), SHORT, far_low, far_high)[0]
    last = (far_low_other, far_high_other, far, *found, same[0], cross[0], same[1], cross[1])

    across = last_grams((2,), BF16, *last)[0]
    from_across = hop(across, 2, 0, 0)
    from_up = hop(last_grams((1,), BF16, *last)[0], 1, 0, 0)
    from_down = hop(last_grams((3,), BF16, *last)[0], -1, 0, 0)
    sources = ((0, 2, 0, 8), (1, 3, 1, 12), (6, 4, 4, 8), (7, 5, 5, 12), (10, 11, 11, 4))
    own = own_grams(
        sources,
        *found,
        left,
        left_other,
        left_more,
        left_more_other,
        right,
        right_other,
        right_more,
        right_more_other,
        far_low,
        far_high,
        far_low_other,
        far_high_other,
        far,
    )
    parts = sum_parts(own, from_across, from_up, from_down)
    parts = lax.all_to_all(parts, "obs", 0, 0, tiled=True)

    own = transposed_weights(parts)
    beyond = lax.ppermute(own, "grid", [(j, (j + 2 * (j % 2) - 1) % n_grid) for j in range(n_grid)])
    part = own_part(own, mean, perturb)
    own, part = lax.optimization_barrier((own, part))
    beside = hop(own, 0, 0, 1)
    return add_sides(beyond, beside, part, sides)


def solution(mesh):
    in_specs = (
        P(("obs", "grid"), None),
        P(("obs", "grid")),
        P(("obs", "grid")),
        P(("obs", "grid"), None, None),
        P(("obs", "grid"), None),
        P("obs", None, "grid"),
    )
    out_specs = P("obs", None, "grid")
    return jax.shard_map(
        on_device, mesh=mesh, in_specs=in_specs, out_specs=out_specs, check_vma=False
    )
```

```python
import functools

import jax
import jax.numpy as jnp
from jax import lax
from jax.experimental import pallas as pl
from jax.experimental.pallas import tpu as pltpu
from jax.sharding import PartitionSpec as P

ITERS = 6
Y, X, CORES = 4, 4, 2
F32, BF16 = jnp.float32, jnp.bfloat16
K = 128
LOW = 512
BLOCKS = 4
HALF = 2 * K + 16
PACK = 80
VMEM = 20 * 1024 * 1024


def params():
    return pltpu.CompilerParams(vmem_limit_bytes=VMEM)


LONG, SHORT = 6e10, 1e6
AWAY = (1, 2, 3)


def cost(flops):
    return pl.CostEstimate(flops=int(flops), bytes_accessed=100_000, transcendentals=0)


def in_vmem(count):
    return [pl.BlockSpec(memory_space=pltpu.VMEM)] * count


def hop(value, dy, dx, dc):
    pairs = []
    for place in range(Y * X * CORES):
        y, x, c = place // (X * CORES), place // CORES % X, place % CORES
        pairs.append((place, ((y + dy) % Y * X + (x + dx) % X) * CORES + (c ^ dc)))
    return lax.ppermute(value, "grid", pairs)


def dims(m, n):
    return (((m,), (n,)), ((), ()))


def send_picks(turned, cx, swapped):
    lines = []
    for y in range(Y):
        rows = turned[pl.ds(y * X * CORES + cx, 8, stride=Y * X * CORES), :]
        pair = [rows[0:4], rows[4:8]]
        pairs = jnp.concatenate(pair[::-1] if swapped else pair, axis=1)
        fours = jnp.concatenate([pairs[0:2], pairs[2:4]], axis=1)
        lines.append(jnp.concatenate([fours[0:1], fours[1:2]], axis=1))
    picks = jnp.concatenate(lines, axis=0)
    power = jnp.maximum(lax.shift_right_arithmetic(picks, 7), 0)
    code = lax.shift_left(128 + jnp.bitwise_and(picks, 127), power)
    return jnp.where(picks >= 0, code, 0).astype(F32)


def read_picks(rows):
    left = rows.astype(F32)
    high = jnp.zeros_like(left)
    for step in (8, 4, 2, 1):
        large = left >= 128.0 * 2**step
        left = jnp.where(large, left * 0.5**step, left)
        high = jnp.where(large, high + step, high)
    return jnp.where(left > 0.0, left - 128.0 + 128.0 * high, -1.0).astype(jnp.int32)


def message_kernel(departures, innovation, obs_weight, send_rows, *refs):
    outs, (rows, innov, weight, picks, turned) = refs[:3], refs[3:8]
    built, in_sems = outs, refs[8]
    small = ((send_rows, picks), (obs_weight, weight), (innovation, innov))
    small = [pltpu.make_async_copy(*pair, in_sems.at[i]) for i, pair in enumerate(small)]
    large = []
    for block in range(BLOCKS):
        span = pl.ds(block * LOW, LOW)
        large.append(
            pltpu.make_async_copy(departures.at[span], rows.at[span], in_sems.at[3 + block])
        )
    for copy in small + large:
        copy.start()
    small[0].wait()
    grid = lax.axis_index("grid")
    x, c = lax.rem(lax.div(grid, CORES), X), lax.rem(grid, CORES)
    turned[...] = picks[...].T
    groups = []
    for dx in range(X):
        for dc in range(CORES):
            cx = lax.rem(x + dx, X) * CORES + lax.rem(c + dc, CORES)
            groups.append(send_picks(turned, cx, dc == 1))
    small[1].wait()
    small[2].wait()
    root = jnp.sqrt(weight[...].reshape(1, BLOCKS * LOW))
    scaled = innov[...].reshape(1, BLOCKS * LOW) * root
    blank = jnp.zeros((2, LOW), F32)
    both = built[2]
    for half in range(2):
        one = built[half]
        at = half * HALF
        innovs = []
        for block in range(2):
            start = (2 * half + block) * LOW
            span = slice(start, start + LOW)
            large[2 * half + block].wait()
            part = (rows[span, :].astype(F32).T * root[:, span]).astype(BF16)
            one[block * K : (block + 1) * K, :] = part
            both[at + block * K : at + (block + 1) * K, :] = part
            innovs.append(scaled[:, span])
        top = innovs + [blank, groups[4 + half]]
        next_one = groups[2:4] if half == 0 else groups[6:8]
        one[2 * K :, :] = jnp.concatenate(top + next_one, axis=0).astype(BF16)
        both[at + 2 * K : at + HALF, :] = jnp.concatenate(top + groups[0:2], axis=0).astype(BF16)


def make_messages(*args):
    shapes = [(HALF, LOW), (HALF, LOW), (2 * HALF, LOW)]
    hbm = pl.BlockSpec(memory_space=pltpu.HBM)
    return pl.pallas_call(
        message_kernel,
        out_shape=[jax.ShapeDtypeStruct(shape, BF16) for shape in shapes],
        in_specs=[hbm] * 4,
        out_specs=in_vmem(3),
        scratch_shapes=[pltpu.VMEM(arg.shape, arg.dtype) for arg in args]
        + [pltpu.VMEM(args[3].shape[::-1], jnp.int32)]
        + [pltpu.SemaphoreType.DMA((3 + BLOCKS,))],
        compiler_params=pltpu.CompilerParams(vmem_limit_bytes=VMEM),
        cost_estimate=cost(2e9),
    )(*[pltpu.with_memory_space_constraint(arg, pltpu.HBM) for arg in args])


def pick(parts, picks):
    high = lax.shift_right_arithmetic(picks, 9)
    first = parts[0][0]
    live = picks >= 0 if len(parts) == 2 else lax.shift_right_arithmetic(high, 1) == first
    low = jnp.where(live, jnp.bitwise_and(picks, LOW - 1), -1)
    place = lax.broadcasted_iota(jnp.int32, (LOW, 256), 0).astype(jnp.int16)
    low = jnp.broadcast_to(low, (LOW, 256)).astype(jnp.int16)
    one_hot = jnp.where(place == low, jnp.ones((), BF16), jnp.zeros((), BF16))
    blocks, innovs = [], []
    for _, rows in parts:
        found = jnp.dot(rows, one_hot, preferred_element_type=F32)
        blocks += [found[:K], found[K : 2 * K]]
        innovs += [found[2 * K : 2 * K + 1], found[2 * K + 1 : 2 * K + 2]]
    members, innov = blocks[0], innovs[0]
    for block in range(1, len(blocks)):
        here = high == 2 * first + block
        members = jnp.where(here, blocks[block], members)
        innov = jnp.where(here, innovs[block], innov)
    return jnp.concatenate([members, jnp.broadcast_to(innov, (16, 256))], axis=0).astype(BF16)


def tail_picks(ref, at, row):
    return read_picks(ref[at + 2 * K : at + HALF, :].astype(F32)[row : row + 4])


def pick_kernel(sources, shifts, count, *refs):
    outs, scratch = refs[count:-1], refs[-1]
    place = lax.div(lax.axis_index("grid"), X * CORES)
    for n, (_, (which, at, row), _) in enumerate(sources):
        scratch[n] = tail_picks(refs[which], at, row)
    for shift in shifts:
        y = lax.rem(place + shift, Y)
        for i in range(2):
            span = slice(i * 256, i * 256 + 256)
            for n, (out, (parts, _, before)) in enumerate(zip(outs, sources)):
                tables = [(half, refs[which][at : at + HALF, :]) for half, which, at in parts]
                found = pick(tables, scratch[n, pl.ds(y, 1), :][:, span])
                out[2 * y + i] = found if before is None else found + refs[before][2 * y + i]


def pick_rows(sources, shifts, flops, *args):
    return pl.pallas_call(
        functools.partial(pick_kernel, sources, shifts, len(args)),
        out_shape=[jax.ShapeDtypeStruct((2 * Y, 144, 256), BF16)] * len(sources),
        in_specs=in_vmem(len(args)),
        out_specs=in_vmem(len(sources)),
        scratch_shapes=[pltpu.VMEM((len(sources), Y, LOW), jnp.int32)],
        compiler_params=params(),
        cost_estimate=cost(flops),
    )(*args)


def join(first, second):
    low = lax.broadcasted_iota(jnp.int32, first.shape, 1) < K // 2
    return jnp.where(low, first, second), jnp.where(low, second, first)


def pack(total):
    row = lax.broadcasted_iota(jnp.int32, (64, K), 0)
    lane = lax.broadcasted_iota(jnp.int32, (64, K), 1)
    lower = total[64:K]
    upper = jnp.where(lane < row, pltpu.roll(lower, 64, 1), total[0:64])
    diagonal = jnp.sum(jnp.where(lane == row + 64, lower, 0.0), axis=0, keepdims=True)
    return upper, diagonal, total[K : K + 1]


def unpack(packed):
    row = lax.broadcasted_iota(jnp.int32, (64, K), 0)
    lane = lax.broadcasted_iota(jnp.int32, (64, K), 1)
    upper = packed[0:64]
    above = jnp.where(lane > row, upper, 0.0)
    below = pltpu.roll(jnp.where(lane < row, upper, 0.0), 64, 1)
    off = jnp.concatenate([above, below], axis=0)
    low = jnp.where(lane == row + 64, packed[64:65], 0.0)
    diagonal = jnp.concatenate([jnp.where(lane == row, upper, 0.0), low], axis=0)
    return off + off.T + diagonal, packed[65:66]


def write_grams(out, i, shards, tail):
    tail_row = lax.broadcasted_iota(jnp.int32, (16, K), 0)
    for half in range(2):
        span = slice(half * K, half * K + K)
        pairs = [
            join(shards[n][:, span], shards[n + 1][:, span]) for n in range(0, len(shards), 2)
        ]
        for side in range(2):
            rows = jnp.concatenate([pair[side] for pair in pairs], axis=1)
            total = lax.dot_general(rows, rows[:K], dims(1, 1), preferred_element_type=F32)
            patch = i + 2 * half + 4 * side
            upper, diagonal, pull = pack(total)
            out[patch * 64 : patch * 64 + 64, :] = upper.astype(out.dtype)
            tail = jnp.where(tail_row == 2 * patch, diagonal, tail)
            tail = jnp.where(tail_row == 2 * patch + 1, pull, tail)
    return tail


def last_kernel(shifts, low, high, same, *rest):
    found, outs, picks = rest[:6], rest[6:-1], rest[-1]
    place = lax.div(lax.axis_index("grid"), X * CORES)
    picks[...] = tail_picks(high, 0, 4)
    table = ((0, low[...]), (1, high[...]))
    for out, shift in zip(outs, shifts):
        y = lax.rem(place + shift, Y)
        tail = jnp.zeros((16, K), F32)
        for i in range(2):
            span = slice(i * 256, i * 256 + 256)
            last = pick(table, picks[pl.ds(y, 1), :][:, span])
            shards = [ref[2 * y + i] for ref in (*found, same)] + [last]
            tail = write_grams(out, i, shards, tail)
        out[8 * 64 :, :] = tail.astype(out.dtype)


def own_grams_kernel(sources, *refs):
    found, tables, (out, scratch) = refs[:2], refs[2:-2], refs[-2:]
    y = lax.div(lax.axis_index("grid"), X * CORES)
    for n, (_, _, which, row) in enumerate(sources):
        scratch[n] = tail_picks(tables[which], 0, row)
    tail = jnp.zeros((16, K), F32)
    for i in range(2):
        span = slice(i * 256, i * 256 + 256)
        shards = [ref[2 * y + i] for ref in found]
        for n, (low, high, _, _) in enumerate(sources):
            parts = ((0, tables[low][...]), (1, tables[high][...]))
            shards.append(pick(parts, scratch[n, pl.ds(y, 1), :][:, span]))
        tail = write_grams(out, i, shards, tail)
    out[8 * 64 :, :] = tail


def own_grams(sources, *args):
    return pl.pallas_call(
        functools.partial(own_grams_kernel, sources),
        out_shape=jax.ShapeDtypeStruct((8 * 64 + 16, K), F32),
        in_specs=in_vmem(len(args)),
        out_specs=in_vmem(1)[0],
        scratch_shapes=[pltpu.VMEM((len(sources), Y, LOW), jnp.int32)],
        compiler_params=params(),
        cost_estimate=cost(1e9),
    )(*args)


def last_grams(shifts, dtype, *args):
    return pl.pallas_call(
        functools.partial(last_kernel, shifts),
        out_shape=[jax.ShapeDtypeStruct((8 * 64 + 16, K), dtype)] * len(shifts),
        in_specs=in_vmem(len(args)),
        out_specs=in_vmem(len(shifts)),
        scratch_shapes=[pltpu.VMEM((Y, LOW), jnp.int32)],
        compiler_params=params(),
        cost_estimate=cost(1e9 * len(shifts)),
    )(*args)


def sum_kernel(own, a, b, c, out):
    def total(span):
        return own[span, :] + (a[span, :].astype(F32) + b[span, :].astype(F32) + c[span, :].astype(F32))

    tails = total(slice(8 * 64, 8 * 64 + 16))
    first = lax.broadcasted_iota(jnp.int32, (16, K), 0) == 0
    for patch in range(8):
        out[patch, 0:64, :] = total(slice(patch * 64, patch * 64 + 64)).astype(BF16)
        tail = jnp.where(first, tails[2 * patch : 2 * patch + 1], tails[2 * patch + 1 : 2 * patch + 2])
        out[patch, 64:PACK, :] = tail.astype(BF16)


def sum_parts(*args):
    return pl.pallas_call(
        sum_kernel,
        out_shape=jax.ShapeDtypeStruct((8, PACK, K), BF16),
        in_specs=in_vmem(4),
        out_specs=in_vmem(1)[0],
        compiler_params=params(),
        cost_estimate=cost(5e8),
    )(*args)


def split(value):
    high = value.astype(BF16)
    return high, (value - high.astype(F32)).astype(BF16)


def product(left, right):
    lh, ll = split(left)
    rh, rl = split(right)
    return jnp.dot(
        jnp.concatenate([lh, lh, ll], axis=1),
        jnp.concatenate([rh, rl, rh], axis=0),
        preferred_element_type=F32,
    )


def weights_kernel(parts, out):
    gram, pull = unpack(jnp.sum(parts[...].astype(F32), axis=0))
    row = lax.broadcasted_iota(jnp.int32, (K, K), 0)
    col = lax.broadcasted_iota(jnp.int32, (K, K), 1)
    identity = (row == col).astype(F32)
    system = gram + (K - 1.0) * identity
    squares = jnp.sum(jnp.sum(system * system, axis=0, keepdims=True), axis=1, keepdims=True)
    frob = jnp.sqrt(squares)
    iterate = system / frob
    inverse = 1.5 * identity - 0.5 * iterate
    iterate = product(inverse, iterate)
    for sweep in range(1, ITERS):
        newton = 1.5 * identity - 0.5 * product(inverse, iterate)
        if sweep < ITERS - 1:
            both = product(newton, jnp.concatenate([iterate, inverse], axis=1))
            iterate, inverse = both[:, :K], both[:, K:]
        else:
            inverse = product(newton, inverse)
    shift = product(product(jnp.broadcast_to(pull, (16, K)), inverse), inverse)[0:1] / frob
    out[...] = (jnp.sqrt((K - 1.0) / frob) * inverse.T + shift).astype(BF16)


def transposed_weights(parts):
    return pl.pallas_call(
        weights_kernel,
        out_shape=jax.ShapeDtypeStruct((K, K), BF16),
        in_specs=in_vmem(1),
        out_specs=in_vmem(1)[0],
        compiler_params=params(),
        cost_estimate=cost(4e9),
    )(parts)


def column_coefs():
    position = lax.broadcasted_iota(jnp.int32, (1, 2 * K), 1) % K
    position = (position.astype(F32) + 0.5) / K
    return jnp.maximum(0.5 - position, 0.0), jnp.maximum(position - 0.5, 0.0)


def perturb_kernel(state, mean, perturb, sides):
    for pair in range(mean.shape[0]):
        for i in range(2):
            span = slice(i * K, (i + 1) * K)
            values = state[2 * pair + i].astype(F32)
            average = jnp.mean(values, axis=0, keepdims=True)
            mean[pair : pair + 1, span] = average
            rounded = (values - average).astype(BF16)
            perturb[pair, :, span] = rounded
            for side, coef in enumerate(column_coefs()):
                sides[pair, side * K : (side + 1) * K, span] = coef[:, span].astype(BF16) * rounded


def perturbations(state):
    pairs = state.shape[0] // 2
    return pl.pallas_call(
        perturb_kernel,
        out_shape=[
            jax.ShapeDtypeStruct((pairs, 2 * K), F32),
            jax.ShapeDtypeStruct((pairs, K, 2 * K), BF16),
            jax.ShapeDtypeStruct((pairs, 2 * K, 2 * K), BF16),
        ],
        in_specs=in_vmem(1),
        out_specs=in_vmem(3),
        compiler_params=params(),
        cost_estimate=cost(LONG),
    )(state)


def own_kernel(own, mean, perturb, out):
    left_coef, right_coef = column_coefs()
    own_coef = 1.0 - left_coef - right_coef
    for pair in range(mean.shape[0]):
        sums = jnp.dot(own[...], perturb[pair], preferred_element_type=F32)
        out[pair] = mean[pair : pair + 1] + own_coef * sums


def own_part(own, mean, perturb):
    return pl.pallas_call(
        own_kernel,
        out_shape=jax.ShapeDtypeStruct(perturb.shape, F32),
        in_specs=in_vmem(3),
        out_specs=in_vmem(1)[0],
        compiler_params=params(),
        cost_estimate=cost(2e9),
    )(own, mean, perturb)


def side_kernel(beyond, beside, part, sides, out, held, sems):
    first_core = lax.rem(lax.axis_index("grid"), CORES) == 0
    left = jnp.where(first_core, beyond[...], beside[...])
    right = jnp.where(first_core, beside[...], beyond[...])
    weights = jnp.concatenate([left, right], axis=1)
    chunks = sems.shape[0]
    pairs = sides.shape[0] // chunks
    copies = []
    for chunk in range(chunks):
        for pair in range(chunk * pairs, (chunk + 1) * pairs):
            total = part[pair] + jnp.dot(weights, sides[pair], preferred_element_type=F32)
            total = total.astype(BF16)
            for i in range(2):
                held[2 * pair + i] = total[:, i * K : (i + 1) * K]
        rows = pl.ds(2 * chunk * pairs, 2 * pairs)
        copies.append(pltpu.make_async_copy(held.at[rows], out.at[rows], sems.at[chunk]))
        copies[-1].start()
    for copy in copies:
        copy.wait()


def add_sides(beyond, beside, part, sides):
    shape = (2 * sides.shape[0], K, K)
    return pl.pallas_call(
        side_kernel,
        out_shape=jax.ShapeDtypeStruct(shape, BF16),
        in_specs=in_vmem(4),
        out_specs=pl.BlockSpec(memory_space=pltpu.HBM),
        scratch_shapes=[pltpu.VMEM(shape, BF16), pltpu.SemaphoreType.DMA((12,))],
        compiler_params=params(),
        cost_estimate=cost(2e9),
    )(beyond, beside, part, sides)


def on_device(departures, innovation, obs_weight, send_rows, send_counts, state):
    n_grid = lax.axis_size("grid")
    low_half, high_half, near = make_messages(
        departures, innovation, obs_weight, send_rows[0].T
    )
    left = hop(low_half, 0, 1, 0)
    right = hop(high_half, 0, -1, 0)
    other = hop(near, 0, 0, 1)

    whole = lambda which: ((0, which, 0), (1, which, HALF))
    found = pick_rows(
        ((whole(0), (0, 0, 8), None), (whole(1), (1, 0, 12), None)), (0, 1, 2, 3), SHORT, near, other
    )
    mean, perturb, sides = perturbations(state)
    low_half, high_half, mean, perturb, sides = lax.optimization_barrier(
        (low_half, high_half, mean, perturb, sides)
    )
    left_more = hop(high_half, 0, 1, 0)
    right_more = hop(low_half, 0, -1, 0)
    left, found, mean, perturb = lax.optimization_barrier((left, found, mean, perturb))
    far_low = hop(left, 0, 1, 0)
    left, right, found = lax.optimization_barrier((left, right, found))
    far_high = hop(right, 0, -1, 0)

    def firsts(core):
        row = 8 + 4 * core
        return (((0, 0, 0),), (0, 0, row), None), (((1, 1, 0),), (1, 0, row), None)

    def seconds(core):
        row = 8 + 4 * core
        return (((1, 2, 0),), (0, 0, row), 4), (((0, 3, 0),), (1, 0, row), 5)

    same = pick_rows(firsts(0), AWAY, SHORT, left, right)
    left, right, same = lax.optimization_barrier((left, right, same))
    left_other, right_other = hop(left, 0, 0, 1), hop(right, 0, 0, 1)
    same = pick_rows(seconds(0), AWAY, LONG, left, right, left_more, right_more, *same)
    left_more, right_more, same = lax.optimization_barrier((left_more, right_more, same))
    left_more_other, right_more_other = hop(left_more, 0, 0, 1), hop(right_more, 0, 0, 1)
    cross = pick_rows(firsts(1), AWAY, LONG, left_other, right_other)
    cross = pick_rows(
        seconds(1), AWAY, SHORT, left_other, right_other, left_more_other, right_more_other, *cross
    )
    far_low, far_high, cross = lax.optimization_barrier((far_low, far_high, cross))
    far_low_other, far_high_other = hop(far_low, 0, 0, 1), hop(far_high, 0, 0, 1)
    far = pick_rows(((((0, 0, 0), (1, 1, 0)), (0, 0, 4), None),), AWAY, SHORT, far_low, far_high)[0]
    last = (far_low_other, far_high_other, far, *found, same[0], cross[0], same[1], cross[1])

    across = last_grams((2,), BF16, *last)[0]
    from_across = hop(across, 2, 0, 0)
    from_up = hop(last_grams((1,), BF16, *last)[0], 1, 0, 0)
    from_down = hop(last_grams((3,), BF16, *last)[0], -1, 0, 0)
    sources = ((0, 2, 0, 8), (1, 3, 1, 12), (6, 4, 4, 8), (7, 5, 5, 12), (8, 9, 8, 4), (10, 11, 11, 4))
    own = own_grams(
        sources,
        *found,
        left,
        left_other,
        left_more,
        left_more_other,
        right,
        right_other,
        right_more,
        right_more_other,
        far_low,
        far_high,
        far_low_other,
        far_high_other,
    )
    parts = sum_parts(own, from_across, from_up, from_down)
    parts = lax.all_to_all(parts, "obs", 0, 0, tiled=True)

    own = transposed_weights(parts)
    beyond = lax.ppermute(own, "grid", [(j, (j + 2 * (j % 2) - 1) % n_grid) for j in range(n_grid)])
    part = own_part(own, mean, perturb)
    own, part = lax.optimization_barrier((own, part))
    beside = hop(own, 0, 0, 1)
    return add_sides(beyond, beside, part, sides)


def solution(mesh):
    in_specs = (
        P(("obs", "grid"), None),
        P(("obs", "grid")),
        P(("obs", "grid")),
        P(("obs", "grid"), None, None),
        P(("obs", "grid"), None),
        P("obs", None, "grid"),
    )
    out_specs = P("obs", None, "grid")
    return jax.shard_map(
        on_device, mesh=mesh, in_specs=in_specs, out_specs=out_specs, check_vma=False
    )
```
